32 devices in a mesh: height: 4 (over z), chan: 4 (over x, core), dp: 2 (over y).
Axes of the slice: x: 2, y: 2, z: 4, core: 2. Of those that a mesh axis runs over, the one named last changes fastest.
Arguments:
- inputs: bfloat16 [96, 8, 7, 2048], P('dp', 'height'), may hold values from -9 to 9, as said below
- cotangent: bfloat16 [96, 8, 7, 2048], P('dp', 'height', None, 'chan'), may hold values from -6 to 6
- reduce_master: float32 [2048, 1024], P(('height', 'dp'), 'chan'), may hold values from -0.125 to 0.125
- reduce_first: float32 [2048, 1024], P(('height', 'dp'), 'chan'), may hold values from -274.34286 to 274.34286
- reduce_second: float32 [2048, 1024], P(('height', 'dp'), 'chan'), may hold values from 2352 to 18816
- reduce_average: float32 [2048, 1024], P(('height', 'dp'), 'chan'), may hold values from -0.125 to 0.125
- group_master: float32 [288, 1024], P(('height', 'dp'), 'chan'), may hold values from -0.375 to 0.375
- group_first: float32 [288, 1024], P(('height', 'dp'), 'chan'), may hold values from -137.17143 to 137.17143
- group_second: float32 [288, 1024], P(('height', 'dp'), 'chan'), may hold values from 588 to 4704
- group_average: float32 [288, 1024], P(('height', 'dp'), 'chan'), may hold values from -0.375 to 0.375
- expand_master: float32 [1024, 2048], P('chan', ('height', 'dp')), may hold values from -0.1875 to 0.1875
- expand_first: float32 [1024, 2048], P('chan', ('height', 'dp')), may hold values from -137.17143 to 137.17143
- expand_second: float32 [1024, 2048], P('chan', ('height', 'dp')), may hold values from 588 to 4704
- expand_average: float32 [1024, 2048], P('chan', ('height', 'dp')), may hold values from -0.1875 to 0.1875
- inner_master: float32 [4, 1024], P(None, 'chan'), may hold values from -0.9 to 1.5, as said below
- inner_first: float32 [4, 1024], P(None, 'chan'), may hold values from -274.34286 to 274.34286
- inner_second: float32 [4, 1024], P(None, 'chan'), may hold values from 2352 to 18816
- inner_average: float32 [4, 1024], P(None, 'chan'), may hold values from -0.9 to 1.5, as said below
- outer_master: float32 [2, 2048], P(None, 'chan'), may hold values from -0.9 to 1.5, as said below
- outer_first: float32 [2, 2048], P(None, 'chan'), may hold values from -274.34286 to 274.34286
- outer_second: float32 [2, 2048], P(None, 'chan'), may hold values from 2352 to 18816
- outer_average: float32 [2, 2048], P(None, 'chan'), may hold values from -0.9 to 1.5, as said below
Outputs:
- block_out: bfloat16 [96, 8, 7, 2048], P('dp', 'height', None, 'chan')
- input_grad: float32 [96, 8, 7, 2048], P('dp', 'height', None, 'chan')
- reduce_grad: float32 [2048, 1024], P(('height', 'dp'), 'chan')
- reduce_first_new: float32 [2048, 1024], P(('height', 'dp'), 'chan')
- reduce_second_new: float32 [2048, 1024], P(('height', 'dp'), 'chan')
- reduce_master_new: float32 [2048, 1024], P(('height', 'dp'), 'chan')
- reduce_copy: bfloat16 [2048, 1024], P(('height', 'dp'), 'chan')
- reduce_average_new: float32 [2048, 1024], P(('height', 'dp'), 'chan')
- group_grad: float32 [288, 1024], P(('height', 'dp'), 'chan')
- group_first_new: float32 [288, 1024], P(('height', 'dp'), 'chan')
- group_second_new: float32 [288, 1024], P(('height', 'dp'), 'chan')
- group_master_new: float32 [288, 1024], P(('height', 'dp'), 'chan')
- group_copy: bfloat16 [288, 1024], P(('height', 'dp'), 'chan')
- group_average_new: float32 [288, 1024], P(('height', 'dp'), 'chan')
- expand_grad: float32 [1024, 2048], P('chan', ('height', 'dp'))
- expand_first_new: float32 [1024, 2048], P('chan', ('height', 'dp'))
- expand_second_new: float32 [1024, 2048], P('chan', ('height', 'dp'))
- expand_master_new: float32 [1024, 2048], P('chan', ('height', 'dp'))
- expand_copy: bfloat16 [1024, 2048], P('chan', ('height', 'dp'))
- expand_average_new: float32 [1024, 2048], P('chan', ('height', 'dp'))
- inner_grad: float32 [4, 1024], P(None, 'chan')
- inner_first_new: float32 [4, 1024], P(None, 'chan')
- inner_second_new: float32 [4, 1024], P(None, 'chan')
- inner_master_new: float32 [4, 1024], P(None, 'chan')
- inner_average_new: float32 [4, 1024], P(None, 'chan')
- outer_grad: float32 [2, 2048], P(None, 'chan')
- outer_first_new: float32 [2, 2048], P(None, 'chan')
- outer_second_new: float32 [2, 2048], P(None, 'chan')
- outer_master_new: float32 [2, 2048], P(None, 'chan')
- outer_average_new: float32 [2, 2048], P(None, 'chan')
The draws below stay inside these ranges and needn't reach their ends.
Inputs may be any that keep to these rules, and one draw needn't show every extreme that they name: `inputs`: row 7 of every image is zero. `inner_master`: rows 0 and 2 are gains, rows 1 and 3 shifts. `inner_average`: rows 0 and 2 are averaged gains, rows 1 and 3 shifts. `outer_master`: row 0 is the gain, row 1 the shift. `outer_average`: row 0 is the averaged gain, row 1 the shift.
All inputs are finite; a program needn't handle non-finite values.
Results may differ from the reference program's by a relative error of at most 0.02.
Values may be sent and summed in bfloat16 or wider, within the bound.
A program may use at most 128 MiB of HBM per device.

```python
import math
import jax
import jax.numpy as jnp
from jax import lax

C_IN = 2048
C_MID = 1024
GROUP = 32
HEIGHT = 7
WIDTH = 7
STEP = 10
IMAGES = 96
PADDED = 8


def draw_inputs(key, part):
    key = jax.random.fold_in(key, 11)
    shape = (IMAGES, PADDED, WIDTH, C_IN)
    position = jnp.arange(IMAGES, dtype=jnp.float32)[:, None, None, None] / max(IMAGES - 1, 1)
    row_keep = (jnp.arange(PADDED) < HEIGHT).astype(jnp.float32)[None, :, None, None]
    values = jnp.clip(jax.random.normal(key, shape, jnp.float32), -4.5, 4.5)
    scaled = values * 0.6 * (1.0 + 2.0 * position)
    return (scaled * row_keep).astype(jnp.bfloat16)


def norm_table(key, pairs, columns, gain_low, gain_high, shift_bound):
    table = []
    for number in range(pairs):
        gain_key = jax.random.fold_in(key, 2 * number)
        shift_key = jax.random.fold_in(key, 2 * number + 1)
        table.append(jax.random.uniform(gain_key, (columns,), jnp.float32, gain_low, gain_high))
        table.append(jax.random.uniform(shift_key, (columns,), jnp.float32, -shift_bound, shift_bound))
    return jnp.stack(table)


def draw_inner_master(key, part):
    key = jax.random.fold_in(key, 21)
    return norm_table(key, 2, C_MID, 0.6, 1.4, 0.5)


def draw_inner_average(key, part):
    key = jax.random.fold_in(key, 22)
    return norm_table(key, 2, C_MID, 0.6, 1.4, 0.5)


def draw_outer_master(key, part):
    key = jax.random.fold_in(key, 23)
    return norm_table(key, 1, C_IN, 0.6, 1.4, 0.5)


def draw_outer_average(key, part):
    key = jax.random.fold_in(key, 24)
    return norm_table(key, 1, C_IN, 0.6, 1.4, 0.5)


def shard_levels(rng, extent, cuts, smallest, top_value):
    level, own = 1.0, jax.random.fold_in(rng, 6)
    for axis_at, shards_of in cuts:
        draws = jnp.exp(jax.random.uniform(jax.random.fold_in(own, axis_at), (shards_of,), jnp.float32, smallest / len(cuts), top_value / len(cuts)))
        level = level * jnp.repeat(draws, extent[axis_at] // shards_of).reshape([-1 if axis == axis_at else 1 for axis in range(len(extent))])
    return level


def gaussian(rng, extent, spread, most, split=(), kind=jnp.bfloat16):
    drawn = jax.random.normal(rng, extent, jnp.float32) * spread
    if len(split) > 0:
        drawn = shard_levels(rng, extent, split, -0.22, 0.18) * drawn
    return jnp.clip(drawn, min=-most, max=most).astype(kind)


def setup_inputs(seed: int = 0) -> dict:
    arg_keys = jax.random.split(jax.random.key(seed), 23)
    return {
        "inputs": draw_inputs(jax.random.fold_in(arg_keys[22], 71), 0),
        "cotangent": gaussian(arg_keys[1], (IMAGES, PADDED, WIDTH, C_IN), 1.0, 6.0, ((0, 2), (1, 4), (3, 4))),
        "reduce_master": gaussian(arg_keys[2], (C_IN, C_MID), C_IN ** -0.5, 0.125, ((0, 8), (1, 4)), jnp.float32),
        "reduce_first": gaussian(arg_keys[3], (C_IN, C_MID), ((IMAGES * HEIGHT * WIDTH) ** 0.5), 274.34286, ((0, 8), (1, 4)), jnp.float32),
        "reduce_second": jnp.clip(jnp.exp(math.log(18816.0) - 2.0794415 * jax.random.uniform(arg_keys[4], (C_IN, C_MID), jnp.float32) ** shard_levels(arg_keys[4], (C_IN, C_MID), ((0, 8), (1, 4)), -0.2, 0.2)), 2352.0, 18816.0),
        "reduce_average": gaussian(arg_keys[5], (C_IN, C_MID), C_IN ** -0.5, 0.125, ((0, 8), (1, 4)), jnp.float32),
        "group_master": gaussian(arg_keys[6], (9 * GROUP, C_MID), (9 * GROUP) ** -0.5, 0.375, ((0, 8), (1, 4)), jnp.float32),
        "group_first": gaussian(arg_keys[7], (9 * GROUP, C_MID), (0.5 * (IMAGES * HEIGHT * WIDTH) ** 0.5), 137.17143, ((0, 8), (1, 4)), jnp.float32),
        "group_second": jnp.clip(jnp.exp(math.log(4704.0) - 2.0794415 * jax.random.uniform(arg_keys[8], (9 * GROUP, C_MID), jnp.float32) ** shard_levels(arg_keys[8], (9 * GROUP, C_MID), ((0, 8), (1, 4)), -0.2, 0.2)), 588.0, 4704.0),
        "group_average": gaussian(arg_keys[9], (9 * GROUP, C_MID), (9 * GROUP) ** -0.5, 0.375, ((0, 8), (1, 4)), jnp.float32),
        "expand_master": gaussian(arg_keys[10], (C_MID, C_IN), C_MID ** -0.5, 0.1875, ((0, 4), (1, 8)), jnp.float32),
        "expand_first": gaussian(arg_keys[11], (C_MID, C_IN), (0.5 * (IMAGES * HEIGHT * WIDTH) ** 0.5), 137.17143, ((0, 4), (1, 8)), jnp.float32),
        "expand_second": jnp.clip(jnp.exp(math.log(4704.0) - 2.0794415 * jax.random.uniform(arg_keys[12], (C_MID, C_IN), jnp.float32) ** shard_levels(arg_keys[12], (C_MID, C_IN), ((0, 4), (1, 8)), -0.2, 0.2)), 588.0, 4704.0),
        "expand_average": gaussian(arg_keys[13], (C_MID, C_IN), C_MID ** -0.5, 0.1875, ((0, 4), (1, 8)), jnp.float32),
        "inner_master": draw_inner_master(jax.random.fold_in(arg_keys[22], 71), 0),
        "inner_first": gaussian(arg_keys[15], (4, C_MID), ((IMAGES * HEIGHT * WIDTH) ** 0.5), 274.34286, ((1, 4),), jnp.float32),
        "inner_second": jnp.clip(jnp.exp(math.log(18816.0) - 2.0794415 * jax.random.uniform(arg_keys[16], (4, C_MID), jnp.float32) ** shard_levels(arg_keys[16], (4, C_MID), ((1, 4),), -0.2, 0.2)), 2352.0, 18816.0),
        "inner_average": draw_inner_average(jax.random.fold_in(arg_keys[22], 71), 0),
        "outer_master": draw_outer_master(jax.random.fold_in(arg_keys[22], 71), 0),
        "outer_first": gaussian(arg_keys[19], (2, C_IN), ((IMAGES * HEIGHT * WIDTH) ** 0.5), 274.34286, ((1, 4),), jnp.float32),
        "outer_second": jnp.clip(jnp.exp(math.log(18816.0) - 2.0794415 * jax.random.uniform(arg_keys[20], (2, C_IN), jnp.float32) ** shard_levels(arg_keys[20], (2, C_IN), ((1, 4),), -0.2, 0.2)), 2352.0, 18816.0),
        "outer_average": draw_outer_average(jax.random.fold_in(arg_keys[22], 71), 0),
    }


@jax.custom_vjp
def low(v):
    return lax.optimization_barrier(v.astype(jnp.bfloat16)).astype(jnp.float32)

@jax.custom_vjp
def low_back(v):
    return v

def low_keep(v):
    return (low(v), None)

def low_pass(kept, grad):
    return (grad,)

def back_keep(v):
    return (v, None)

def back_low(kept, grad):
    return (low(grad),)
low.defvjp(low_keep, low_pass)
low_back.defvjp(back_keep, back_low)
HIGHEST = lax.Precision.HIGHEST
NORM_EPS = 1e-05
CONV_RATE = 0.02
NORM_RATE = 0.3

def batch_norm(values, gain, shift, valid_rows, pixels):
    average = lax.optimization_barrier(jnp.sum(values * valid_rows, axis=(0, 1, 2))) / pixels
    power = lax.optimization_barrier(jnp.sum(values * values * valid_rows, axis=(0, 1, 2))) / pixels
    inverse = lax.rsqrt(power - average * average + NORM_EPS)
    return (values - average) * inverse * gain + shift

def forward(inputs, reduce_master, group_master, expand_master, inner_master, outer_master):
    valid_rows = (jnp.arange(inputs.shape[1]) < HEIGHT).astype(jnp.float32)[None, :, None, None]
    pixels = inputs.shape[0] * HEIGHT * WIDTH * 1.0
    first = low_back(jnp.einsum('nhwc,cd->nhwd', inputs, low(reduce_master), precision=HIGHEST))
    act_one = low(jax.nn.silu(batch_norm(first, inner_master[0], inner_master[1], valid_rows, pixels)) * valid_rows)
    kernel = low(group_master).reshape(3, 3, GROUP, C_MID)
    second = low_back(lax.conv_general_dilated(act_one, kernel, (1, 1), ((1, 1), (1, 1)), dimension_numbers=('NHWC', 'HWIO', 'NHWC'), feature_group_count=C_MID // GROUP, precision=HIGHEST))
    act_two = low(jax.nn.silu(batch_norm(second, inner_master[2], inner_master[3], valid_rows, pixels)) * valid_rows)
    third = low_back(jnp.einsum('nhwd,dc->nhwc', act_two, low(expand_master), precision=HIGHEST))
    pre = batch_norm(third, outer_master[0], outer_master[1], valid_rows, pixels) + inputs
    return jax.nn.silu(pre) * valid_rows

def adamw_step(master, gradient, moment_one, moment_two, average, rate):
    first_new = 0.5 * moment_one + 0.5 * gradient
    second_new = 0.5 * moment_two + 0.5 * gradient * gradient
    correct = 1.0 - 0.5 ** STEP
    direction = first_new / correct / (jnp.sqrt(second_new / correct) + 1e-08)
    master_new = master - rate * (direction + 0.05 * master)
    average_new = 0.75 * average + 0.25 * master_new
    return (first_new, second_new, master_new, average_new)

def reference(inputs, cotangent, reduce_master, reduce_first, reduce_second, reduce_average, group_master, group_first, group_second, group_average, expand_master, expand_first, expand_second, expand_average, inner_master, inner_first, inner_second, inner_average, outer_master, outer_first, outer_second, outer_average):
    inputs_full = inputs.astype(jnp.float32)
    result, pullback = jax.vjp(forward, inputs_full, reduce_master, group_master, expand_master, inner_master, outer_master)
    gradients = pullback(cotangent.astype(jnp.float32))
    block_out = result.astype(jnp.bfloat16)
    red = adamw_step(reduce_master, gradients[1], reduce_first, reduce_second, reduce_average, CONV_RATE)
    grp = adamw_step(group_master, gradients[2], group_first, group_second, group_average, CONV_RATE)
    exp_new = adamw_step(expand_master, gradients[3], expand_first, expand_second, expand_average, CONV_RATE)
    inn = adamw_step(inner_master, gradients[4], inner_first, inner_second, inner_average, NORM_RATE)
    out_new = adamw_step(outer_master, gradients[5], outer_first, outer_second, outer_average, NORM_RATE)
    return (block_out, gradients[0], gradients[1], red[0], red[1], red[2], red[2].astype(jnp.bfloat16), red[3], gradients[2], grp[0], grp[1], grp[2], grp[2].astype(jnp.bfloat16), grp[3], gradients[3], exp_new[0], exp_new[1], exp_new[2], exp_new[2].astype(jnp.bfloat16), exp_new[3], gradients[4], inn[0], inn[1], inn[2], inn[3], gradients[5], out_new[0], out_new[1], out_new[2], out_new[3])
```

```python
import functools

import jax
import jax.numpy as jnp
from jax import lax
from jax.experimental import pallas as pl
from jax.experimental.pallas import tpu as pltpu
from jax.sharding import PartitionSpec as P

GROUP = 32
HEIGHT = 7
STEP = 10
NORM_EPS = 1e-05
CONV_RATE = 0.02
NORM_RATE = 0.3

BF = jnp.bfloat16
F32 = jnp.float32
MESH = pl.DeviceIdType.MESH
SEMAPHORES = 192
SLOT = 48


def dot(a, b):
    return jnp.dot(a, b, preferred_element_type=F32)


def dot_nt(a, b):
    return lax.dot_general(a, b, (((1,), (1,)), ((), ())), preferred_element_type=F32)


def block_kernel(names, dims, *refs):
    r = dict(zip(names, refs, strict=True))
    H, D, N, W, MID, OUT, CIN = (dims[k] for k in ("H", "D", "N", "W", "MID", "OUT", "CIN"))
    own_gather = dims["own_gather"]
    R = W * N
    PITCH = (W + 2) * N
    HD = H * D
    pixels = float(N * D * HEIGHT * W)
    x_ref, ct_ref, inner_ref, outer_ref = r["x"], r["ct"], r["inner"], r["outer"]

    z = lax.axis_index("height")
    c = lax.axis_index("chan")
    y = lax.axis_index("dp")
    xp = lax.div(c, 2)
    k = lax.rem(c, 2)
    cx = lax.rem(c + 2, 4)
    cc = c + 1 - 2 * k
    owner = z * D + y

    def dev(dz=0, chan=None, dy=0):
        return {
            "height": lax.rem(z + dz, H),
            "chan": c if chan is None else chan,
            "dp": lax.rem(y + dy, D),
        }

    offsets = [(dz, dy) for dz in range(H) for dy in range(D)]
    family = [dev(dz, None, dy) for dz, dy in offsets if dz or dy]
    twin_family = [dev(dz, cx, dy) for dz, dy in offsets]
    core_peer = dev(0, cc, 0)
    x_peer = dev(0, cx, 0)

    def rows(h):
        return pl.ds(pl.multiple_of(h * R, 16), R)

    def tile(h, w):
        return pl.ds(pl.multiple_of(h * R + w * N, 16), N)

    def slab(hh, ww, count):
        return pl.ds(pl.multiple_of((hh * (W + 2) + ww) * N, 16), count)

    def quarter(j, core):
        return pl.ds(pl.multiple_of((2 * j + core) * OUT, 128), OUT)

    def valid(h):
        return jnp.where(z * 2 + h < HEIGHT, 1.0, 0.0).astype(F32)

    sends = []
    used = [0]

    def make(src, dst, target):
        i = used[0]
        used[0] += 1
        return pltpu.make_async_remote_copy(
            src_ref=src,
            dst_ref=dst,
            send_sem=r["ssem"].at[i],
            recv_sem=r["rsem"].at[i],
            device_id=target,
            device_id_type=MESH,
        )

    def send(src, dst, target):
        copy = make(src, dst, target)
        copy.start()
        sends.append(copy)
        return copy

    a1, b2 = r["a1"], r["b2"]
    a1[...] = jnp.zeros(a1.shape, BF)
    b2[...] = jnp.zeros(b2.shape, BF)
    lane_group = lax.shift_right_logical(lax.broadcasted_iota(jnp.int32, (MID, MID), 1), 5)
    row_group = lax.shift_right_logical(lax.broadcasted_iota(jnp.int32, (MID, MID), 0), 5)
    block_diagonal = lane_group == row_group
    if own_gather:
        wr, we, wg = r["wr"], r["we"], r["wg"]
        RB, EB = r["rm"].shape[0], r["em"].shape[1]
        GB = r["gm"].shape[0]

        def reduce_block(o):
            return wr.at[pl.ds(pl.multiple_of(o * RB, 16), RB), :]

        def expand_block(o):
            return we.at[:, pl.ds(pl.multiple_of(o * EB, 128), EB)]

        def group_block(o):
            return wg.at[o]

        reduce_block(owner)[...] = r["rm"][...].astype(BF)
        expand_block(owner)[...] = r["em"][...].astype(BF)
        wg[owner] = jnp.concatenate(
            [r["gm"][...], jnp.zeros((SLOT - GB, MID), F32)], axis=0
        ).astype(BF)
    else:
        wr, we = r["wr_full"], r["we_full"]

    barrier = pltpu.get_barrier_semaphore()
    everyone = family + twin_family + [core_peer]
    for target in everyone:
        pl.semaphore_signal(barrier, inc=1, device_id=target, device_id_type=MESH)
    pl.semaphore_wait(barrier, len(everyone))

    class Gather:
        def __init__(self, block):
            self.block = block
            self.here = block(owner)

        def start(self):
            self.along_z = [
                (dz, send(self.here, self.here, dev(dz, None, 0))) for dz in range(1, H)
            ]

        def start_y(self):
            self.along_y = [send(self.here, self.here, dev(0, None, dy)) for dy in range(1, D)]

        def forward(self):
            for dz, copy in self.along_z:
                copy.wait_recv()
                block = self.block(lax.rem(z - dz + H, H) * D + y)
                for dy in range(1, D):
                    self.along_y.append(send(block, block, dev(0, None, dy)))

        def finish(self):
            for copy in self.along_y:
                copy.wait_recv()

    if own_gather:
        g_reduce, g_group, g_expand = Gather(reduce_block), Gather(group_block), Gather(expand_block)
        g_reduce.start()
        g_reduce.start_y()
        g_group.start()
        g_group.start_y()
    ct2, out2 = r["ct2"], r["out2"]
    ct_in = send(ct_ref.at[rows(1 - xp)], ct2.at[xp], x_peer)
    ct2[xp] = ct_ref[rows(xp), :]
    out2[xp] = outer_ref[...]
    outer_in = send(out2.at[xp], out2.at[xp], x_peer)
    wep = r["wep"]
    twin_in = []
    if not own_gather:
        twin_in.append(send(we, wep, x_peer))

    def statistics(buf, position, targets, value):
        buf[position] = value
        return [send(buf.at[position], buf.at[position], t) for t in targets]

    def total(buf, copies):
        for copy in copies:
            copy.wait_recv()
        return jnp.sum(buf[...], axis=0)

    first = r["first"]

    def product(blocks, start):
        def body(h, carry):
            left = jnp.concatenate(
                [x_ref[rows(h), pl.ds(pl.multiple_of(o * RB, 128), RB)] for o in blocks], axis=1
            )
            right = jnp.concatenate([reduce_block(o)[...] for o in blocks], axis=0)
            part = dot(left, right)
            first[rows(h), :] = part if start else first[rows(h), :] + part
            return carry

        lax.fori_loop(0, 2, body, 0)

    if own_gather:
        g_reduce.forward()
        g_expand.start()
        g_expand.start_y()
        twin_in.append(send(g_expand.here, wep.at[:, pl.ds(pl.multiple_of(owner * EB, 128), EB)], x_peer))
        g_group.forward()
        product([zz * D + y for zz in range(H)], True)
        g_reduce.finish()
        for dy in range(1, D):
            product([zz * D + lax.rem(y + dy, D) for zz in range(H)], False)
    else:
        def body(h, carry):
            first[rows(h), :] = dot(x_ref[rows(h), :], wr[...])
            return carry

        lax.fori_loop(0, 2, body, 0)

    def moments(ref):
        def body(h, carry):
            v = ref[rows(h), :]
            return (
                carry[0] + jnp.sum(v, axis=0, keepdims=True) * valid(h),
                carry[1] + jnp.sum(v * v, axis=0, keepdims=True) * valid(h),
            )

        zero = jnp.zeros((1, ref.shape[1]), F32)
        return jnp.concatenate(lax.fori_loop(0, 2, body, (zero, zero)), axis=0)

    def average_and_inverse(sums):
        mean = sums[0:1] / pixels
        return mean, lax.rsqrt(sums[1:2] / pixels - mean * mean + NORM_EPS)

    stat1 = statistics(r["st1"], owner, family, moments(first))

    wall, wallt, gf = r["wall"], r["wallt"], r["gf"]
    if own_gather:
        g_group.finish()
        for o in range(HD):
            gf[o * GB : (o + 1) * GB, :] = wg[o].astype(F32)[0:GB]
    else:
        gf[...] = r["wg_full"][...].astype(F32)

    def spread(t, carry):
        piece = gf[pl.ds(pl.multiple_of(t * GROUP, 8), GROUP), :]
        full = jnp.where(block_diagonal, jnp.concatenate([piece] * (MID // GROUP), axis=0), 0.0)
        wall[pl.ds(pl.multiple_of(t * MID, 16), MID), :] = full.astype(BF)
        wallt[pl.ds(pl.multiple_of((8 - t) * MID, 16), MID), :] = full.T.astype(BF)
        return carry

    lax.fori_loop(0, 9, spread, 0)
    if own_gather:
        g_expand.forward()
        for dz in range(1, H):
            o = lax.rem(z - dz + H, H) * D + y
            there = pl.ds(pl.multiple_of(o * EB, 128), EB)
            twin_in.append(send(expand_block(o), wep.at[:, there], x_peer))

    mean1, inv1 = average_and_inverse(total(r["st1"], stat1))
    gain1, shift1 = inner_ref[0:1, :], inner_ref[1:2, :]
    slope1 = r["slope1"]

    def activate(h):
        ok = valid(h)

        def body(w, carry):
            v = (first[tile(h, w), :] - mean1) * inv1
            v = v * gain1 + shift1
            q = jax.nn.sigmoid(v)
            a1[slab(h + 1, w + 1, N), :] = (v * q * ok).astype(BF)
            slope1[tile(h, w), :] = q * (1.0 + v * (1.0 - q)) * ok
            return carry

        lax.fori_loop(0, W, body, 0)

    class Halo:
        def __init__(self, ref):
            self.up = make(ref.at[slab(1, 1, R)], ref.at[slab(3, 1, R)], dev(H - 1, None, 0))
            self.down = make(ref.at[slab(2, 1, R)], ref.at[slab(0, 1, R)], dev(1, None, 0))

        def start_up(self):
            pl.when(z > 0)(self.up.start)

        def start_down(self):
            pl.when(z < H - 1)(self.down.start)

        def arrived(self):
            pl.when(z > 0)(self.down.wait_recv)
            pl.when(z < H - 1)(self.up.wait_recv)

        def sent(self):
            pl.when(z > 0)(self.up.wait_send)
            pl.when(z < H - 1)(self.down.wait_send)

    halo1, halo2 = Halo(a1), Halo(b2)
    activate(0)
    halo1.start_up()
    activate(1)
    halo1.start_down()

    def convolve(ref, weights, out, edge):
        def body(h, carry):
            if edge:
                hh, base, count = 3 * h, 6 * h, 1
            else:
                hh, base, count = 1, 3 * (1 - h), 2
            left = jnp.concatenate(
                [ref[slab(hh + i, kc, R), :] for i in range(count) for kc in range(3)], axis=1
            )
            part = dot(left, weights[pl.ds(pl.multiple_of(base * MID, 16), 3 * count * MID), :])
            out[rows(h), :] = out[rows(h), :] + part if edge else part
            return carry

        lax.fori_loop(0, 2, body, 0)

    second = r["second"]
    convolve(a1, wall, second, False)
    halo1.arrived()
    convolve(a1, wall, second, True)
    stat2 = statistics(r["st2"], owner, family, moments(second))
    if own_gather:
        g_expand.finish()
        for dy in range(1, D):
            for zz in range(H):
                o = zz * D + lax.rem(y + dy, D)
                there = pl.ds(pl.multiple_of(o * EB, 128), EB)
                twin_in.append(send(expand_block(o), wep.at[:, there], x_peer))
    mean2, inv2 = average_and_inverse(total(r["st2"], stat2))
    gain2, shift2 = inner_ref[2:3, :], inner_ref[3:4, :]
    a2, slope2 = r["a2"], r["slope2"]

    def activate_two(h):
        ok = valid(h)

        def body(w, carry):
            n = (second[tile(h, w), :] - mean2) * inv2
            second[tile(h, w), :] = n
            v = n * gain2 + shift2
            q = jax.nn.sigmoid(v)
            a2[tile(h, w), :] = (v * q * ok).astype(BF)
            slope2[tile(h, w), :] = q * (1.0 + v * (1.0 - q)) * ok
            return carry

        lax.fori_loop(0, W, body, 0)

    activate_two(1 - xp)
    ax_in = send(a2.at[rows(1 - xp)], r["ax"], x_peer)
    activate_two(xp)

    for copy in twin_in:
        copy.wait_recv()
    ax_in.wait_recv()
    third, tsend, trecv = r["third"], r["tsend"], r["trecv"]
    left = jnp.concatenate([a2[rows(xp), :], r["ax"][...]], axis=1)

    def expand(j, core):
        right = jnp.concatenate([we[:, quarter(j, core)], wep[:, quarter(j, core)]], axis=0)
        return dot(left, right)

    core_in = []
    for j in range(2):
        tsend[j] = expand(j, 1 - k).astype(BF)
        core_in.append(send(tsend.at[j], trecv.at[j], core_peer))
    for j in range(2):
        third[j] = expand(j, k)
    okx = valid(xp)
    sums = []
    for j in range(2):
        core_in[j].wait_recv()

        def body(w, carry):
            at = pl.ds(pl.multiple_of(w * N, 16), N)
            v = third[j, at, :] + trecv[j, at, :].astype(F32)
            third[j, at, :] = v
            return carry[0] + jnp.sum(v, axis=0, keepdims=True), carry[1] + jnp.sum(
                v * v, axis=0, keepdims=True
            )

        zero = jnp.zeros((1, OUT), F32)
        sums.append(lax.fori_loop(0, W, body, (zero, zero)))
    position = xp * HD + owner
    both = family + twin_family
    stat3 = statistics(
        r["st3"],
        position,
        both,
        jnp.concatenate(
            [jnp.concatenate([s[i] for s in sums], axis=1) * okx for i in range(2)], axis=0
        ),
    )
    ct_in.wait_recv()
    outer_in.wait_recv()
    mean3, inv3 = average_and_inverse(total(r["st3"], stat3))
    dpre, boj = r["dpre"], r["boj"]
    sums = []
    for j in range(2):
        lanes = slice(j * OUT, (j + 1) * OUT)
        m, iv = mean3[:, lanes], inv3[:, lanes]
        g, s = out2[j, 0:1, :], out2[j, 1:2, :]

        def body(w, carry):
            at = pl.ds(pl.multiple_of(w * N, 16), N)
            n = (third[j, at, :] - m) * iv
            third[j, at, :] = n
            v = n * g + s + x_ref[tile(xp, w), quarter(j, k)].astype(F32)
            q = jax.nn.sigmoid(v)
            boj[j, at, :] = (v * q * okx).astype(BF)
            d = ct2[j, at, :].astype(F32) * okx * (q * (1.0 + v * (1.0 - q)))
            dpre[j, at, :] = d
            return carry[0] + jnp.sum(d, axis=0, keepdims=True), carry[1] + jnp.sum(
                d * n, axis=0, keepdims=True
            )

        zero = jnp.zeros((1, OUT), F32)
        sums.append(lax.fori_loop(0, W, body, (zero, zero)))
    stat3b = statistics(
        r["st3b"],
        position,
        both,
        jnp.concatenate(
            [jnp.concatenate([s[i] for s in sums], axis=1) for i in range(2)], axis=0
        ),
    )
    a2t = r["a2t"]
    a2t[...] = a2[...].T
    total3 = total(r["st3b"], stat3b)
    r["tot3"][...] = total3
    piece = r["piece"]
    core_in = []
    for j in range(2):
        lanes = slice(j * OUT, (j + 1) * OUT)
        factor = out2[j, 0:1, :] * inv3[:, lanes] * okx
        sh = total3[0:1, lanes] / pixels
        ga = total3[1:2, lanes] / pixels

        def body(w, carry):
            at = pl.ds(pl.multiple_of(w * N, 16), N)
            v = factor * (dpre[j, at, :] - sh - third[j, at, :] * ga)
            piece[tile(xp, w), quarter(j, k)] = v.astype(BF)
            return carry

        lax.fori_loop(0, W, body, 0)
        part = piece.at[rows(xp), quarter(j, k)]
        core_in.append(send(part, part, core_peer))
    for copy in core_in:
        copy.wait_recv()
    agrad = r["agrad"]
    r["agsend"][...] = dot_nt(piece[rows(xp), :], wep[...]).astype(BF)
    ag_in = send(r["agsend"], r["agrecv"], x_peer)
    piece_in = []
    for j in range(2):
        part = piece.at[rows(xp), quarter(j, k)]
        piece_in.append(send(part, part, x_peer))
    agrad[rows(xp), :] = dot_nt(piece[rows(xp), :], we[...])

    def slope_two(h, received, carry):
        def body(w, carry):
            if received:
                up = r["agrecv"][pl.ds(pl.multiple_of(w * N, 16), N), :].astype(F32)
            else:
                up = agrad[tile(h, w), :]
            d = up * slope2[tile(h, w), :]
            agrad[tile(h, w), :] = d
            return carry[0] + jnp.sum(d, axis=0, keepdims=True), carry[1] + jnp.sum(
                d * second[tile(h, w), :], axis=0, keepdims=True
            )

        return lax.fori_loop(0, W, body, carry)

    zero = jnp.zeros((1, MID), F32)
    carry = slope_two(xp, False, (zero, zero))
    ag_in.wait_recv()
    carry = slope_two(1 - xp, True, carry)
    stat2b = statistics(r["st2b"], owner, family, jnp.concatenate(carry, axis=0))
    bo_in = send(boj.at[1 - xp], r["borecv"], x_peer)
    total2 = total(r["st2b"], stat2b)
    b2n = r["b2n"]

    def norm_two(h):
        factor = gain2 * inv2 * valid(h)
        sh, ga = total2[0:1] / pixels, total2[1:2] / pixels

        def body(w, carry):
            v = factor * (agrad[tile(h, w), :] - sh - second[tile(h, w), :] * ga)
            v = v.astype(BF)
            b2[slab(h + 1, w + 1, N), :] = v
            b2n[tile(h, w), :] = v
            return carry

        lax.fori_loop(0, W, body, 0)

    norm_two(0)
    halo2.start_up()
    norm_two(1)
    halo2.start_down()
    back1 = r["second_back"]
    convolve(b2, wallt, back1, False)
    b2t = r["b2t"]
    b2t[...] = b2n[...].T
    halo2.arrived()
    convolve(b2, wallt, back1, True)

    def slope_one(i, carry):
        h, w = lax.div(i, W), lax.rem(i, W)
        d = back1[tile(h, w), :] * slope1[tile(h, w), :]
        n = (first[tile(h, w), :] - mean1) * inv1
        first[tile(h, w), :] = n
        back1[tile(h, w), :] = d
        return carry[0] + jnp.sum(d, axis=0, keepdims=True), carry[1] + jnp.sum(
            d * n, axis=0, keepdims=True
        )

    carry = lax.fori_loop(0, 2 * W, slope_one, (zero, zero))
    stat1b = statistics(r["st1b"], owner, family, jnp.concatenate(carry, axis=0))

    core_in = []
    for j in range(2):
        piece_in[j].wait_recv()
        part = piece.at[rows(1 - xp), quarter(j, k)]
        core_in.append(send(part, part, core_peer))
    ggf = r["ggf"]
    fold = jnp.where(
        jnp.bitwise_and(lax.broadcasted_iota(jnp.int32, (GROUP, MID), 1), GROUP - 1)
        == lax.broadcasted_iota(jnp.int32, (GROUP, MID), 0),
        1.0,
        0.0,
    ).astype(BF)

    def group_grad(t, carry):
        kr, kc = lax.div(t, 3), lax.rem(t, 3)
        left = jnp.concatenate([a1[slab(kr, kc, R), :], a1[slab(kr + 1, kc, R), :]], axis=0)
        turned = jnp.where(block_diagonal, dot(b2t[...], left), 0.0).astype(BF)
        ggf[pl.ds(pl.multiple_of(t * GROUP, 8), GROUP), :] = dot_nt(fold, turned)
        return carry

    lax.fori_loop(0, 9, group_grad, 0)

    class Scatter:
        def __init__(self, name, block):
            self.block = block
            self.ys, self.yr = r[name + "_ys"], r[name + "_yr"]
            self.zs, self.zr = r[name + "_zs"], r[name + "_zr"]

        def start(self):
            self.along_y = []
            for dz in list(range(1, H)) + [0]:
                zi = lax.rem(z + dz, H)
                for dy in range(1, D):
                    n = (dy - 1) * H + dz
                    self.ys[n] = self.block(zi * D + lax.rem(y + dy, D)).astype(BF)
                    self.along_y.append((dz, n, send(self.ys.at[n], self.yr.at[n], dev(0, None, dy))))

        def middle(self):
            self.along_z = []
            for dz in list(range(1, H)) + [0]:
                value = self.block(lax.rem(z + dz, H) * D + y)
                for at, n, copy in self.along_y:
                    if at == dz:
                        copy.wait_recv()
                        value = value + self.yr[n].astype(F32)
                if dz:
                    self.zs[dz - 1] = value.astype(BF)
                    self.along_z.append(send(self.zs.at[dz - 1], self.zr.at[dz - 1], dev(dz, None, 0)))
                else:
                    self.own = value

        def finish(self):
            value = self.own
            for i, copy in enumerate(self.along_z):
                copy.wait_recv()
                value = value + self.zr[i].astype(F32)
            return value

    def wide(left_ref, right_ref, o):
        return dot(left_ref[...], right_ref[:, pl.ds(pl.multiple_of(o * EB, 128), EB)])

    for copy in core_in:
        copy.wait_recv()
    if own_gather:
        def group_part(o):
            return r["ggs"][o].astype(F32)

        for o in range(HD):
            r["ggs"][o] = jnp.concatenate(
                [ggf[o * GB : (o + 1) * GB, :], jnp.zeros((SLOT - GB, MID), F32)], axis=0
            )
        s_group = Scatter("gg", group_part)
        s_expand = Scatter("eg", lambda o: wide(a2t, piece, o))
        s_group.start()
        s_expand.start()
    else:
        r["group_out"][...] = ggf[...].astype(BF)
        r["expand_out"][...] = dot(a2t[...], piece[...]).astype(BF)

    total1 = total(r["st1b"], stat1b)
    b1 = r["b1"]

    def norm_one(i, carry):
        h, w = lax.div(i, W), lax.rem(i, W)
        factor = gain1 * inv1 * valid(h)
        sh, ga = total1[0:1] / pixels, total1[1:2] / pixels
        v = factor * (back1[tile(h, w), :] - sh - first[tile(h, w), :] * ga)
        b1[tile(h, w), :] = v.astype(BF)
        return carry

    lax.fori_loop(0, 2 * W, norm_one, 0)

    ipsend, iprecv, xsend, xrecv = r["ipsend"], r["iprecv"], r["xsend"], r["xrecv"]
    ig = r["ig"]

    def share(j, core, h):
        return dot_nt(b1[rows(h), :], wr[quarter(j, core), :])

    core_in = []
    for n, j in enumerate((1 - xp, xp)):
        for h in range(2):
            ipsend[n, rows(h), :] = share(j, 1 - k, h).astype(BF)
            core_in.append(send(ipsend.at[n, rows(h)], iprecv.at[n, rows(h)], core_peer))
        if n == 0:
            x_in = []
            for h in range(2):
                part = share(j, k, h)
                here = jnp.where(xp == h, 1.0, 0.0).astype(F32)
                core_in[h].wait_recv()
                part = part + iprecv[0, rows(h), :].astype(F32) + here * dpre[j]
                xsend[rows(h), :] = part.astype(BF)
                x_in.append(send(xsend.at[rows(h)], xrecv.at[rows(h)], x_peer))
    b1t = r["b1t"]
    b1t[...] = b1[...].T
    if own_gather:
        s_reduce = Scatter("rg", lambda o: wide(b1t, x_ref, o))
        s_group.middle()
        s_reduce.start()
        s_expand.middle()
    else:
        r["reduce_out"][...] = dot(b1t[...], x_ref[...]).astype(BF)
    for h in range(2):
        part = share(xp, k, h)
        here = jnp.where(xp == h, 1.0, 0.0).astype(F32)
        core_in[2 + h].wait_recv()
        ig[rows(h), :] = part + iprecv[1, rows(h), :].astype(F32) + here * dpre[xp]
    r["inner_grad"][...] = jnp.concatenate(
        [total1[1:2], total1[0:1], total2[1:2], total2[0:1]], axis=0
    )
    mine = r["tot3"][:, pl.ds(pl.multiple_of(xp * OUT, 128), OUT)]
    r["outer_grad"][...] = jnp.concatenate([mine[1:2], mine[0:1]], axis=0)
    bo = r["bo"]
    bo[rows(xp), :] = boj[xp]
    bo_in.wait_recv()
    bo[rows(1 - xp), :] = r["borecv"][...]
    if own_gather:
        s_reduce.middle()
        r["group_out"][...] = s_group.finish()[0:GB]
        r["expand_out"][...] = s_expand.finish()
        r["reduce_out"][...] = s_reduce.finish().T
    for h in range(2):
        x_in[h].wait_recv()
        ig[rows(h), :] = ig[rows(h), :] + xrecv[rows(h), :].astype(F32)
    for copy in sends:
        copy.wait_send()
    halo1.sent()
    halo2.sent()


def adamw_step(master, gradient, moment_one, moment_two, average, rate):
    first_new = 0.5 * moment_one + 0.5 * gradient
    second_new = 0.5 * moment_two + 0.5 * gradient * gradient
    correct = 1.0 - 0.5**STEP
    direction = first_new / correct / (jnp.sqrt(second_new / correct) + 1e-08)
    master_new = master - rate * (direction + 0.05 * master)
    average_new = 0.75 * average + 0.25 * master_new
    return (first_new, second_new, master_new, average_new)


def adamw_kernel(*refs):
    ins, outs = refs[:25], list(refs[25:])
    for n in range(5):
        gradient, master, one, two, average = (ref[...] for ref in ins[5 * n : 5 * n + 5])
        rate = CONV_RATE if n < 3 else NORM_RATE
        first, second, new, mean = adamw_step(master, gradient, one, two, average, rate)
        values = [gradient, first, second, new] + ([new.astype(BF)] if n < 3 else []) + [mean]
        for value in values:
            outs.pop(0)[...] = value


def step_sizes(leaves):
    return [jax.ShapeDtypeStruct(a.shape, a.dtype) for a in leaves]


def local(
    inputs, cotangent,
    reduce_master, reduce_first, reduce_second, reduce_average,
    group_master, group_first, group_second, group_average,
    expand_master, expand_first, expand_second, expand_average,
    inner_master, inner_first, inner_second, inner_average,
    outer_master, outer_first, outer_second, outer_average,
):
    N, rows, W, CIN = inputs.shape
    OUT = cotangent.shape[3]
    MID = inner_master.shape[1]
    H, D = lax.axis_size("height"), lax.axis_size("dp")
    HD = H * D
    R = W * N
    GB = group_master.shape[0]
    RB, EB = reduce_master.shape[0], expand_master.shape[1]
    own_gather = RB % 128 == 0 and EB % 128 == 0
    dims = dict(H=H, D=D, N=N, W=W, MID=MID, OUT=OUT, CIN=CIN, own_gather=own_gather)

    x = inputs.transpose(1, 2, 0, 3).reshape(rows * R, CIN)
    ct = cotangent.transpose(1, 2, 0, 3).reshape(rows * R, OUT)
    ins = dict(x=x, ct=ct, inner=inner_master, outer=outer_master)
    outs = dict(
        bo=((rows * R, OUT), BF),
        ig=((rows * R, OUT), F32),
        inner_grad=(inner_master.shape, F32),
        outer_grad=(outer_master.shape, F32),
    )
    scratch = dict(
        wep=((MID, CIN), BF),
        ct2=((2, R, OUT), BF),
        out2=((2, 2, OUT), F32),
        first=((2 * R, MID), F32),
        second=((2 * R, MID), F32),
        slope1=((2 * R, MID), F32),
        slope2=((2 * R, MID), F32),
        a1=((4 * (W + 2) * N, MID), BF),
        b2=((4 * (W + 2) * N, MID), BF),
        wall=((9 * MID, MID), BF),
        wallt=((9 * MID, MID), BF),
        gf=((9 * GROUP, MID), F32),
        ggf=((9 * GROUP, MID), F32),
        st1=((HD, 2, MID), F32),
        st2=((HD, 2, MID), F32),
        st3=((2 * HD, 2, 2 * OUT), F32),
        st3b=((2 * HD, 2, 2 * OUT), F32),
        st2b=((HD, 2, MID), F32),
        st1b=((HD, 2, MID), F32),
        tot3=((2, 2 * OUT), F32),
        a2=((2 * R, MID), BF),
        a2t=((MID, 2 * R), BF),
        ax=((R, MID), BF),
        third=((2, R, OUT), F32),
        tsend=((2, R, OUT), BF),
        trecv=((2, R, OUT), BF),
        dpre=((2, R, OUT), F32),
        boj=((2, R, OUT), BF),
        borecv=((R, OUT), BF),
        piece=((2 * R, CIN), BF),
        agrad=((2 * R, MID), F32),
        agsend=((R, MID), BF),
        agrecv=((R, MID), BF),
        b2n=((2 * R, MID), BF),
        b2t=((MID, 2 * R), BF),
        second_back=((2 * R, MID), F32),
        b1=((2 * R, MID), BF),
        b1t=((MID, 2 * R), BF),
        ipsend=((2, 2 * R, OUT), BF),
        iprecv=((2, 2 * R, OUT), BF),
        xsend=((2 * R, OUT), BF),
        xrecv=((2 * R, OUT), BF),
    )
    if own_gather:
        ins.update(rm=reduce_master, gm=group_master, em=expand_master)
        outs.update(
            reduce_out=((RB, MID), F32), group_out=((GB, MID), F32), expand_out=((MID, EB), F32)
        )
        scratch.update(
            wr=((CIN, MID), BF), we=((MID, CIN), BF), wg=((HD, SLOT, MID), BF),
            ggs=((HD, SLOT, MID), F32),
        )
        for name, shape in (("rg", (MID, RB)), ("eg", (MID, EB)), ("gg", (SLOT, MID))):
            scratch[name + "_ys"] = scratch[name + "_yr"] = (((D - 1) * H, *shape), BF)
            scratch[name + "_zs"] = scratch[name + "_zr"] = ((H - 1, *shape), BF)
    else:
        both = ("height", "dp")
        ins.update(
            wr_full=lax.all_gather(reduce_master.astype(BF), both, axis=0, tiled=True),
            wg_full=lax.all_gather(group_master.astype(BF), both, axis=0, tiled=True),
            we_full=lax.all_gather(expand_master.astype(BF), both, axis=1, tiled=True),
        )
        outs.update(
            reduce_out=((MID, CIN), BF),
            group_out=((9 * GROUP, MID), BF),
            expand_out=((MID, CIN), BF),
        )
    names = [*ins, *outs, *scratch, "ssem", "rsem"]
    whole = pl.BlockSpec(memory_space=pltpu.VMEM)
    results = pl.pallas_call(
        functools.partial(block_kernel, names, dims),
        out_shape=[jax.ShapeDtypeStruct(*v) for v in outs.values()],
        in_specs=[whole] * len(ins),
        out_specs=[whole] * len(outs),
        scratch_shapes=[pltpu.VMEM(*v) for v in scratch.values()]
        + [pltpu.SemaphoreType.DMA((dims.get("semaphores", SEMAPHORES + 16 * D),))] * 2,
        compiler_params=pltpu.CompilerParams(
            collective_id=0, has_side_effects=True, vmem_limit_bytes=56 << 20
        ),
        name="block",
    )(*ins.values())
    got = dict(zip(outs, results, strict=True))
    block_out = got["bo"].reshape(rows, W, N, OUT).transpose(2, 0, 1, 3)
    input_grad = got["ig"].reshape(rows, W, N, OUT).transpose(2, 0, 1, 3)
    reduce_grad, group_grad, expand_grad = got["reduce_out"], got["group_out"], got["expand_out"]
    if not own_gather:
        both = ("height", "dp")
        reduce_grad = lax.psum_scatter(reduce_grad.T, both, scatter_dimension=0, tiled=True).astype(F32)
        group_grad = lax.psum_scatter(group_grad, both, scatter_dimension=0, tiled=True).astype(F32)
        expand_grad = lax.psum_scatter(expand_grad, both, scatter_dimension=1, tiled=True).astype(F32)
    groups = (
        (reduce_grad, reduce_master, reduce_first, reduce_second, reduce_average),
        (group_grad, group_master, group_first, group_second, group_average),
        (expand_grad, expand_master, expand_first, expand_second, expand_average),
        (got["inner_grad"], inner_master, inner_first, inner_second, inner_average),
        (got["outer_grad"], outer_master, outer_first, outer_second, outer_average),
    )
    shapes = []
    for n, group in enumerate(groups):
        kinds = [F32] * 4 + ([BF] if n < 3 else []) + [F32]
        shapes += [jax.ShapeDtypeStruct(group[0].shape, kind) for kind in kinds]
    flat = [a for group in groups for a in group]
    news = pl.pallas_call(
        adamw_kernel,
        out_shape=shapes,
        in_specs=[whole] * len(flat),
        out_specs=[whole] * len(shapes),
        compiler_params=pltpu.CompilerParams(vmem_limit_bytes=32 << 20),
        name="adamw",
    )(*flat)
    return (block_out, input_grad, *news)


def solution(mesh):
    pixel = P("dp", "height", None, "chan")
    first = P(("height", "dp"), "chan")
    last = P("chan", ("height", "dp"))
    table = P(None, "chan")
    return jax.shard_map(
        local,
        mesh=mesh,
        in_specs=(P("dp", "height", None, None), pixel)
        + (first,) * 8
        + (last,) * 4
        + (table,) * 8,
        out_specs=(pixel, pixel) + (first,) * 12 + (last,) * 6 + (table,) * 10,
        check_vma=False,
    )
```

```python
import functools

import jax
import jax.numpy as jnp
from jax import lax
from jax.experimental import pallas as pl
from jax.experimental.pallas import tpu as pltpu
from jax.sharding import PartitionSpec as P

GROUP = 32
HEIGHT = 7
STEP = 10
NORM_EPS = 1e-05
CONV_RATE = 0.02
NORM_RATE = 0.3

BF = jnp.bfloat16
F32 = jnp.float32
MESH = pl.DeviceIdType.MESH
SEMAPHORES = 192
SLOT = 48


def dot(a, b):
    return jnp.dot(a, b, preferred_element_type=F32)


def dot_nt(a, b):
    return lax.dot_general(a, b, (((1,), (1,)), ((), ())), preferred_element_type=F32)


def block_kernel(names, dims, *refs):
    r = dict(zip(names, refs, strict=True))
    H, D, N, W, MID, OUT, CIN = (dims[k] for k in ("H", "D", "N", "W", "MID", "OUT", "CIN"))
    own_gather = dims["own_gather"]
    R = W * N
    PITCH = (W + 2) * N
    HD = H * D
    pixels = float(N * D * HEIGHT * W)
    x_ref, ct_ref, inner_ref, outer_ref = r["x"], r["ct"], r["inner"], r["outer"]

    z = lax.axis_index("height")
    c = lax.axis_index("chan")
    y = lax.axis_index("dp")
    xp = lax.div(c, 2)
    k = lax.rem(c, 2)
    cx = lax.rem(c + 2, 4)
    cc = c + 1 - 2 * k
    owner = z * D + y

    def dev(dz=0, chan=None, dy=0):
        return {
            "height": lax.rem(z + dz, H),
            "chan": c if chan is None else chan,
            "dp": lax.rem(y + dy, D),
        }

    offsets = [(dz, dy) for dz in range(H) for dy in range(D)]
    family = [dev(dz, None, dy) for dz, dy in offsets if dz or dy]
    twin_family = [dev(dz, cx, dy) for dz, dy in offsets]
    core_peer = dev(0, cc, 0)
    x_peer = dev(0, cx, 0)
    diagonal = dev(0, cx + 1 - 2 * k, 0)

    def rows(h):
        return pl.ds(pl.multiple_of(h * R, 16), R)

    def tile(h, w):
        return pl.ds(pl.multiple_of(h * R + w * N, 16), N)

    def slab(hh, ww, count):
        return pl.ds(pl.multiple_of((hh * (W + 2) + ww) * N, 16), count)

    def quarter(j, core):
        return pl.ds(pl.multiple_of((2 * j + core) * OUT, 128), OUT)

    def valid(h):
        return jnp.where(z * 2 + h < HEIGHT, 1.0, 0.0).astype(F32)

    sends = []
    used = [0]

    def make(src, dst, target, at=None):
        if at is None:
            at = (used[0], used[0])
            used[0] += 1
        return pltpu.make_async_remote_copy(
            src_ref=src,
            dst_ref=dst,
            send_sem=r["ssem"].at[at[0]],
            recv_sem=r["rsem"].at[at[1]],
            device_id=target,
            device_id_type=MESH,
        )

    def send(src, dst, target):
        copy = make(src, dst, target)
        copy.start()
        sends.append(copy)
        return copy

    a1, b2 = r["a1"], r["b2"]
    a1[...] = jnp.zeros(a1.shape, BF)
    b2[...] = jnp.zeros(b2.shape, BF)
    lane_group = lax.shift_right_logical(lax.broadcasted_iota(jnp.int32, (MID, MID), 1), 5)
    row_group = lax.shift_right_logical(lax.broadcasted_iota(jnp.int32, (MID, MID), 0), 5)
    block_diagonal = lane_group == row_group
    if own_gather:
        wr, we, wg = r["wr"], r["we"], r["wg"]
        RB, EB = r["rm"].shape[0], r["em"].shape[1]
        GB = r["gm"].shape[0]

        def reduce_block(o):
            return wr.at[pl.ds(pl.multiple_of(o * RB, 16), RB), :]

        def expand_block(o):
            return we.at[:, pl.ds(pl.multiple_of(o * EB, 128), EB)]

        def group_block(o):
            return wg.at[o]

        reduce_block(owner)[...] = r["rm"][...].astype(BF)
        expand_block(owner)[...] = r["em"][...].astype(BF)
        wg[owner] = jnp.concatenate(
            [r["gm"][...], jnp.zeros((SLOT - GB, MID), F32)], axis=0
        ).astype(BF)
    else:
        wr, we = r["wr_full"], r["we_full"]

    barrier = pltpu.get_barrier_semaphore()
    everyone = family + twin_family + [core_peer, diagonal]
    for target in everyone:
        pl.semaphore_signal(barrier, inc=1, device_id=target, device_id_type=MESH)
    pl.semaphore_wait(barrier, len(everyone))

    near = [z + 1 - 2 * lax.rem(z, 2), jnp.where(z < 2, 2, 1), jnp.where(z < 2, 3, 0)]

    class Gather:
        def __init__(self, block):
            self.block = block
            self.here = block(owner)
            self.base = used[0]
            used[0] += H
            self.along_y = []

        def send_z(self, rank):
            target = {"height": near[rank], "chan": c, "dp": y}
            copy = make(self.here, self.here, target, (self.base + rank, self.base + z))
            copy.start()
            sends.append(copy)

        def send_y(self):
            self.pass_on(self.here)

        def pass_on(self, block):
            self.along_y.append([send(block, block, dev(0, None, dy)) for dy in range(1, D)])

        def forward(self, rank):
            source = near[rank]
            block = self.block(source * D + y)
            make(block, block, dev(), (self.base, self.base + source)).wait_recv()
            self.pass_on(block)
            return source

        def finish(self, number):
            for copy in self.along_y[number]:
                copy.wait_recv()

    if own_gather:
        g_reduce, g_group, g_expand = Gather(reduce_block), Gather(group_block), Gather(expand_block)
        for rank in range(3):
            g_reduce.send_z(rank)
        g_reduce.send_y()
        for rank in range(3):
            g_group.send_z(rank)
        g_group.send_y()
    ct2, out2 = r["ct2"], r["out2"]
    ct_in = send(ct_ref.at[rows(1 - xp)], ct2.at[xp], x_peer)
    ct2[xp] = ct_ref[rows(xp), :]
    out2[xp] = outer_ref[...]
    outer_in = send(out2.at[xp], out2.at[xp], x_peer)
    wep = r["wep"]
    twin_in = []

    def twin(o):
        twin_in.append(
            send(expand_block(o), wep.at[:, pl.ds(pl.multiple_of(o * EB, 128), EB)], x_peer)
        )

    def twin_y(number, zz):
        g_expand.finish(number)
        for dy in range(1, D):
            twin(zz * D + lax.rem(y + dy, D))

    if own_gather:
        g_expand.send_z(0)
        g_expand.send_z(1)
        g_expand.send_y()
        twin(owner)
    else:
        twin_in.append(send(we, wep, x_peer))

    def statistics(buf, position, targets, value):
        buf[position] = value
        return [send(buf.at[position], buf.at[position], t) for t in targets]

    def total(buf, copies):
        for copy in copies:
            copy.wait_recv()
        return jnp.sum(buf[...], axis=0)

    first = r["first"]

    def product(blocks, start):
        def body(h, carry):
            left = jnp.concatenate(
                [x_ref[rows(h), pl.ds(pl.multiple_of(o * RB, 128), RB)] for o in blocks], axis=1
            )
            right = jnp.concatenate([reduce_block(o)[...] for o in blocks], axis=0)
            part = dot(left, right)
            first[rows(h), :] = part if start else first[rows(h), :] + part
            return carry

        lax.fori_loop(0, 2, body, 0)

    if own_gather:
        for rank in range(3):
            g_reduce.forward(rank)
        product([zz * D + y for zz in range(H)], True)
        for rank in range(3):
            g_group.forward(rank)
        for number in range(4):
            g_reduce.finish(number)
        for dy in range(1, D):
            product([zz * D + lax.rem(y + dy, D) for zz in range(H)], False)
    else:
        def body(h, carry):
            first[rows(h), :] = dot(x_ref[rows(h), :], wr[...])
            return carry

        lax.fori_loop(0, 2, body, 0)

    def moments(ref):
        def body(h, carry):
            v = ref[rows(h), :]
            return (
                carry[0] + jnp.sum(v, axis=0, keepdims=True) * valid(h),
                carry[1] + jnp.sum(v * v, axis=0, keepdims=True) * valid(h),
            )

        zero = jnp.zeros((1, ref.shape[1]), F32)
        return jnp.concatenate(lax.fori_loop(0, 2, body, (zero, zero)), axis=0)

    def average_and_inverse(sums):
        mean = sums[0:1] / pixels
        return mean, lax.rsqrt(sums[1:2] / pixels - mean * mean + NORM_EPS)

    stat1 = statistics(r["st1"], owner, family, moments(first))

    wall, wallt, gf = r["wall"], r["wallt"], r["gf"]
    if own_gather:
        g_expand.send_z(2)
        sources = [z] + [g_expand.forward(rank) for rank in range(2)]
        for source in sources[1:]:
            twin(source * D + y)
        twin_y(0, z)
        for number in range(4):
            g_group.finish(number)
        for o in range(HD):
            gf[o * GB : (o + 1) * GB, :] = wg[o].astype(F32)[0:GB]
    else:
        gf[...] = r["wg_full"][...].astype(F32)

    def spread(t, carry):
        piece = gf[pl.ds(pl.multiple_of(t * GROUP, 8), GROUP), :]
        full = jnp.where(block_diagonal, jnp.concatenate([piece] * (MID // GROUP), axis=0), 0.0)
        wall[pl.ds(pl.multiple_of(t * MID, 16), MID), :] = full.astype(BF)
        wallt[pl.ds(pl.multiple_of((8 - t) * MID, 16), MID), :] = full.T.astype(BF)
        return carry

    lax.fori_loop(0, 9, spread, 0)
    mean1, inv1 = average_and_inverse(total(r["st1"], stat1))
    gain1, shift1 = inner_ref[0:1, :], inner_ref[1:2, :]
    slope1 = r["slope1"]

    def activate(h):
        ok = valid(h)

        def body(w, carry):
            v = (first[tile(h, w), :] - mean1) * inv1
            v = v * gain1 + shift1
            q = jax.nn.sigmoid(v)
            a1[slab(h + 1, w + 1, N), :] = (v * q * ok).astype(BF)
            slope1[tile(h, w), :] = q * (1.0 + v * (1.0 - q)) * ok
            return carry

        lax.fori_loop(0, W, body, 0)

    class Halo:
        def __init__(self, ref):
            self.up = make(ref.at[slab(1, 1, R)], ref.at[slab(3, 1, R)], dev(H - 1, None, 0))
            self.down = make(ref.at[slab(2, 1, R)], ref.at[slab(0, 1, R)], dev(1, None, 0))

        def start_up(self):
            pl.when(z > 0)(self.up.start)

        def start_down(self):
            pl.when(z < H - 1)(self.down.start)

        def arrived(self):
            pl.when(z > 0)(self.down.wait_recv)
            pl.when(z < H - 1)(self.up.wait_recv)

        def sent(self):
            pl.when(z > 0)(self.up.wait_send)
            pl.when(z < H - 1)(self.down.wait_send)

    halo1, halo2 = Halo(a1), Halo(b2)
    activate(0)
    halo1.start_up()
    activate(1)
    halo1.start_down()

    def convolve(ref, weights, out, edge):
        def body(h, carry):
            if edge:
                hh, base, count = 3 * h, 6 * h, 1
            else:
                hh, base, count = 1, 3 * (1 - h), 2
            left = jnp.concatenate(
                [ref[slab(hh + i, kc, R), :] for i in range(count) for kc in range(3)], axis=1
            )
            part = dot(left, weights[pl.ds(pl.multiple_of(base * MID, 16), 3 * count * MID), :])
            out[rows(h), :] = out[rows(h), :] + part if edge else part
            return carry

        lax.fori_loop(0, 2, body, 0)

    second = r["second"]
    convolve(a1, wall, second, False)
    if own_gather:
        sources.append(g_expand.forward(2))
        twin(sources[3] * D + y)
        twin_y(1, sources[1])
        twin_y(2, sources[2])
    halo1.arrived()
    convolve(a1, wall, second, True)
    stat2 = statistics(r["st2"], owner, family, moments(second))
    if own_gather:
        twin_y(3, sources[3])
    mean2, inv2 = average_and_inverse(total(r["st2"], stat2))
    gain2, shift2 = inner_ref[2:3, :], inner_ref[3:4, :]
    a2, slope2 = r["a2"], r["slope2"]

    def activate_two(h):
        ok = valid(h)

        def body(w, carry):
            n = (second[tile(h, w), :] - mean2) * inv2
            second[tile(h, w), :] = n
            v = n * gain2 + shift2
            q = jax.nn.sigmoid(v)
            a2[tile(h, w), :] = (v * q * ok).astype(BF)
            slope2[tile(h, w), :] = q * (1.0 + v * (1.0 - q)) * ok
            return carry

        lax.fori_loop(0, W, body, 0)

    activate_two(1 - xp)
    ax_in = send(a2.at[rows(1 - xp)], r["ax"], x_peer)
    activate_two(xp)

    for copy in twin_in:
        copy.wait_recv()
    ax_in.wait_recv()
    third, tsend, trecv = r["third"], r["tsend"], r["trecv"]
    left = jnp.concatenate([a2[rows(xp), :], r["ax"][...]], axis=1)

    def expand(j, core):
        right = jnp.concatenate([we[:, quarter(j, core)], wep[:, quarter(j, core)]], axis=0)
        return dot(left, right)

    core_in = []
    for j in range(2):
        tsend[j] = expand(j, 1 - k).astype(BF)
        core_in.append(send(tsend.at[j], trecv.at[j], core_peer))
    for j in range(2):
        third[j] = expand(j, k)
    okx = valid(xp)
    sums = []
    for j in range(2):
        core_in[j].wait_recv()

        def body(w, carry):
            at = pl.ds(pl.multiple_of(w * N, 16), N)
            v = third[j, at, :] + trecv[j, at, :].astype(F32)
            third[j, at, :] = v
            return carry[0] + jnp.sum(v, axis=0, keepdims=True), carry[1] + jnp.sum(
                v * v, axis=0, keepdims=True
            )

        zero = jnp.zeros((1, OUT), F32)
        sums.append(lax.fori_loop(0, W, body, (zero, zero)))
    r["tx"][...] = third[1 - xp].astype(BF)
    position = xp * HD + owner
    both = family + twin_family
    stat3 = statistics(
        r["st3"],
        position,
        both,
        jnp.concatenate(
            [jnp.concatenate([s[i] for s in sums], axis=1) * okx for i in range(2)], axis=0
        ),
    )
    cut = (W + 1) // 2
    parts = [pl.ds(0, cut * N), pl.ds(cut * N, (W - cut) * N)]
    tx_in = [send(r["tx"].at[parts[0]], r["tother"].at[parts[0]], x_peer)]
    wrq = r["wrq"]

    def mids(chan):
        return pl.ds(pl.multiple_of(chan * MID, 128), MID)

    wrq[:, mids(c)] = wr[quarter(xp, k), :]
    wrq_in = [send(wr.at[quarter(xp, 1 - k), :], wrq.at[:, mids(c)], core_peer)]
    share = OUT // 2

    def send_wrq(n):
        target, core = ((x_peer, k), (diagonal, 1 - k))[n // 2]
        at = pl.ds(pl.multiple_of((2 * (1 - xp) + core) * OUT + n % 2 * share, 16), share)
        there = wrq.at[pl.ds(n % 2 * share, share), mids(c)]
        wrq_in.append(send(wr.at[at, :], there, target))

    a2t = r["a2t"]
    a2t[...] = a2[...].T
    ct_in.wait_recv()
    outer_in.wait_recv()
    mean3, inv3 = average_and_inverse(total(r["st3"], stat3))
    dpre, dother, bo = r["dpre"], r["dother"], r["bo"]
    mi3 = r["mi3"]
    for j in range(2):
        lanes = slice(j * OUT, (j + 1) * OUT)
        mi3[j] = jnp.concatenate([mean3[:, lanes], inv3[:, lanes]], axis=0)

    def outer_norm(j, h, values, grads, write, start=0, stop=W):
        m, iv = mi3[j, 0:1, :], mi3[j, 1:2, :]
        g, s = out2[j, 0:1, :], out2[j, 1:2, :]
        ok = valid(h)

        def body(w, carry):
            at = pl.ds(pl.multiple_of(w * N, 16), N)
            n = (values[0](at) - m) * iv
            values[1](at, n)
            v = n * g + s + x_ref[tile(h, w), quarter(j, k)].astype(F32)
            q = jax.nn.sigmoid(v)
            if write:
                bo[tile(h, w), :] = (v * q * ok).astype(BF)
            d = grads[0](at, w) * ok * (q * (1.0 + v * (1.0 - q)))
            grads[1](at, d)
            return carry[0] + jnp.sum(d, axis=0, keepdims=True), carry[1] + jnp.sum(
                d * n, axis=0, keepdims=True
            )

        zero = jnp.zeros((1, OUT), F32)
        return lax.fori_loop(start, stop, body, (zero, zero))

    def third_access(j):
        def get(at):
            return third[j, at, :]

        def put(at, n):
            third[j, at, :] = n

        def get_ct(at, w):
            return ct2[j, at, :].astype(F32)

        def put_d(at, d):
            dpre[j, at, :] = d

        return (get, put), (get_ct, put_d)

    st3b = r["st3b"]
    pair = r["pair"]
    for j, write in ((xp, True), (1 - xp, False)):
        pair[j] = jnp.concatenate(outer_norm(j, xp, *third_access(j), write), axis=0)
    stat3b = statistics(st3b, position, both, jnp.concatenate([pair[0], pair[1]], axis=1))

    tx_in.append(send(r["tx"].at[parts[1]], r["tother"].at[parts[1]], x_peer))
    send_wrq(0)
    tx_in[0].wait_recv()
    nother = r["nother"]

    def get_other(at):
        return r["tother"][at, :].astype(F32)

    def put_other(at, n):
        nother[at, :] = n

    def get_ct_other(at, w):
        return ct_ref[tile(1 - xp, w), :].astype(F32)

    def put_d_other(at, d):
        dother[at, :] = d

    other_row = ((get_other, put_other), (get_ct_other, put_d_other), True)
    outer_norm(xp, 1 - xp, *other_row, 0, cut)
    total3 = total(st3b, stat3b)
    r["tot3"][...] = total3
    for j in range(2):
        lanes = slice(j * OUT, (j + 1) * OUT)
        pair[j] = total3[:, lanes] / pixels
    piece = r["piece"]

    def back_three(j, h, upstream, normed):
        factor = out2[j, 0:1, :] * mi3[j, 1:2, :] * valid(h)
        sh, ga = pair[j, 0:1, :], pair[j, 1:2, :]

        def body(w, carry):
            at = pl.ds(pl.multiple_of(w * N, 16), N)
            v = factor * (upstream(at) - sh - normed(at) * ga)
            piece[tile(h, w), quarter(j, k)] = v.astype(BF)
            return carry

        lax.fori_loop(0, W, body, 0)
        part = piece.at[rows(h), quarter(j, k)]
        return send(part, part, core_peer)

    core_in = [
        back_three(j, xp, lambda at, j=j: dpre[j, at, :], lambda at, j=j: third[j, at, :])
        for j in range(2)
    ]
    for copy in core_in:
        copy.wait_recv()
    agrad = r["agrad"]
    r["agsend"][...] = dot_nt(piece[rows(xp), :], wep[...]).astype(BF)
    ag_in = send(r["agsend"], r["agrecv"], x_peer)
    part = piece.at[rows(xp), quarter(xp, k)]
    piece_in = send(part, part, x_peer)
    for n in range(1, 4):
        send_wrq(n)
    agrad[rows(xp), :] = dot_nt(piece[rows(xp), :], we[...])
    tx_in[1].wait_recv()
    outer_norm(xp, 1 - xp, *other_row, cut, W)
    core_other = back_three(xp, 1 - xp, lambda at: dother[at, :], lambda at: nother[at, :])

    class Scatter:
        def __init__(self, name, block):
            self.block = block
            self.ys, self.yr = r[name + "_ys"], r[name + "_yr"]
            self.zs, self.zr = r[name + "_zs"], r[name + "_zr"]
            self.own = r[name + "_own"]
            self.along_y, self.along_z = {}, []
            self.base = used[0]
            used[0] += H

        def start(self, targets):
            for slot, zi in targets:
                self.along_y[slot] = []
                for dy in range(1, D):
                    n = (dy - 1) * H + slot
                    self.ys[n] = self.block(zi * D + lax.rem(y + dy, D)).astype(BF)
                    self.along_y[slot].append(
                        (n, send(self.ys.at[n], self.yr.at[n], dev(0, None, dy)))
                    )

        def middle(self, targets):
            for slot, zi in targets:
                value = self.block(zi * D + y)
                for n, copy in self.along_y[slot]:
                    copy.wait_recv()
                    value = value + self.yr[n].astype(F32)
                other = zi != z

                @pl.when(jnp.logical_not(other))
                def keep():
                    self.own[...] = value

                self.zs[slot] = value.astype(BF)
                target = {"height": zi, "chan": c, "dp": y}
                at = (self.base + slot, self.base + z)
                copy = make(self.zs.at[slot], self.zr.at[z], target, at)
                pl.when(other)(copy.start)
                self.along_z.append((other, copy))

        def finish(self):
            value = self.own[...]
            for dz in range(1, H):
                s = lax.rem(z + dz, H)
                at = (self.base, self.base + s)
                make(self.zs.at[0], self.zr.at[s], dev(dz), at).wait_recv()
                value = value + self.zr[s].astype(F32)
            return value

        def sent(self):
            for other, copy in self.along_z:
                pl.when(other)(copy.wait_send)

    def wide(left_ref, right_ref, o):
        return dot(left_ref[...], right_ref[:, pl.ds(pl.multiple_of(o * EB, 128), EB)])

    def slope_two(h, received, carry):
        def body(w, carry):
            if received:
                up = r["agrecv"][pl.ds(pl.multiple_of(w * N, 16), N), :].astype(F32)
            else:
                up = agrad[tile(h, w), :]
            d = up * slope2[tile(h, w), :]
            agrad[tile(h, w), :] = d
            return carry[0] + jnp.sum(d, axis=0, keepdims=True), carry[1] + jnp.sum(
                d * second[tile(h, w), :], axis=0, keepdims=True
            )

        return lax.fori_loop(0, W, body, carry)

    zero = jnp.zeros((1, MID), F32)
    carry = slope_two(xp, False, (zero, zero))
    half = H // 2
    early = [(i, xp * half + i) for i in range(half)]
    late = [(half + i, (1 - xp) * half + i) for i in range(half)]
    around = [(0, lax.rem(z + 2, 4)), (1, 3 - z), (2, near[0]), (3, z)]
    if own_gather:
        s_expand = Scatter("eg", lambda o: wide(a2t, piece, o))
    ag_in.wait_recv()
    carry = slope_two(1 - xp, True, carry)
    stat2b = statistics(r["st2b"], owner, family, jnp.concatenate(carry, axis=0))
    if own_gather:
        core_other.wait_recv()
        s_expand.start(early)
    total2 = total(r["st2b"], stat2b)
    b2n = r["b2n"]

    def norm_two(h):
        factor = gain2 * inv2 * valid(h)
        sh, ga = total2[0:1] / pixels, total2[1:2] / pixels

        def body(w, carry):
            v = factor * (agrad[tile(h, w), :] - sh - second[tile(h, w), :] * ga)
            v = v.astype(BF)
            b2[slab(h + 1, w + 1, N), :] = v
            b2n[tile(h, w), :] = v
            return carry

        lax.fori_loop(0, W, body, 0)

    norm_two(0)
    halo2.start_up()
    norm_two(1)
    halo2.start_down()
    back1 = r["second_back"]
    convolve(b2, wallt, back1, False)
    b2t = r["b2t"]
    b2t[...] = b2n[...].T
    ggf = r["ggf"]
    fold = jnp.where(
        jnp.bitwise_and(lax.broadcasted_iota(jnp.int32, (GROUP, MID), 1), GROUP - 1)
        == lax.broadcasted_iota(jnp.int32, (GROUP, MID), 0),
        1.0,
        0.0,
    ).astype(BF)

    def group_grad(t, carry):
        kr, kc = lax.div(t, 3), lax.rem(t, 3)
        left = jnp.concatenate([a1[slab(kr, kc, R), :], a1[slab(kr + 1, kc, R), :]], axis=0)
        turned = jnp.where(block_diagonal, dot(b2t[...], left), 0.0).astype(BF)
        ggf[pl.ds(pl.multiple_of(t * GROUP, 8), GROUP), :] = dot_nt(fold, turned)
        return carry

    lax.fori_loop(0, 9, group_grad, 0)

    piece_in.wait_recv()
    part = piece.at[rows(1 - xp), quarter(1 - xp, k)]
    core_last = send(part, part, core_peer)
    halo2.arrived()
    convolve(b2, wallt, back1, True)

    def slope_one(i, carry):
        h, w = lax.div(i, W), lax.rem(i, W)
        d = back1[tile(h, w), :] * slope1[tile(h, w), :]
        n = (first[tile(h, w), :] - mean1) * inv1
        first[tile(h, w), :] = n
        back1[tile(h, w), :] = d
        return carry[0] + jnp.sum(d, axis=0, keepdims=True), carry[1] + jnp.sum(
            d * n, axis=0, keepdims=True
        )

    carry = lax.fori_loop(0, 2 * W, slope_one, (zero, zero))
    stat1b = statistics(r["st1b"], owner, family, jnp.concatenate(carry, axis=0))

    core_last.wait_recv()
    if not own_gather:
        core_other.wait_recv()
    if own_gather:
        s_expand.middle(early)
        s_expand.start(late)
        for o in range(HD):
            r["ggs"][o] = jnp.concatenate(
                [ggf[o * GB : (o + 1) * GB, :], jnp.zeros((SLOT - GB, MID), F32)], axis=0
            )
        s_group = Scatter("gg", lambda o: r["ggs"][o])
        s_group.start(around)
    else:
        r["group_out"][...] = ggf[...].astype(BF)
        r["expand_out"][...] = dot(a2t[...], piece[...]).astype(BF)

    total1 = total(r["st1b"], stat1b)
    b1, ball = r["b1"], r["ball"]

    def norm_one(h):
        factor = gain1 * inv1 * valid(h)
        sh, ga = total1[0:1] / pixels, total1[1:2] / pixels

        def body(w, carry):
            v = factor * (back1[tile(h, w), :] - sh - first[tile(h, w), :] * ga)
            v = v.astype(BF)
            b1[tile(h, w), :] = v
            ball[tile(h, w), mids(c)] = v
            return carry

        lax.fori_loop(0, W, body, 0)

    ball_x, ball_core, ball_far = [], [], []
    for h in range(2):
        norm_one(h)
        part = ball.at[rows(h), mids(c)]
        ball_x.append(send(part, part, x_peer))
        ball_core.append(send(part, part, core_peer))

    def forward_ball(h):
        ball_x[h].wait_recv()
        part = ball.at[rows(h), mids(cx)]
        ball_far.append(send(part, part, core_peer))

    b1t = r["b1t"]
    b1t[...] = b1[...].T
    if own_gather:
        s_reduce = Scatter("rg", lambda o: wide(b1t, x_ref, o))
        s_reduce.start(around)
        s_expand.middle(late)
        s_group.middle(around)
        s_reduce.middle(around[0:1])
        forward_ball(0)
        s_reduce.middle(around[1:2])
        forward_ball(1)
        s_reduce.middle(around[2:3])
    else:
        forward_ball(0)
        forward_ball(1)
        r["reduce_out"][...] = dot(b1t[...], x_ref[...]).astype(BF)
    ig = r["ig"]

    def chip_mids(n):
        return pl.ds(pl.multiple_of(n * 2 * MID, 128), 2 * MID)

    r["inner_grad"][...] = jnp.concatenate(
        [total1[1:2], total1[0:1], total2[1:2], total2[0:1]], axis=0
    )
    mine = r["tot3"][:, pl.ds(pl.multiple_of(xp * OUT, 128), OUT)]
    r["outer_grad"][...] = jnp.concatenate([mine[1:2], mine[0:1]], axis=0)
    for copy in wrq_in:
        copy.wait_recv()
    ig[rows(xp), :] = dpre[xp]
    ig[rows(1 - xp), :] = dother[...]

    def input_part(h, n):
        ig[rows(h), :] = ig[rows(h), :] + dot_nt(ball[rows(h), chip_mids(n)], wrq[:, chip_mids(n)])

    for h in range(2):
        ball_core[h].wait_recv()
        input_part(h, xp)
    if own_gather:
        s_reduce.middle(around[3:])
    for h in range(2):
        ball_far[h].wait_recv()
        input_part(h, 1 - xp)
    if own_gather:
        r["group_out"][...] = s_group.finish()[0:GB]
        r["expand_out"][...] = s_expand.finish()
        r["reduce_out"][...] = s_reduce.finish().T
        for scatter in (s_group, s_expand, s_reduce):
            scatter.sent()
    for copy in sends:
        copy.wait_send()
    halo1.sent()
    halo2.sent()


def adamw_step(master, gradient, moment_one, moment_two, average, rate):
    first_new = 0.5 * moment_one + 0.5 * gradient
    second_new = 0.5 * moment_two + 0.5 * gradient * gradient
    correct = 1.0 - 0.5**STEP
    direction = first_new / correct / (jnp.sqrt(second_new / correct) + 1e-08)
    master_new = master - rate * (direction + 0.05 * master)
    average_new = 0.75 * average + 0.25 * master_new
    return (first_new, second_new, master_new, average_new)


def adamw_kernel(*refs):
    ins, outs = refs[:25], list(refs[25:])
    for n in range(5):
        gradient, master, one, two, average = (ref[...] for ref in ins[5 * n : 5 * n + 5])
        rate = CONV_RATE if n < 3 else NORM_RATE
        first, second, new, mean = adamw_step(master, gradient, one, two, average, rate)
        values = [gradient, first, second, new] + ([new.astype(BF)] if n < 3 else []) + [mean]
        for value in values:
            outs.pop(0)[...] = value


def step_sizes(leaves):
    return [jax.ShapeDtypeStruct(a.shape, a.dtype) for a in leaves]


def local(
    inputs, cotangent,
    reduce_master, reduce_first, reduce_second, reduce_average,
    group_master, group_first, group_second, group_average,
    expand_master, expand_first, expand_second, expand_average,
    inner_master, inner_first, inner_second, inner_average,
    outer_master, outer_first, outer_second, outer_average,
):
    N, rows, W, CIN = inputs.shape
    OUT = cotangent.shape[3]
    MID = inner_master.shape[1]
    H, D = lax.axis_size("height"), lax.axis_size("dp")
    HD = H * D
    R = W * N
    GB = group_master.shape[0]
    RB, EB = reduce_master.shape[0], expand_master.shape[1]
    own_gather = RB % 128 == 0 and EB % 128 == 0
    dims = dict(H=H, D=D, N=N, W=W, MID=MID, OUT=OUT, CIN=CIN, own_gather=own_gather)

    x = inputs.transpose(1, 2, 0, 3).reshape(rows * R, CIN)
    ct = cotangent.transpose(1, 2, 0, 3).reshape(rows * R, OUT)
    ins = dict(x=x, ct=ct, inner=inner_master, outer=outer_master)
    outs = dict(
        bo=((rows * R, OUT), BF),
        ig=((rows * R, OUT), F32),
        inner_grad=(inner_master.shape, F32),
        outer_grad=(outer_master.shape, F32),
    )
    scratch = dict(
        wep=((MID, CIN), BF),
        ct2=((2, R, OUT), BF),
        out2=((2, 2, OUT), F32),
        first=((2 * R, MID), F32),
        second=((2 * R, MID), F32),
        slope1=((2 * R, MID), F32),
        slope2=((2 * R, MID), F32),
        a1=((4 * (W + 2) * N, MID), BF),
        b2=((4 * (W + 2) * N, MID), BF),
        wall=((9 * MID, MID), BF),
        wallt=((9 * MID, MID), BF),
        gf=((9 * GROUP, MID), F32),
        ggf=((9 * GROUP, MID), F32),
        st1=((HD, 2, MID), F32),
        st2=((HD, 2, MID), F32),
        st3=((2 * HD, 2, 2 * OUT), F32),
        st3b=((2 * HD, 2, 2 * OUT), F32),
        st2b=((HD, 2, MID), F32),
        st1b=((HD, 2, MID), F32),
        tot3=((2, 2 * OUT), F32),
        a2=((2 * R, MID), BF),
        a2t=((MID, 2 * R), BF),
        ax=((R, MID), BF),
        third=((2, R, OUT), F32),
        tx=((R, OUT), BF),
        tother=((R, OUT), BF),
        nother=((R, OUT), F32),
        dother=((R, OUT), F32),
        mi3=((2, 2, OUT), F32),
        pair=((2, 2, OUT), F32),
        wrq=((OUT, 4 * MID), BF),
        ball=((2 * R, 4 * MID), BF),
        tsend=((2, R, OUT), BF),
        trecv=((2, R, OUT), BF),
        dpre=((2, R, OUT), F32),
        piece=((2 * R, CIN), BF),
        agrad=((2 * R, MID), F32),
        agsend=((R, MID), BF),
        agrecv=((R, MID), BF),
        b2n=((2 * R, MID), BF),
        b2t=((MID, 2 * R), BF),
        second_back=((2 * R, MID), F32),
        b1=((2 * R, MID), BF),
        b1t=((MID, 2 * R), BF),
    )
    if own_gather:
        ins.update(rm=reduce_master, gm=group_master, em=expand_master)
        outs.update(
            reduce_out=((RB, MID), F32), group_out=((GB, MID), F32), expand_out=((MID, EB), F32)
        )
        scratch.update(
            wr=((CIN, MID), BF), we=((MID, CIN), BF), wg=((HD, SLOT, MID), BF),
            ggs=((HD, SLOT, MID), F32),
        )
        for name, shape in (("rg", (MID, RB)), ("eg", (MID, EB)), ("gg", (SLOT, MID))):
            scratch[name + "_ys"] = scratch[name + "_yr"] = (((D - 1) * H, *shape), BF)
            scratch[name + "_zs"] = scratch[name + "_zr"] = ((H, *shape), BF)
            scratch[name + "_own"] = (shape, F32)
    else:
        both = ("height", "dp")
        ins.update(
            wr_full=lax.all_gather(reduce_master.astype(BF), both, axis=0, tiled=True),
            wg_full=lax.all_gather(group_master.astype(BF), both, axis=0, tiled=True),
            we_full=lax.all_gather(expand_master.astype(BF), both, axis=1, tiled=True),
        )
        outs.update(
            reduce_out=((MID, CIN), BF),
            group_out=((9 * GROUP, MID), BF),
            expand_out=((MID, CIN), BF),
        )
    names = [*ins, *outs, *scratch, "ssem", "rsem"]
    whole = pl.BlockSpec(memory_space=pltpu.VMEM)
    results = pl.pallas_call(
        functools.partial(block_kernel, names, dims),
        out_shape=[pltpu.VMEM(*v) for v in outs.values()],
        in_specs=[whole] * len(ins),
        out_specs=[whole] * len(outs),
        scratch_shapes=[pltpu.VMEM(*v) for v in scratch.values()]
        + [pltpu.SemaphoreType.DMA((dims.get("semaphores", SEMAPHORES + 16 * D),))] * 2,
        compiler_params=pltpu.CompilerParams(
            collective_id=0, has_side_effects=True, vmem_limit_bytes=40 << 20
        ),
        name="block",
    )(*(pltpu.with_memory_space_constraint(v, pltpu.VMEM) for v in ins.values()))
    got = dict(zip(outs, results, strict=True))
    block_out = got["bo"].reshape(rows, W, N, OUT).transpose(2, 0, 1, 3)
    input_grad = got["ig"].reshape(rows, W, N, OUT).transpose(2, 0, 1, 3)
    reduce_grad, group_grad, expand_grad = got["reduce_out"], got["group_out"], got["expand_out"]
    if not own_gather:
        both = ("height", "dp")
        reduce_grad = lax.psum_scatter(reduce_grad.T, both, scatter_dimension=0, tiled=True).astype(F32)
        group_grad = lax.psum_scatter(group_grad, both, scatter_dimension=0, tiled=True).astype(F32)
        expand_grad = lax.psum_scatter(expand_grad, both, scatter_dimension=1, tiled=True).astype(F32)
    groups = (
        (reduce_grad, reduce_master, reduce_first, reduce_second, reduce_average),
        (group_grad, group_master, group_first, group_second, group_average),
        (expand_grad, expand_master, expand_first, expand_second, expand_average),
        (got["inner_grad"], inner_master, inner_first, inner_second, inner_average),
        (got["outer_grad"], outer_master, outer_first, outer_second, outer_average),
    )
    shapes = []
    for n, group in enumerate(groups):
        kinds = [F32] * 4 + ([BF] if n < 3 else []) + [F32]
        shapes += [jax.ShapeDtypeStruct(group[0].shape, kind) for kind in kinds]
    flat = [a for group in groups for a in group]
    news = pl.pallas_call(
        adamw_kernel,
        out_shape=shapes,
        in_specs=[whole] * len(flat),
        out_specs=[whole] * len(shapes),
        compiler_params=pltpu.CompilerParams(vmem_limit_bytes=32 << 20),
        name="adamw",
    )(*flat)
    return (block_out, input_grad, *news)


def solution(mesh):
    pixel = P("dp", "height", None, "chan")
    first = P(("height", "dp"), "chan")
    last = P("chan", ("height", "dp"))
    table = P(None, "chan")
    return jax.shard_map(
        local,
        mesh=mesh,
        in_specs=(P("dp", "height", None, None), pixel)
        + (first,) * 8
        + (last,) * 4
        + (table,) * 8,
        out_specs=(pixel, pixel) + (first,) * 12 + (last,) * 6 + (table,) * 10,
        check_vma=False,
    )
```

```python
import functools

import jax
import jax.numpy as jnp
from jax import lax
from jax.experimental import pallas as pl
from jax.experimental.pallas import tpu as pltpu
from jax.sharding import PartitionSpec as P

GROUP = 32
HEIGHT = 7
STEP = 10
NORM_EPS = 1e-05
CONV_RATE = 0.02
NORM_RATE = 0.3

BF = jnp.bfloat16
F32 = jnp.float32
MESH = pl.DeviceIdType.MESH
SEMAPHORES = 192
SLOT = 48


def dot(a, b):
    return jnp.dot(a, b, preferred_element_type=F32)


def dot_nt(a, b):
    return lax.dot_general(a, b, (((1,), (1,)), ((), ())), preferred_element_type=F32)


def block_kernel(names, dims, *refs):
    r = dict(zip(names, refs, strict=True))
    H, D, N, W, MID, OUT, CIN = (dims[k] for k in ("H", "D", "N", "W", "MID", "OUT", "CIN"))
    own_gather = dims["own_gather"]
    R = W * N
    PITCH = (W + 2) * N
    HD = H * D
    pixels = float(N * D * HEIGHT * W)
    x_ref, ct_ref, inner_ref, outer_ref = r["x"], r["ct"], r["inner_in"], r["outer_in"]
    loads = {
        name: pltpu.make_async_copy(r[name + "_hbm"], r[name + "_in"], r["lsem"].at[i])
        for i, name in enumerate(dims["loads"])
    }
    for name in reversed(dims["loads"]):
        loads[name].start()

    z = lax.axis_index("height")
    c = lax.axis_index("chan")
    y = lax.axis_index("dp")
    xp = lax.div(c, 2)
    k = lax.rem(c, 2)
    cx = lax.rem(c + 2, 4)
    cc = c + 1 - 2 * k
    owner = z * D + y

    def dev(dz=0, chan=None, dy=0):
        return {
            "height": lax.rem(z + dz, H),
            "chan": c if chan is None else chan,
            "dp": lax.rem(y + dy, D),
        }

    offsets = [(dz, dy) for dz in range(H) for dy in range(D)]
    family = [dev(dz, None, dy) for dz, dy in offsets if dz or dy]
    twin_family = [dev(dz, cx, dy) for dz, dy in offsets]
    core_peer = dev(0, cc, 0)
    x_peer = dev(0, cx, 0)
    diagonal = dev(0, cx + 1 - 2 * k, 0)

    def rows(h):
        return pl.ds(pl.multiple_of(h * R, 16), R)

    def tile(h, w):
        return pl.ds(pl.multiple_of(h * R + w * N, 16), N)

    def slab(hh, ww, count):
        return pl.ds(pl.multiple_of((hh * (W + 2) + ww) * N, 16), count)

    def quarter(j, core):
        return pl.ds(pl.multiple_of((2 * j + core) * OUT, 128), OUT)

    def valid(h):
        return jnp.where(z * 2 + h < HEIGHT, 1.0, 0.0).astype(F32)

    sends = []
    used = [0]

    def make(src, dst, target, at=None):
        if at is None:
            at = (used[0], used[0])
            used[0] += 1
        return pltpu.make_async_remote_copy(
            src_ref=src,
            dst_ref=dst,
            send_sem=r["ssem"].at[at[0]],
            recv_sem=r["rsem"].at[at[1]],
            device_id=target,
            device_id_type=MESH,
        )

    def send(src, dst, target):
        copy = make(src, dst, target)
        copy.start()
        sends.append(copy)
        return copy

    barrier = pltpu.get_barrier_semaphore()
    everyone = family + twin_family + [core_peer, diagonal]
    for target in everyone:
        pl.semaphore_signal(barrier, inc=1, device_id=target, device_id_type=MESH)
    a1, b2 = r["a1"], r["b2"]
    lane_group = lax.shift_right_logical(lax.broadcasted_iota(jnp.int32, (MID, MID), 1), 5)
    row_group = lax.shift_right_logical(lax.broadcasted_iota(jnp.int32, (MID, MID), 0), 5)
    block_diagonal = lane_group == row_group
    if own_gather:
        wr, we, wg = r["wr"], r["we"], r["wg"]
        RB, EB = r["rm_in"].shape[0], r["em_in"].shape[1]
        GB = r["gm_in"].shape[0]

        def reduce_block(o):
            return wr.at[pl.ds(pl.multiple_of(o * RB, 16), RB), :]

        def expand_block(o):
            return we.at[:, pl.ds(pl.multiple_of(o * EB, 128), EB)]

        def group_block(o):
            return wg.at[o]

        for name in ("rm", "em", "gm"):
            loads[name].wait()
        reduce_block(owner)[...] = r["rm_in"][...].astype(BF)
        expand_block(owner)[...] = r["em_in"][...].astype(BF)
        wg[owner] = jnp.concatenate(
            [r["gm_in"][...], jnp.zeros((SLOT - GB, MID), F32)], axis=0
        ).astype(BF)
    else:
        wr, we = r["wr_full"], r["we_full"]

    pl.semaphore_wait(barrier, len(everyone))

    near = [z + 1 - 2 * lax.rem(z, 2), jnp.where(z < 2, 2, 1), jnp.where(z < 2, 3, 0)]

    class Gather:
        def __init__(self, block):
            self.block = block
            self.here = block(owner)
            self.base = used[0]
            used[0] += H
            self.along_y = []

        def send_z(self, rank):
            target = {"height": near[rank], "chan": c, "dp": y}
            copy = make(self.here, self.here, target, (self.base + rank, self.base + z))
            copy.start()
            sends.append(copy)

        def send_y(self):
            self.pass_on(self.here)

        def pass_on(self, block):
            self.along_y.append([send(block, block, dev(0, None, dy)) for dy in range(1, D)])

        def forward(self, rank):
            source = near[rank]
            block = self.block(source * D + y)
            make(block, block, dev(), (self.base, self.base + source)).wait_recv()
            self.pass_on(block)
            return source

        def finish(self, number):
            for copy in self.along_y[number]:
                copy.wait_recv()

    if own_gather:
        g_reduce, g_group, g_expand = Gather(reduce_block), Gather(group_block), Gather(expand_block)
        for rank in range(3):
            g_reduce.send_z(rank)
        g_reduce.send_y()
        for rank in range(3):
            g_group.send_z(rank)
        g_group.send_y()
    wep = r["wep"]
    twin_in = []

    def twin(o):
        twin_in.append(
            send(expand_block(o), wep.at[:, pl.ds(pl.multiple_of(o * EB, 128), EB)], x_peer)
        )

    def twin_y(number, zz):
        g_expand.finish(number)
        for dy in range(1, D):
            twin(zz * D + lax.rem(y + dy, D))

    if own_gather:
        g_expand.send_z(0)
        g_expand.send_z(1)
        g_expand.send_y()
        twin(owner)
    else:
        twin_in.append(send(we, wep, x_peer))

    def relay(source, target):
        def body(w, carry):
            turned = jnp.swapaxes(source[:, w], 0, 1)
            for h in range(2):
                target[tile(h, w), :] = turned[h]
            return carry

        lax.fori_loop(0, W, body, 0)

    loads["inner"].wait()
    loads["outer"].wait()
    loads["ct"].wait()
    relay(r["ct_in"], ct_ref)
    ct2, out2 = r["ct2"], r["out2"]
    ct_in = send(ct_ref.at[rows(1 - xp)], ct2.at[xp], x_peer)
    ct2[xp] = ct_ref[rows(xp), :]
    out2[xp] = outer_ref[...]
    outer_in = send(out2.at[xp], out2.at[xp], x_peer)
    a1[...] = jnp.zeros(a1.shape, BF)
    b2[...] = jnp.zeros(b2.shape, BF)
    loads["x"].wait()
    relay(r["x_in"], x_ref)

    def statistics(buf, position, targets, value):
        buf[position] = value
        return [send(buf.at[position], buf.at[position], t) for t in targets]

    def total(buf, copies):
        for copy in copies:
            copy.wait_recv()
        return jnp.sum(buf[...], axis=0)

    first = r["first"]

    def product(blocks, start):
        def body(h, carry):
            left = jnp.concatenate(
                [x_ref[rows(h), pl.ds(pl.multiple_of(o * RB, 128), RB)] for o in blocks], axis=1
            )
            right = jnp.concatenate([reduce_block(o)[...] for o in blocks], axis=0)
            part = dot(left, right)
            first[rows(h), :] = part if start else first[rows(h), :] + part
            return carry

        lax.fori_loop(0, 2, body, 0)

    if own_gather:
        g_reduce.forward(0)
        twin_y(0, z)
        g_reduce.forward(1)
        g_reduce.forward(2)
        product([zz * D + y for zz in range(H)], True)
        for rank in range(3):
            g_group.forward(rank)
        sources = [z]
        sources.append(g_expand.forward(0))
        twin(sources[1] * D + y)
        for number in range(4):
            g_reduce.finish(number)
        for dy in range(1, D):
            product([zz * D + lax.rem(y + dy, D) for zz in range(H)], False)
    else:
        def body(h, carry):
            first[rows(h), :] = dot(x_ref[rows(h), :], wr[...])
            return carry

        lax.fori_loop(0, 2, body, 0)

    def moments(ref):
        def body(h, carry):
            v = ref[rows(h), :]
            return (
                carry[0] + jnp.sum(v, axis=0, keepdims=True) * valid(h),
                carry[1] + jnp.sum(v * v, axis=0, keepdims=True) * valid(h),
            )

        zero = jnp.zeros((1, ref.shape[1]), F32)
        return jnp.concatenate(lax.fori_loop(0, 2, body, (zero, zero)), axis=0)

    def average_and_inverse(sums):
        mean = sums[0:1] / pixels
        return mean, lax.rsqrt(sums[1:2] / pixels - mean * mean + NORM_EPS)

    stat1 = statistics(r["st1"], owner, family, moments(first))

    wall, wallt, gf = r["wall"], r["wallt"], r["gf"]
    if own_gather:
        g_expand.send_z(2)
        sources.append(g_expand.forward(1))
        twin(sources[2] * D + y)
        for number in range(4):
            g_group.finish(number)
        for o in range(HD):
            gf[o * GB : (o + 1) * GB, :] = wg[o].astype(F32)[0:GB]
    else:
        gf[...] = r["wg_full"][...].astype(F32)

    def spread(t, carry):
        piece = gf[pl.ds(pl.multiple_of(t * GROUP, 8), GROUP), :]
        full = jnp.where(block_diagonal, jnp.concatenate([piece] * (MID // GROUP), axis=0), 0.0)
        wall[pl.ds(pl.multiple_of(t * MID, 16), MID), :] = full.astype(BF)
        wallt[pl.ds(pl.multiple_of((8 - t) * MID, 16), MID), :] = full.T.astype(BF)
        return carry

    lax.fori_loop(0, 9, spread, 0)
    mean1, inv1 = average_and_inverse(total(r["st1"], stat1))
    gain1, shift1 = inner_ref[0:1, :], inner_ref[1:2, :]
    slope1 = r["slope1"]

    def activate(h):
        ok = valid(h)

        def body(w, carry):
            v = (first[tile(h, w), :] - mean1) * inv1
            v = v * gain1 + shift1
            q = jax.nn.sigmoid(v)
            a1[slab(h + 1, w + 1, N), :] = (v * q * ok).astype(BF)
            slope1[tile(h, w), :] = q * (1.0 + v * (1.0 - q)) * ok
            return carry

        lax.fori_loop(0, W, body, 0)

    class Halo:
        def __init__(self, ref):
            self.up = make(ref.at[slab(1, 1, R)], ref.at[slab(3, 1, R)], dev(H - 1, None, 0))
            self.down = make(ref.at[slab(2, 1, R)], ref.at[slab(0, 1, R)], dev(1, None, 0))

        def start_up(self):
            pl.when(z > 0)(self.up.start)

        def start_down(self):
            pl.when(z < H - 1)(self.down.start)

        def arrived(self):
            pl.when(z > 0)(self.down.wait_recv)
            pl.when(z < H - 1)(self.up.wait_recv)

        def sent(self):
            pl.when(z > 0)(self.up.wait_send)
            pl.when(z < H - 1)(self.down.wait_send)

    halo1, halo2 = Halo(a1), Halo(b2)
    activate(0)
    halo1.start_up()
    activate(1)
    halo1.start_down()

    def convolve(ref, weights, out, edge):
        def body(h, carry):
            if edge:
                hh, base, count = 3 * h, 6 * h, 1
            else:
                hh, base, count = 1, 3 * (1 - h), 2
            left = jnp.concatenate(
                [ref[slab(hh + i, kc, R), :] for i in range(count) for kc in range(3)], axis=1
            )
            part = dot(left, weights[pl.ds(pl.multiple_of(base * MID, 16), 3 * count * MID), :])
            out[rows(h), :] = out[rows(h), :] + part if edge else part
            return carry

        lax.fori_loop(0, 2, body, 0)

    second = r["second"]
    convolve(a1, wall, second, False)
    if own_gather:
        sources.append(g_expand.forward(2))
        twin(sources[3] * D + y)
        twin_y(1, sources[1])
        twin_y(2, sources[2])
    halo1.arrived()
    convolve(a1, wall, second, True)
    stat2 = statistics(r["st2"], owner, family, moments(second))
    if own_gather:
        twin_y(3, sources[3])
    mean2, inv2 = average_and_inverse(total(r["st2"], stat2))
    gain2, shift2 = inner_ref[2:3, :], inner_ref[3:4, :]
    a2, slope2 = r["a2"], r["slope2"]

    def activate_two(h):
        ok = valid(h)

        def body(w, carry):
            n = (second[tile(h, w), :] - mean2) * inv2
            second[tile(h, w), :] = n
            v = n * gain2 + shift2
            q = jax.nn.sigmoid(v)
            a2[tile(h, w), :] = (v * q * ok).astype(BF)
            slope2[tile(h, w), :] = q * (1.0 + v * (1.0 - q)) * ok
            return carry

        lax.fori_loop(0, W, body, 0)

    activate_two(1 - xp)
    ax_in = send(a2.at[rows(1 - xp)], r["ax"], x_peer)
    activate_two(xp)

    for copy in twin_in:
        copy.wait_recv()
    ax_in.wait_recv()
    third, tsend, trecv = r["third"], r["tsend"], r["trecv"]
    left = jnp.concatenate([a2[rows(xp), :], r["ax"][...]], axis=1)

    def expand(j, core):
        right = jnp.concatenate([we[:, quarter(j, core)], wep[:, quarter(j, core)]], axis=0)
        return dot(left, right)

    core_in = []
    for j in range(2):
        tsend[j] = expand(j, 1 - k).astype(BF)
        core_in.append(send(tsend.at[j], trecv.at[j], core_peer))
    for j in range(2):
        third[j] = expand(j, k)
    okx = valid(xp)
    sums = []
    for j in range(2):
        core_in[j].wait_recv()

        def body(w, carry):
            at = pl.ds(pl.multiple_of(w * N, 16), N)
            v = third[j, at, :] + trecv[j, at, :].astype(F32)
            third[j, at, :] = v
            return carry[0] + jnp.sum(v, axis=0, keepdims=True), carry[1] + jnp.sum(
                v * v, axis=0, keepdims=True
            )

        zero = jnp.zeros((1, OUT), F32)
        sums.append(lax.fori_loop(0, W, body, (zero, zero)))
    r["tx"][...] = third[1 - xp].astype(BF)
    position = xp * HD + owner
    both = family + twin_family
    stat3 = statistics(
        r["st3"],
        position,
        both,
        jnp.concatenate(
            [jnp.concatenate([s[i] for s in sums], axis=1) * okx for i in range(2)], axis=0
        ),
    )
    cut = (W + 1) // 2
    parts = [pl.ds(0, cut * N), pl.ds(cut * N, (W - cut) * N)]
    tx_in = [send(r["tx"].at[parts[0]], r["tother"].at[parts[0]], x_peer)]
    wrq = r["wrq"]

    def mids(chan):
        return pl.ds(pl.multiple_of(chan * MID, 128), MID)

    wrq[:, mids(c)] = wr[quarter(xp, k), :]
    wrq_in = [send(wr.at[quarter(xp, 1 - k), :], wrq.at[:, mids(c)], core_peer)]
    share = OUT // 2

    def send_wrq(n):
        target, core = ((x_peer, k), (diagonal, 1 - k))[n // 2]
        at = pl.ds(pl.multiple_of((2 * (1 - xp) + core) * OUT + n % 2 * share, 16), share)
        there = wrq.at[pl.ds(n % 2 * share, share), mids(c)]
        wrq_in.append(send(wr.at[at, :], there, target))

    a2t = r["a2t"]
    a2t[...] = a2[...].T
    ct_in.wait_recv()
    outer_in.wait_recv()
    mean3, inv3 = average_and_inverse(total(r["st3"], stat3))
    dpre, dother, bo = r["dpre"], r["dother"], r["bo"]
    mi3 = r["mi3"]
    for j in range(2):
        lanes = slice(j * OUT, (j + 1) * OUT)
        mi3[j] = jnp.concatenate([mean3[:, lanes], inv3[:, lanes]], axis=0)

    def outer_norm(j, h, values, grads, write, start=0, stop=W):
        m, iv = mi3[j, 0:1, :], mi3[j, 1:2, :]
        g, s = out2[j, 0:1, :], out2[j, 1:2, :]
        ok = valid(h)

        def body(w, carry):
            at = pl.ds(pl.multiple_of(w * N, 16), N)
            n = (values[0](at) - m) * iv
            values[1](at, n)
            v = n * g + s + x_ref[tile(h, w), quarter(j, k)].astype(F32)
            q = jax.nn.sigmoid(v)
            if write:
                bo[tile(h, w), :] = (v * q * ok).astype(BF)
            d = grads[0](at, w) * ok * (q * (1.0 + v * (1.0 - q)))
            grads[1](at, d)
            return carry[0] + jnp.sum(d, axis=0, keepdims=True), carry[1] + jnp.sum(
                d * n, axis=0, keepdims=True
            )

        zero = jnp.zeros((1, OUT), F32)
        return lax.fori_loop(start, stop, body, (zero, zero))

    def third_access(j):
        def get(at):
            return third[j, at, :]

        def put(at, n):
            third[j, at, :] = n

        def get_ct(at, w):
            return ct2[j, at, :].astype(F32)

        def put_d(at, d):
            dpre[j, at, :] = d

        return (get, put), (get_ct, put_d)

    st3b = r["st3b"]
    pair = r["pair"]
    for j, write in ((xp, True), (1 - xp, False)):
        pair[j] = jnp.concatenate(outer_norm(j, xp, *third_access(j), write), axis=0)
    stat3b = statistics(st3b, position, both, jnp.concatenate([pair[0], pair[1]], axis=1))

    tx_in.append(send(r["tx"].at[parts[1]], r["tother"].at[parts[1]], x_peer))
    send_wrq(0)
    tx_in[0].wait_recv()
    nother = r["nother"]

    def get_other(at):
        return r["tother"][at, :].astype(F32)

    def put_other(at, n):
        nother[at, :] = n

    def get_ct_other(at, w):
        return ct_ref[tile(1 - xp, w), :].astype(F32)

    def put_d_other(at, d):
        dother[at, :] = d

    other_row = ((get_other, put_other), (get_ct_other, put_d_other), True)
    outer_norm(xp, 1 - xp, *other_row, 0, cut)
    total3 = total(st3b, stat3b)
    r["tot3"][...] = total3
    for j in range(2):
        lanes = slice(j * OUT, (j + 1) * OUT)
        pair[j] = total3[:, lanes] / pixels
    piece = r["piece"]

    def back_three(j, h, upstream, normed):
        factor = out2[j, 0:1, :] * mi3[j, 1:2, :] * valid(h)
        sh, ga = pair[j, 0:1, :], pair[j, 1:2, :]

        def body(w, carry):
            at = pl.ds(pl.multiple_of(w * N, 16), N)
            v = factor * (upstream(at) - sh - normed(at) * ga)
            piece[tile(h, w), quarter(j, k)] = v.astype(BF)
            return carry

        lax.fori_loop(0, W, body, 0)
        part = piece.at[rows(h), quarter(j, k)]
        return send(part, part, core_peer)

    core_in = [
        back_three(j, xp, lambda at, j=j: dpre[j, at, :], lambda at, j=j: third[j, at, :])
        for j in range(2)
    ]
    for copy in core_in:
        copy.wait_recv()
    agrad = r["agrad"]
    r["agsend"][...] = dot_nt(piece[rows(xp), :], wep[...]).astype(BF)
    ag_in = send(r["agsend"], r["agrecv"], x_peer)
    part = piece.at[rows(xp), quarter(xp, k)]
    piece_in = send(part, part, x_peer)
    for n in range(1, 4):
        send_wrq(n)
    agrad[rows(xp), :] = dot_nt(piece[rows(xp), :], we[...])
    tx_in[1].wait_recv()
    outer_norm(xp, 1 - xp, *other_row, cut, W)
    core_other = back_three(xp, 1 - xp, lambda at: dother[at, :], lambda at: nother[at, :])

    class Scatter:
        def __init__(self, name, block):
            self.block = block
            self.ys, self.yr = r[name + "_ys"], r[name + "_yr"]
            self.zs, self.zr = r[name + "_zs"], r[name + "_zr"]
            self.own = r[name + "_own"]
            self.along_y, self.along_z = {}, []
            self.base = used[0]
            used[0] += H

        def start(self, targets):
            for slot, zi in targets:
                self.along_y[slot] = []
                for dy in range(1, D):
                    n = (dy - 1) * H + slot
                    self.ys[n] = self.block(zi * D + lax.rem(y + dy, D)).astype(BF)
                    self.along_y[slot].append(
                        (n, send(self.ys.at[n], self.yr.at[n], dev(0, None, dy)))
                    )

        def middle(self, targets):
            for slot, zi in targets:
                value = self.block(zi * D + y)
                for n, copy in self.along_y[slot]:
                    copy.wait_recv()
                    value = value + self.yr[n].astype(F32)
                other = zi != z

                @pl.when(jnp.logical_not(other))
                def keep():
                    self.own[...] = value

                self.zs[slot] = value.astype(BF)
                target = {"height": zi, "chan": c, "dp": y}
                at = (self.base + slot, self.base + z)
                copy = make(self.zs.at[slot], self.zr.at[z], target, at)
                pl.when(other)(copy.start)
                self.along_z.append((other, copy))

        def fold(self, targets):
            (slot, zi), (kept, zk) = targets
            value = self.block(zi * D + y)
            for n, copy in self.along_y[slot]:
                copy.wait_recv()
                value = value + self.yr[n].astype(F32)
            self.zs[slot] = value.astype(BF)
            target = {"height": near[0], "chan": c, "dp": y}
            pair = send(self.zs.at[slot], self.zr.at[slot], target)

            def rest():
                value = self.block(zk * D + y)
                for n, copy in self.along_y[kept]:
                    copy.wait_recv()
                    value = value + self.yr[n].astype(F32)
                pair.wait_recv()
                value = value + self.zr[slot].astype(F32)
                other = zk != z

                @pl.when(jnp.logical_not(other))
                def keep():
                    self.own[...] = value

                self.zs[kept] = value.astype(BF)
                target = {"height": lax.rem(z + 2, 4), "chan": c, "dp": y}
                at = (self.base, self.base)
                copy = make(self.zs.at[kept], self.zr.at[H], target, at)
                pl.when(other)(copy.start)
                self.along_z.append((other, copy))
                self.last = copy

            return rest

        def finish_fold(self):
            self.last.wait_recv()
            return self.own[...] + self.zr[H].astype(F32)

        def finish(self):
            value = self.own[...]
            for dz in range(1, H):
                s = lax.rem(z + dz, H)
                at = (self.base, self.base + s)
                make(self.zs.at[0], self.zr.at[s], dev(dz), at).wait_recv()
                value = value + self.zr[s].astype(F32)
            return value

        def sent(self):
            for other, copy in self.along_z:
                pl.when(other)(copy.wait_send)

    def wide(left_ref, right_ref, o):
        return dot(left_ref[...], right_ref[:, pl.ds(pl.multiple_of(o * EB, 128), EB)])

    def slope_two(h, received, carry):
        def body(w, carry):
            if received:
                up = r["agrecv"][pl.ds(pl.multiple_of(w * N, 16), N), :].astype(F32)
            else:
                up = agrad[tile(h, w), :]
            d = up * slope2[tile(h, w), :]
            agrad[tile(h, w), :] = d
            return carry[0] + jnp.sum(d, axis=0, keepdims=True), carry[1] + jnp.sum(
                d * second[tile(h, w), :], axis=0, keepdims=True
            )

        return lax.fori_loop(0, W, body, carry)

    zero = jnp.zeros((1, MID), F32)
    carry = slope_two(xp, False, (zero, zero))
    half = H // 2
    parity = lax.rem(z, 2)
    early = [(i, xp * half + lax.rem(parity + 1 + i, 2)) for i in range(half)]
    late = [(half + i, (1 - xp) * half + lax.rem(parity + 1 + i, 2)) for i in range(half)]
    around = [(0, lax.rem(z + 2, 4)), (1, 3 - z), (2, near[0]), (3, z)]
    if own_gather:
        s_expand = Scatter("eg", lambda o: wide(a2t, piece, o))
    ag_in.wait_recv()
    carry = slope_two(1 - xp, True, carry)
    stat2b = statistics(r["st2b"], owner, family, jnp.concatenate(carry, axis=0))
    if own_gather:
        core_other.wait_recv()
        s_expand.start(early)

    def turn(w, carry):
        r["turned"][:, w] = jnp.swapaxes(jnp.stack([bo[tile(h, w), :] for h in range(2)]), 0, 1)
        return carry

    lax.fori_loop(0, W, turn, 0)
    total2 = total(r["st2b"], stat2b)
    b2n = r["b2n"]

    def norm_two(h):
        factor = gain2 * inv2 * valid(h)
        sh, ga = total2[0:1] / pixels, total2[1:2] / pixels

        def body(w, carry):
            v = factor * (agrad[tile(h, w), :] - sh - second[tile(h, w), :] * ga)
            v = v.astype(BF)
            b2[slab(h + 1, w + 1, N), :] = v
            b2n[tile(h, w), :] = v
            return carry

        lax.fori_loop(0, W, body, 0)

    norm_two(0)
    halo2.start_up()
    norm_two(1)
    halo2.start_down()
    back1 = r["second_back"]
    convolve(b2, wallt, back1, False)
    b2t = r["b2t"]
    b2t[...] = b2n[...].T
    ggf = r["ggf"]
    fold = jnp.where(
        jnp.bitwise_and(lax.broadcasted_iota(jnp.int32, (GROUP, MID), 1), GROUP - 1)
        == lax.broadcasted_iota(jnp.int32, (GROUP, MID), 0),
        1.0,
        0.0,
    ).astype(BF)

    def group_grad(t, carry):
        kr, kc = lax.div(t, 3), lax.rem(t, 3)
        left = jnp.concatenate([a1[slab(kr, kc, R), :], a1[slab(kr + 1, kc, R), :]], axis=0)
        turned = jnp.where(block_diagonal, dot(b2t[...], left), 0.0).astype(BF)
        ggf[pl.ds(pl.multiple_of(t * GROUP, 8), GROUP), :] = dot_nt(fold, turned)
        return carry

    lax.fori_loop(0, 9, group_grad, 0)

    if own_gather:
        for o in range(HD):
            r["ggs"][o] = jnp.concatenate(
                [ggf[o * GB : (o + 1) * GB, :], jnp.zeros((SLOT - GB, MID), F32)], axis=0
            )
        s_group = Scatter("gg", lambda o: r["ggs"][o])
        s_group.start(around)
    piece_in.wait_recv()
    part = piece.at[rows(1 - xp), quarter(1 - xp, k)]
    core_last = send(part, part, core_peer)
    halo2.arrived()
    convolve(b2, wallt, back1, True)

    def slope_one(i, carry):
        h, w = lax.div(i, W), lax.rem(i, W)
        d = back1[tile(h, w), :] * slope1[tile(h, w), :]
        n = (first[tile(h, w), :] - mean1) * inv1
        first[tile(h, w), :] = n
        back1[tile(h, w), :] = d
        return carry[0] + jnp.sum(d, axis=0, keepdims=True), carry[1] + jnp.sum(
            d * n, axis=0, keepdims=True
        )

    carry = lax.fori_loop(0, 2 * W, slope_one, (zero, zero))
    stat1b = statistics(r["st1b"], owner, family, jnp.concatenate(carry, axis=0))

    core_last.wait_recv()
    if not own_gather:
        core_other.wait_recv()
    if own_gather:
        rest_early = s_expand.fold(early)
        s_expand.start(late)
    else:
        r["group_out"][...] = ggf[...].astype(BF)
        r["expand_out"][...] = dot(a2t[...], piece[...]).astype(BF)

    total1 = total(r["st1b"], stat1b)
    b1, ball = r["b1"], r["ball"]

    def norm_one(h):
        factor = gain1 * inv1 * valid(h)
        sh, ga = total1[0:1] / pixels, total1[1:2] / pixels

        def body(w, carry):
            v = factor * (back1[tile(h, w), :] - sh - first[tile(h, w), :] * ga)
            v = v.astype(BF)
            b1[tile(h, w), :] = v
            ball[tile(h, w), mids(c)] = v
            return carry

        lax.fori_loop(0, W, body, 0)

    ball_x, ball_core, ball_far = [], [], []
    for h in range(2):
        norm_one(h)
        part = ball.at[rows(h), mids(c)]
        ball_x.append(send(part, part, x_peer))
        ball_core.append(send(part, part, core_peer))

    def forward_ball(h):
        ball_x[h].wait_recv()
        part = ball.at[rows(h), mids(cx)]
        ball_far.append(send(part, part, core_peer))

    b1t = r["b1t"]
    b1t[...] = b1[...].T
    if own_gather:
        s_reduce = Scatter("rg", lambda o: wide(b1t, x_ref, o))
        s_reduce.start(around)
        rest_early()
        rest_late = s_expand.fold(late)
        s_group.middle(around)
        s_reduce.middle(around[0:1])
        forward_ball(0)
        s_reduce.middle(around[1:2])
        forward_ball(1)
        s_reduce.middle(around[2:3])
        rest_late()
    else:
        forward_ball(0)
        forward_ball(1)
        r["reduce_out"][...] = dot(b1t[...], x_ref[...]).astype(BF)
    ig = r["ig"]

    def chip_mids(n):
        return pl.ds(pl.multiple_of(n * 2 * MID, 128), 2 * MID)

    r["inner_grad"][...] = jnp.concatenate(
        [total1[1:2], total1[0:1], total2[1:2], total2[0:1]], axis=0
    )
    mine = r["tot3"][:, pl.ds(pl.multiple_of(xp * OUT, 128), OUT)]
    r["outer_grad"][...] = jnp.concatenate([mine[1:2], mine[0:1]], axis=0)
    for copy in wrq_in:
        copy.wait_recv()
    ig[rows(xp), :] = dpre[xp]
    ig[rows(1 - xp), :] = dother[...]

    def input_part(h, n):
        ig[rows(h), :] = ig[rows(h), :] + dot_nt(ball[rows(h), chip_mids(n)], wrq[:, chip_mids(n)])

    for h in range(2):
        ball_core[h].wait_recv()
        input_part(h, xp)
    if own_gather:
        s_reduce.middle(around[3:])
    for h in range(2):
        ball_far[h].wait_recv()
        input_part(h, 1 - xp)
    if own_gather:
        r["group_out"][...] = s_group.finish()[0:GB]
        r["expand_out"][...] = s_expand.finish_fold()
        r["reduce_out"][...] = s_reduce.finish().T
        for scatter in (s_group, s_expand, s_reduce):
            scatter.sent()
    for copy in sends:
        copy.wait_send()
    halo1.sent()
    halo2.sent()


def adamw_step(master, gradient, moment_one, moment_two, average, rate):
    first_new = 0.5 * moment_one + 0.5 * gradient
    second_new = 0.5 * moment_two + 0.5 * gradient * gradient
    correct = 1.0 - 0.5**STEP
    direction = first_new / correct / (jnp.sqrt(second_new / correct) + 1e-08)
    master_new = master - rate * (direction + 0.05 * master)
    average_new = 0.75 * average + 0.25 * master_new
    return (first_new, second_new, master_new, average_new)


def last_kernel(*refs):
    ig_ref, bo_ref = refs[:2]
    ins, (bo_out, ig_out), outs = refs[2:27], refs[27:29], list(refs[29:-3])
    turned, bo_sem, ig_sem = refs[-3:]
    W = turned.shape[1]
    bo_copy = pltpu.make_async_copy(bo_ref, bo_out, bo_sem)
    bo_copy.start()

    def body(w, carry):
        turned[:, w] = jnp.swapaxes(ig_ref[:, w], 0, 1)
        return carry

    lax.fori_loop(0, W, body, 0)
    ig_copy = pltpu.make_async_copy(turned, ig_out, ig_sem)
    ig_copy.start()
    for n in range(5):
        gradient, master, one, two, average = (ref[...] for ref in ins[5 * n : 5 * n + 5])
        rate = CONV_RATE if n < 3 else NORM_RATE
        first, second, new, mean = adamw_step(master, gradient, one, two, average, rate)
        values = [gradient, first, second, new] + ([new.astype(BF)] if n < 3 else []) + [mean]
        for value in values:
            outs.pop(0)[...] = value
    bo_copy.wait()
    ig_copy.wait()


def local(
    inputs, cotangent,
    reduce_master, reduce_first, reduce_second, reduce_average,
    group_master, group_first, group_second, group_average,
    expand_master, expand_first, expand_second, expand_average,
    inner_master, inner_first, inner_second, inner_average,
    outer_master, outer_first, outer_second, outer_average,
):
    N, rows, W, CIN = inputs.shape
    OUT = cotangent.shape[3]
    MID = inner_master.shape[1]
    H, D = lax.axis_size("height"), lax.axis_size("dp")
    HD = H * D
    R = W * N
    GB = group_master.shape[0]
    RB, EB = reduce_master.shape[0], expand_master.shape[1]
    own_gather = RB % 128 == 0 and EB % 128 == 0
    dims = dict(H=H, D=D, N=N, W=W, MID=MID, OUT=OUT, CIN=CIN, own_gather=own_gather)

    shards = dict(x=inputs.transpose(0, 2, 1, 3), ct=cotangent.transpose(0, 2, 1, 3))
    shards.update(inner=inner_master, outer=outer_master)
    ins = {}
    outs = dict(
        turned=((N, W, rows, OUT), BF),
        ig=((rows * R, OUT), F32),
        inner_grad=(inner_master.shape, F32),
        outer_grad=(outer_master.shape, F32),
    )
    scratch = dict(
        x=((rows * R, CIN), BF),
        bo=((rows * R, OUT), BF),
        ct=((rows * R, OUT), BF),
        wep=((MID, CIN), BF),
        ct2=((2, R, OUT), BF),
        out2=((2, 2, OUT), F32),
        first=((2 * R, MID), F32),
        second=((2 * R, MID), F32),
        slope1=((2 * R, MID), F32),
        slope2=((2 * R, MID), F32),
        a1=((4 * (W + 2) * N, MID), BF),
        b2=((4 * (W + 2) * N, MID), BF),
        wall=((9 * MID, MID), BF),
        wallt=((9 * MID, MID), BF),
        gf=((9 * GROUP, MID), F32),
        ggf=((9 * GROUP, MID), F32),
        st1=((HD, 2, MID), F32),
        st2=((HD, 2, MID), F32),
        st3=((2 * HD, 2, 2 * OUT), F32),
        st3b=((2 * HD, 2, 2 * OUT), F32),
        st2b=((HD, 2, MID), F32),
        st1b=((HD, 2, MID), F32),
        tot3=((2, 2 * OUT), F32),
        a2=((2 * R, MID), BF),
        a2t=((MID, 2 * R), BF),
        ax=((R, MID), BF),
        third=((2, R, OUT), F32),
        tx=((R, OUT), BF),
        tother=((R, OUT), BF),
        nother=((R, OUT), F32),
        dother=((R, OUT), F32),
        mi3=((2, 2, OUT), F32),
        pair=((2, 2, OUT), F32),
        wrq=((OUT, 4 * MID), BF),
        ball=((2 * R, 4 * MID), BF),
        tsend=((2, R, OUT), BF),
        trecv=((2, R, OUT), BF),
        dpre=((2, R, OUT), F32),
        piece=((2 * R, CIN), BF),
        agrad=((2 * R, MID), F32),
        agsend=((R, MID), BF),
        agrecv=((R, MID), BF),
        b2n=((2 * R, MID), BF),
        b2t=((MID, 2 * R), BF),
        second_back=((2 * R, MID), F32),
        b1=((2 * R, MID), BF),
        b1t=((MID, 2 * R), BF),
    )
    if own_gather:
        shards.update(rm=reduce_master, gm=group_master, em=expand_master)
        outs.update(
            reduce_out=((RB, MID), F32), group_out=((GB, MID), F32), expand_out=((MID, EB), F32)
        )
        scratch.update(
            wr=((CIN, MID), BF), we=((MID, CIN), BF), wg=((HD, SLOT, MID), BF),
            ggs=((HD, SLOT, MID), F32),
        )
        for name, shape in (("rg", (MID, RB)), ("eg", (MID, EB)), ("gg", (SLOT, MID))):
            scratch[name + "_ys"] = scratch[name + "_yr"] = (((D - 1) * H, *shape), BF)
            scratch[name + "_zs"] = scratch[name + "_zr"] = ((H + 1, *shape), BF)
            scratch[name + "_own"] = (shape, F32)
    else:
        both = ("height", "dp")
        ins.update(
            wr_full=lax.all_gather(reduce_master.astype(BF), both, axis=0, tiled=True),
            wg_full=lax.all_gather(group_master.astype(BF), both, axis=0, tiled=True),
            we_full=lax.all_gather(expand_master.astype(BF), both, axis=1, tiled=True),
        )
        outs.update(
            reduce_out=((MID, CIN), BF),
            group_out=((9 * GROUP, MID), BF),
            expand_out=((MID, CIN), BF),
        )
    dims["loads"] = list(shards)
    scratch.update({name + "_in": (a.shape, a.dtype) for name, a in shards.items()})
    names = [*(name + "_hbm" for name in shards), *ins, *outs, *scratch, "lsem", "ssem", "rsem"]
    whole = pl.BlockSpec(memory_space=pltpu.VMEM)
    results = pl.pallas_call(
        functools.partial(block_kernel, names, dims),
        out_shape=[pltpu.VMEM(*v) for v in outs.values()],
        in_specs=[pl.BlockSpec(memory_space=pltpu.HBM)] * len(shards) + [whole] * len(ins),
        out_specs=[whole] * len(outs),
        scratch_shapes=[pltpu.VMEM(*v) for v in scratch.values()]
        + [pltpu.SemaphoreType.DMA((len(shards),))]
        + [pltpu.SemaphoreType.DMA((dims.get("semaphores", SEMAPHORES + 16 * D),))] * 2,
        compiler_params=pltpu.CompilerParams(
            collective_id=0, has_side_effects=True, vmem_limit_bytes=48 << 20
        ),
        name="block",
    )(
        *(pltpu.with_memory_space_constraint(v, pltpu.HBM) for v in shards.values()),
        *(pltpu.with_memory_space_constraint(v, pltpu.VMEM) for v in ins.values()),
    )
    got = dict(zip(outs, results, strict=True))
    reduce_grad, group_grad, expand_grad = got["reduce_out"], got["group_out"], got["expand_out"]
    if not own_gather:
        both = ("height", "dp")
        reduce_grad = lax.psum_scatter(reduce_grad.T, both, scatter_dimension=0, tiled=True).astype(F32)
        group_grad = lax.psum_scatter(group_grad, both, scatter_dimension=0, tiled=True).astype(F32)
        expand_grad = lax.psum_scatter(expand_grad, both, scatter_dimension=1, tiled=True).astype(F32)
    groups = (
        (reduce_grad, reduce_master, reduce_first, reduce_second, reduce_average),
        (group_grad, group_master, group_first, group_second, group_average),
        (expand_grad, expand_master, expand_first, expand_second, expand_average),
        (got["inner_grad"], inner_master, inner_first, inner_second, inner_average),
        (got["outer_grad"], outer_master, outer_first, outer_second, outer_average),
    )
    shapes = [
        jax.ShapeDtypeStruct((N, W, rows, OUT), BF),
        jax.ShapeDtypeStruct((N, W, rows, OUT), F32),
    ]
    for n, group in enumerate(groups):
        kinds = [F32] * 4 + ([BF] if n < 3 else []) + [F32]
        shapes += [jax.ShapeDtypeStruct(group[0].shape, kind) for kind in kinds]
    flat = [got["ig"].reshape(rows, W, N, OUT), got["turned"]]
    flat += [a for group in groups for a in group]
    news = pl.pallas_call(
        last_kernel,
        out_shape=shapes,
        in_specs=[whole] * len(flat),
        out_specs=[pl.BlockSpec(memory_space=pltpu.HBM)] * 2 + [whole] * (len(shapes) - 2),
        scratch_shapes=[
            pltpu.VMEM((N, W, rows, OUT), F32),
            pltpu.SemaphoreType.DMA,
            pltpu.SemaphoreType.DMA,
        ],
        compiler_params=pltpu.CompilerParams(vmem_limit_bytes=40 << 20),
        name="adamw",
    )(*flat)
    pixel_outs = (a.transpose(0, 2, 1, 3) for a in news[:2])
    return (*pixel_outs, *news[2:])


def solution(mesh):
    pixel = P("dp", "height", None, "chan")
    first = P(("height", "dp"), "chan")
    last = P("chan", ("height", "dp"))
    table = P(None, "chan")
    return jax.shard_map(
        local,
        mesh=mesh,
        in_specs=(P("dp", "height", None, None), pixel)
        + (first,) * 8
        + (last,) * 4
        + (table,) * 8,
        out_specs=(pixel, pixel) + (first,) * 12 + (last,) * 6 + (table,) * 10,
        check_vma=False,
    )
```

```python
import functools

import jax
import jax.numpy as jnp
from jax import lax
from jax.experimental import pallas as pl
from jax.experimental.pallas import tpu as pltpu
from jax.sharding import PartitionSpec as P

GROUP = 32
HEIGHT = 7
STEP = 10
NORM_EPS = 1e-05
CONV_RATE = 0.02
NORM_RATE = 0.3

BF = jnp.bfloat16
F32 = jnp.float32
MESH = pl.DeviceIdType.MESH
SEMAPHORES = 192
SLOT = 48


def dot(a, b):
    return jnp.dot(a, b, preferred_element_type=F32)


def dot_nt(a, b):
    return lax.dot_general(a, b, (((1,), (1,)), ((), ())), preferred_element_type=F32)


def block_kernel(names, dims, *refs):
    r = dict(zip(names, refs, strict=True))
    H, D, N, W, MID, OUT, CIN = (dims[k] for k in ("H", "D", "N", "W", "MID", "OUT", "CIN"))
    own_gather = dims["own_gather"]
    R = W * N
    PITCH = (W + 2) * N
    HD = H * D
    pixels = float(N * D * HEIGHT * W)
    x_ref, ct_ref, inner_ref, outer_ref = r["x"], r["ct"], r["inner_in"], r["outer_in"]
    loads = {
        name: pltpu.make_async_copy(r[name + "_hbm"], r[name + "_in"], r["lsem"].at[i])
        for i, name in enumerate(dims["loads"])
    }
    for name in reversed(dims["loads"]):
        loads[name].start()

    z = lax.axis_index("height")
    c = lax.axis_index("chan")
    y = lax.axis_index("dp")
    xp = lax.div(c, 2)
    k = lax.rem(c, 2)
    cx = lax.rem(c + 2, 4)
    cc = c + 1 - 2 * k
    owner = z * D + y

    def dev(dz=0, chan=None, dy=0):
        return {
            "height": lax.rem(z + dz, H),
            "chan": c if chan is None else chan,
            "dp": lax.rem(y + dy, D),
        }

    offsets = [(dz, dy) for dz in range(H) for dy in range(D)]
    family = [dev(dz, None, dy) for dz, dy in offsets if dz or dy]
    twin_family = [dev(dz, cx, dy) for dz, dy in offsets]
    core_peer = dev(0, cc, 0)
    x_peer = dev(0, cx, 0)
    diagonal = dev(0, cx + 1 - 2 * k, 0)

    def rows(h):
        return pl.ds(pl.multiple_of(h * R, 16), R)

    def tile(h, w):
        return pl.ds(pl.multiple_of(h * R + w * N, 16), N)

    def slab(hh, ww, count):
        return pl.ds(pl.multiple_of((hh * (W + 2) + ww) * N, 16), count)

    def quarter(j, core):
        return pl.ds(pl.multiple_of((2 * j + core) * OUT, 128), OUT)

    def valid(h):
        return jnp.where(z * 2 + h < HEIGHT, 1.0, 0.0).astype(F32)

    sends = []
    used = [0]

    def make(src, dst, target, at=None):
        if at is None:
            at = (used[0], used[0])
            used[0] += 1
        return pltpu.make_async_remote_copy(
            src_ref=src,
            dst_ref=dst,
            send_sem=r["ssem"].at[at[0]],
            recv_sem=r["rsem"].at[at[1]],
            device_id=target,
            device_id_type=MESH,
        )

    def send(src, dst, target):
        copy = make(src, dst, target)
        copy.start()
        sends.append(copy)
        return copy

    barrier = pltpu.get_barrier_semaphore()
    everyone = family + twin_family + [core_peer, diagonal]
    for target in everyone:
        pl.semaphore_signal(barrier, inc=1, device_id=target, device_id_type=MESH)
    a1, b2 = r["a1"], r["b2"]
    lane_group = lax.shift_right_logical(lax.broadcasted_iota(jnp.int32, (MID, MID), 1), 5)
    row_group = lax.shift_right_logical(lax.broadcasted_iota(jnp.int32, (MID, MID), 0), 5)
    block_diagonal = lane_group == row_group
    if own_gather:
        wr, we, wg = r["wr"], r["we"], r["wg"]
        RB, EB = r["rm_in"].shape[0], r["em_in"].shape[1]
        GB = r["gm_in"].shape[0]

        def reduce_block(o):
            return wr.at[pl.ds(pl.multiple_of(o * RB, 16), RB), :]

        def expand_block(o):
            return we.at[:, pl.ds(pl.multiple_of(o * EB, 128), EB)]

        def group_block(o):
            return wg.at[o]

        for name in ("rm", "em", "gm"):
            loads[name].wait()
        reduce_block(owner)[...] = r["rm_in"][...].astype(BF)
        expand_block(owner)[...] = r["em_in"][...].astype(BF)
        wg[owner] = jnp.concatenate(
            [r["gm_in"][...], jnp.zeros((SLOT - GB, MID), F32)], axis=0
        ).astype(BF)
    else:
        wr, we = r["wr_full"], r["we_full"]

    pl.semaphore_wait(barrier, len(everyone))

    near = [z + 1 - 2 * lax.rem(z, 2), jnp.where(z < 2, 2, 1), jnp.where(z < 2, 3, 0)]

    class Gather:
        def __init__(self, block):
            self.block = block
            self.here = block(owner)
            self.base = used[0]
            used[0] += H
            self.along_y = []

        def send_z(self, rank):
            target = {"height": near[rank], "chan": c, "dp": y}
            copy = make(self.here, self.here, target, (self.base + rank, self.base + z))
            copy.start()
            sends.append(copy)

        def send_y(self):
            self.pass_on(self.here)

        def pass_on(self, block):
            self.along_y.append([send(block, block, dev(0, None, dy)) for dy in range(1, D)])

        def forward(self, rank):
            source = near[rank]
            block = self.block(source * D + y)
            make(block, block, dev(), (self.base, self.base + source)).wait_recv()
            self.pass_on(block)
            return source

        def finish(self, number):
            for copy in self.along_y[number]:
                copy.wait_recv()

    if own_gather:
        def reduce_part(n):
            return lambda o: wr.at[pl.ds(pl.multiple_of(o * RB + n * (RB // 2), 16), RB // 2), :]

        g_reduce = [Gather(reduce_part(n)) for n in range(2)]
        g_group, g_expand = Gather(group_block), Gather(expand_block)
        for rank in range(3):
            for part in g_reduce:
                part.send_z(rank)
        for part in g_reduce:
            part.send_y()
        for rank in range(3):
            g_group.send_z(rank)
        g_group.send_y()
    wep = r["wep"]
    twin_in = []

    def twin(o):
        twin_in.append(
            send(expand_block(o), wep.at[:, pl.ds(pl.multiple_of(o * EB, 128), EB)], x_peer)
        )

    def twin_y(number, zz):
        g_expand.finish(number)
        for dy in range(1, D):
            twin(zz * D + lax.rem(y + dy, D))

    if own_gather:
        g_expand.send_z(0)
        g_expand.send_z(1)
        g_expand.send_y()
        twin(owner)
    else:
        twin_in.append(send(we, wep, x_peer))

    def relay(source, target):
        def body(w, carry):
            turned = jnp.swapaxes(source[:, w], 0, 1)
            for h in range(2):
                target[tile(h, w), :] = turned[h]
            return carry

        lax.fori_loop(0, W, body, 0)

    loads["inner"].wait()
    loads["outer"].wait()
    loads["ct"].wait()
    relay(r["ct_in"], ct_ref)
    ct2, out2 = r["ct2"], r["out2"]
    ct_in = send(ct_ref.at[rows(1 - xp)], ct2.at[xp], x_peer)
    ct2[xp] = ct_ref[rows(xp), :]
    out2[xp] = outer_ref[...]
    outer_in = send(out2.at[xp], out2.at[xp], x_peer)
    a1[...] = jnp.zeros(a1.shape, BF)
    b2[...] = jnp.zeros(b2.shape, BF)
    loads["x"].wait()
    relay(r["x_in"], x_ref)

    def statistics(buf, position, targets, value):
        buf[position] = value
        return [send(buf.at[position], buf.at[position], t) for t in targets]

    def total(buf, copies):
        for copy in copies:
            copy.wait_recv()
        return jnp.sum(buf[...], axis=0)

    first = r["first"]

    def product(blocks, start):
        def body(h, carry):
            left = jnp.concatenate(
                [x_ref[rows(h), pl.ds(pl.multiple_of(o * RB, 128), RB)] for o in blocks], axis=1
            )
            right = jnp.concatenate([reduce_block(o)[...] for o in blocks], axis=0)
            part = dot(left, right)
            first[rows(h), :] = part if start else first[rows(h), :] + part
            return carry

        lax.fori_loop(0, 2, body, 0)

    if own_gather:
        for part in g_reduce:
            part.forward(0)
        twin_y(0, z)
        for rank in (1, 2):
            for part in g_reduce:
                part.forward(rank)
        product([zz * D + y for zz in range(H)], True)
        for rank in range(3):
            g_group.forward(rank)
        sources = [z]
        sources.append(g_expand.forward(0))
        twin(sources[1] * D + y)
        for number in range(4):
            for part in g_reduce:
                part.finish(number)
        for dy in range(1, D):
            product([zz * D + lax.rem(y + dy, D) for zz in range(H)], False)
    else:
        def body(h, carry):
            first[rows(h), :] = dot(x_ref[rows(h), :], wr[...])
            return carry

        lax.fori_loop(0, 2, body, 0)

    def moments(ref):
        def body(h, carry):
            v = ref[rows(h), :]
            return (
                carry[0] + jnp.sum(v, axis=0, keepdims=True) * valid(h),
                carry[1] + jnp.sum(v * v, axis=0, keepdims=True) * valid(h),
            )

        zero = jnp.zeros((1, ref.shape[1]), F32)
        return jnp.concatenate(lax.fori_loop(0, 2, body, (zero, zero)), axis=0)

    def average_and_inverse(sums):
        mean = sums[0:1] / pixels
        return mean, lax.rsqrt(sums[1:2] / pixels - mean * mean + NORM_EPS)

    stat1 = statistics(r["st1"], owner, family, moments(first))

    wall, wallt, gf = r["wall"], r["wallt"], r["gf"]
    if own_gather:
        g_expand.send_z(2)
        sources.append(g_expand.forward(1))
        twin(sources[2] * D + y)
        for number in range(4):
            g_group.finish(number)
        for o in range(HD):
            gf[o * GB : (o + 1) * GB, :] = wg[o].astype(F32)[0:GB]
    else:
        gf[...] = r["wg_full"][...].astype(F32)

    def spread(t, carry):
        piece = gf[pl.ds(pl.multiple_of(t * GROUP, 8), GROUP), :]
        full = jnp.where(block_diagonal, jnp.concatenate([piece] * (MID // GROUP), axis=0), 0.0)
        wall[pl.ds(pl.multiple_of(t * MID, 16), MID), :] = full.astype(BF)
        wallt[pl.ds(pl.multiple_of((8 - t) * MID, 16), MID), :] = full.T.astype(BF)
        return carry

    lax.fori_loop(0, 9, spread, 0)
    mean1, inv1 = average_and_inverse(total(r["st1"], stat1))
    gain1, shift1 = inner_ref[0:1, :], inner_ref[1:2, :]
    slope1 = r["slope1"]

    def activate(h):
        ok = valid(h)

        def body(w, carry):
            v = (first[tile(h, w), :] - mean1) * inv1
            v = v * gain1 + shift1
            q = jax.nn.sigmoid(v)
            a1[slab(h + 1, w + 1, N), :] = (v * q * ok).astype(BF)
            slope1[tile(h, w), :] = q * (1.0 + v * (1.0 - q)) * ok
            return carry

        lax.fori_loop(0, W, body, 0)

    class Halo:
        def __init__(self, ref):
            self.up = make(ref.at[slab(1, 1, R)], ref.at[slab(3, 1, R)], dev(H - 1, None, 0))
            self.down = make(ref.at[slab(2, 1, R)], ref.at[slab(0, 1, R)], dev(1, None, 0))

        def start_up(self):
            pl.when(z > 0)(self.up.start)

        def start_down(self):
            pl.when(z < H - 1)(self.down.start)

        def arrived(self):
            pl.when(z > 0)(self.down.wait_recv)
            pl.when(z < H - 1)(self.up.wait_recv)

        def sent(self):
            pl.when(z > 0)(self.up.wait_send)
            pl.when(z < H - 1)(self.down.wait_send)

    halo1, halo2 = Halo(a1), Halo(b2)
    activate(0)
    halo1.start_up()
    activate(1)
    halo1.start_down()

    def convolve(ref, weights, out, edge):
        def body(h, carry):
            if edge:
                hh, base, count = 3 * h, 6 * h, 1
            else:
                hh, base, count = 1, 3 * (1 - h), 2
            left = jnp.concatenate(
                [ref[slab(hh + i, kc, R), :] for i in range(count) for kc in range(3)], axis=1
            )
            part = dot(left, weights[pl.ds(pl.multiple_of(base * MID, 16), 3 * count * MID), :])
            out[rows(h), :] = out[rows(h), :] + part if edge else part
            return carry

        lax.fori_loop(0, 2, body, 0)

    second = r["second"]
    convolve(a1, wall, second, False)
    if own_gather:
        sources.append(g_expand.forward(2))
        twin(sources[3] * D + y)
        twin_y(1, sources[1])
        twin_y(2, sources[2])
    halo1.arrived()
    convolve(a1, wall, second, True)
    stat2 = statistics(r["st2"], owner, family, moments(second))
    if own_gather:
        twin_y(3, sources[3])
    mean2, inv2 = average_and_inverse(total(r["st2"], stat2))
    gain2, shift2 = inner_ref[2:3, :], inner_ref[3:4, :]
    a2, slope2 = r["a2"], r["slope2"]

    def activate_two(h):
        ok = valid(h)

        def body(w, carry):
            n = (second[tile(h, w), :] - mean2) * inv2
            second[tile(h, w), :] = n
            v = n * gain2 + shift2
            q = jax.nn.sigmoid(v)
            a2[tile(h, w), :] = (v * q * ok).astype(BF)
            slope2[tile(h, w), :] = q * (1.0 + v * (1.0 - q)) * ok
            return carry

        lax.fori_loop(0, W, body, 0)

    activate_two(1 - xp)
    ax_in = send(a2.at[rows(1 - xp)], r["ax"], x_peer)
    activate_two(xp)

    for copy in twin_in:
        copy.wait_recv()
    ax_in.wait_recv()
    third, tsend, trecv = r["third"], r["tsend"], r["trecv"]
    left = jnp.concatenate([a2[rows(xp), :], r["ax"][...]], axis=1)

    def expand(j, core):
        right = jnp.concatenate([we[:, quarter(j, core)], wep[:, quarter(j, core)]], axis=0)
        return dot(left, right)

    core_in = []
    for j in range(2):
        tsend[j] = expand(j, 1 - k).astype(BF)
        core_in.append(send(tsend.at[j], trecv.at[j], core_peer))
    for j in range(2):
        third[j] = expand(j, k)
    okx = valid(xp)
    sums = []
    for j in range(2):
        core_in[j].wait_recv()

        def body(w, carry):
            at = pl.ds(pl.multiple_of(w * N, 16), N)
            v = third[j, at, :] + trecv[j, at, :].astype(F32)
            third[j, at, :] = v
            return carry[0] + jnp.sum(v, axis=0, keepdims=True), carry[1] + jnp.sum(
                v * v, axis=0, keepdims=True
            )

        zero = jnp.zeros((1, OUT), F32)
        sums.append(lax.fori_loop(0, W, body, (zero, zero)))
    r["tx"][...] = third[1 - xp].astype(BF)
    position = xp * HD + owner
    both = family + twin_family
    stat3 = statistics(
        r["st3"],
        position,
        both,
        jnp.concatenate(
            [jnp.concatenate([s[i] for s in sums], axis=1) * okx for i in range(2)], axis=0
        ),
    )
    cut = (W + 1) // 2
    parts = [pl.ds(0, cut * N), pl.ds(cut * N, (W - cut) * N)]
    tx_in = [send(r["tx"].at[parts[0]], r["tother"].at[parts[0]], x_peer)]
    wrq = r["wrq"]

    def mids(chan):
        return pl.ds(pl.multiple_of(chan * MID, 128), MID)

    wrq[:, mids(c)] = wr[quarter(xp, k), :]
    wrq_in = [send(wr.at[quarter(xp, 1 - k), :], wrq.at[:, mids(c)], core_peer)]
    share = OUT // 2

    def send_wrq(n):
        target, core = ((x_peer, k), (diagonal, 1 - k))[n // 2]
        at = pl.ds(pl.multiple_of((2 * (1 - xp) + core) * OUT + n % 2 * share, 16), share)
        there = wrq.at[pl.ds(n % 2 * share, share), mids(c)]
        wrq_in.append(send(wr.at[at, :], there, target))

    a2t = r["a2t"]
    a2t[...] = a2[...].T
    ct_in.wait_recv()
    outer_in.wait_recv()
    mean3, inv3 = average_and_inverse(total(r["st3"], stat3))
    dpre, dother, bo = r["dpre"], r["dother"], r["bo"]
    mi3 = r["mi3"]
    for j in range(2):
        lanes = slice(j * OUT, (j + 1) * OUT)
        mi3[j] = jnp.concatenate([mean3[:, lanes], inv3[:, lanes]], axis=0)

    def outer_norm(j, h, values, grads, write, start=0, stop=W):
        m, iv = mi3[j, 0:1, :], mi3[j, 1:2, :]
        g, s = out2[j, 0:1, :], out2[j, 1:2, :]
        ok = valid(h)

        def body(w, carry):
            at = pl.ds(pl.multiple_of(w * N, 16), N)
            n = (values[0](at) - m) * iv
            values[1](at, n)
            v = n * g + s + x_ref[tile(h, w), quarter(j, k)].astype(F32)
            q = jax.nn.sigmoid(v)
            if write:
                bo[tile(h, w), :] = (v * q * ok).astype(BF)
            d = grads[0](at, w) * ok * (q * (1.0 + v * (1.0 - q)))
            grads[1](at, d)
            return carry[0] + jnp.sum(d, axis=0, keepdims=True), carry[1] + jnp.sum(
                d * n, axis=0, keepdims=True
            )

        zero = jnp.zeros((1, OUT), F32)
        return lax.fori_loop(start, stop, body, (zero, zero))

    def third_access(j):
        def get(at):
            return third[j, at, :]

        def put(at, n):
            third[j, at, :] = n

        def get_ct(at, w):
            return ct2[j, at, :].astype(F32)

        def put_d(at, d):
            dpre[j, at, :] = d

        return (get, put), (get_ct, put_d)

    st3b = r["st3b"]
    pair = r["pair"]
    for j, write in ((xp, True), (1 - xp, False)):
        pair[j] = jnp.concatenate(outer_norm(j, xp, *third_access(j), write), axis=0)
    stat3b = statistics(st3b, position, both, jnp.concatenate([pair[0], pair[1]], axis=1))

    tx_in.append(send(r["tx"].at[parts[1]], r["tother"].at[parts[1]], x_peer))
    send_wrq(0)
    tx_in[0].wait_recv()
    nother = r["nother"]

    def get_other(at):
        return r["tother"][at, :].astype(F32)

    def put_other(at, n):
        nother[at, :] = n

    def get_ct_other(at, w):
        return ct_ref[tile(1 - xp, w), :].astype(F32)

    def put_d_other(at, d):
        dother[at, :] = d

    other_row = ((get_other, put_other), (get_ct_other, put_d_other), True)
    outer_norm(xp, 1 - xp, *other_row, 0, cut)
    total3 = total(st3b, stat3b)
    r["tot3"][...] = total3
    for j in range(2):
        lanes = slice(j * OUT, (j + 1) * OUT)
        pair[j] = total3[:, lanes] / pixels
    piece = r["piece"]

    def back_three(j, h, upstream, normed):
        factor = out2[j, 0:1, :] * mi3[j, 1:2, :] * valid(h)
        sh, ga = pair[j, 0:1, :], pair[j, 1:2, :]

        def body(w, carry):
            at = pl.ds(pl.multiple_of(w * N, 16), N)
            v = factor * (upstream(at) - sh - normed(at) * ga)
            piece[tile(h, w), quarter(j, k)] = v.astype(BF)
            return carry

        lax.fori_loop(0, W, body, 0)
        part = piece.at[rows(h), quarter(j, k)]
        return send(part, part, core_peer)

    core_in = [
        back_three(j, xp, lambda at, j=j: dpre[j, at, :], lambda at, j=j: third[j, at, :])
        for j in range(2)
    ]
    for copy in core_in:
        copy.wait_recv()
    agrad = r["agrad"]
    r["agsend"][...] = dot_nt(piece[rows(xp), :], wep[...]).astype(BF)
    ag_in = send(r["agsend"], r["agrecv"], x_peer)
    part = piece.at[rows(xp), quarter(xp, k)]
    piece_in = send(part, part, x_peer)
    for n in range(1, 4):
        send_wrq(n)
    agrad[rows(xp), :] = dot_nt(piece[rows(xp), :], we[...])
    tx_in[1].wait_recv()
    outer_norm(xp, 1 - xp, *other_row, cut, W)
    core_other = back_three(xp, 1 - xp, lambda at: dother[at, :], lambda at: nother[at, :])

    class Scatter:
        def __init__(self, name, block, parts=1):
            self.block = block
            self.parts = parts
            self.ys, self.yr = r[name + "_ys"], r[name + "_yr"]
            self.zs, self.zr = r[name + "_zs"], r[name + "_zr"]
            self.own = r[name + "_own"]
            self.along_y, self.along_z = {}, []
            self.pair, self.cross = {}, {}
            self.base = used[0]
            used[0] += H * parts

        def start(self, targets):
            for slot, zi in targets:
                self.along_y[slot] = []
                for dy in range(1, D):
                    n = (dy - 1) * H * self.parts + slot
                    self.ys[n] = self.block(zi * D + lax.rem(y + dy, D), slot % self.parts).astype(BF)
                    self.along_y[slot].append(
                        (n, send(self.ys.at[n], self.yr.at[n], dev(0, None, dy)))
                    )

        def middle(self, targets):
            for slot, zi in targets:
                part = slot % self.parts
                value = self.block(zi * D + y, part)
                for n, copy in self.along_y[slot]:
                    copy.wait_recv()
                    value = value + self.yr[n].astype(F32)
                other = zi != z

                @pl.when(jnp.logical_not(other))
                def keep():
                    self.own[part] = value

                self.zs[slot] = value.astype(BF)
                target = {"height": zi, "chan": c, "dp": y}
                here = z * self.parts + part
                at = (self.base + slot, self.base + here)
                copy = make(self.zs.at[slot], self.zr.at[here], target, at)
                pl.when(other)(copy.start)
                self.along_z.append((other, copy))

        def fold(self, base, zone):
            far, kept = zone + 1 - lax.rem(z, 2), zone + lax.rem(z, 2)

            def received(zi):
                value = self.block(zi * D + y, 0)
                for dy in range(1, D):
                    value = value + self.yr[(dy - 1) * H + base + lax.rem(zi - zone + k, 2)].astype(F32)
                return value

            for slot in (base, base + 1):
                for n, copy in self.along_y[slot]:
                    copy.wait_recv()
            self.zs[base] = received(far).astype(BF)
            target = {"height": near[0], "chan": c, "dp": y}
            pair = send(self.zs.at[base], self.zr.at[base], target)

            def rest():
                value = received(kept)
                pair.wait_recv()
                value = value + self.zr[base].astype(F32)
                other = kept != z

                @pl.when(jnp.logical_not(other))
                def keep():
                    self.own[0] = value

                self.zs[base + 1] = value.astype(BF)
                target = {"height": lax.rem(z + 2, 4), "chan": c, "dp": y}
                at = (self.base, self.base)
                copy = make(self.zs.at[base + 1], self.zr.at[H], target, at)
                pl.when(other)(copy.start)
                self.along_z.append((other, copy))
                self.last = copy

            return rest

        def summed_y(self, slot, zi):
            part = slot % self.parts
            value = self.block(zi * D + y, part)
            for n, copy in self.along_y[slot]:
                copy.wait_recv()
                value = value + self.yr[n].astype(F32)
            return value

        def to_near(self, slot, zi):
            self.zs[slot] = self.summed_y(slot, zi).astype(BF)
            target = {"height": near[0], "chan": c, "dp": y}
            self.pair[slot] = send(self.zs.at[slot], self.zr.at[slot], target)

        def from_near(self, slot):
            self.pair[slot].wait_recv()
            return self.zr[slot].astype(F32)

        def across(self, slot, zi, pair):
            value = self.summed_y(slot, zi) + self.from_near(pair)
            self.zs[slot] = value.astype(BF)
            target = {"height": lax.rem(z + 2, 4), "chan": c, "dp": y}
            self.cross[slot] = send(self.zs.at[slot], self.zr.at[slot], target)

        def whole_sum(self, slot, zi, pair, cross):
            value = self.summed_y(slot, zi) + self.from_near(pair)
            self.cross[cross].wait_recv()
            return value + self.zr[cross].astype(F32)

        def finish_fold(self):
            self.last.wait_recv()
            return self.own[0] + self.zr[H].astype(F32)

        def finish(self, part=0):
            value = self.own[part]
            for dz in range(1, H):
                s = lax.rem(z + dz, H) * self.parts + part
                at = (self.base, self.base + s)
                make(self.zs.at[0], self.zr.at[s], dev(dz), at).wait_recv()
                value = value + self.zr[s].astype(F32)
            return value

        def sent(self):
            for other, copy in self.along_z:
                pl.when(other)(copy.wait_send)

    def wide(left_ref, right_ref, o, part, parts):
        share = left_ref.shape[0] // parts
        left = left_ref[part * share : (part + 1) * share, :]
        return dot(left, right_ref[:, pl.ds(pl.multiple_of(o * EB, 128), EB)])

    def slope_two(h, received, carry):
        def body(w, carry):
            if received:
                up = r["agrecv"][pl.ds(pl.multiple_of(w * N, 16), N), :].astype(F32)
            else:
                up = agrad[tile(h, w), :]
            d = up * slope2[tile(h, w), :]
            agrad[tile(h, w), :] = d
            return carry[0] + jnp.sum(d, axis=0, keepdims=True), carry[1] + jnp.sum(
                d * second[tile(h, w), :], axis=0, keepdims=True
            )

        return lax.fori_loop(0, W, body, carry)

    parity = lax.rem(z, 2)
    zones = (2 * xp, 2 * (1 - xp))
    early = [(0, zones[0] + k), (1, zones[0] + 1 - k)]
    late = [(2, zones[1] + k), (3, zones[1] + 1 - k)]
    around = [(0, lax.rem(z + 2, 4)), (1, 3 - z), (2, near[0]), (3, z)]
    if own_gather:
        s_expand = Scatter("eg", lambda o, part: wide(a2t, piece, o, part, 1))
        core_other.wait_recv()
        s_expand.start(early)
    zero = jnp.zeros((1, MID), F32)
    carry = slope_two(xp, False, (zero, zero))
    ag_in.wait_recv()
    carry = slope_two(1 - xp, True, carry)
    stat2b = statistics(r["st2b"], owner, family, jnp.concatenate(carry, axis=0))

    def turn(w, carry):
        r["turned"][:, w] = jnp.swapaxes(jnp.stack([bo[tile(h, w), :] for h in range(2)]), 0, 1)
        return carry

    lax.fori_loop(0, W, turn, 0)
    if own_gather:
        rest_early = s_expand.fold(0, zones[0])
    total2 = total(r["st2b"], stat2b)
    b2n = r["b2n"]

    def norm_two(h):
        factor = gain2 * inv2 * valid(h)
        sh, ga = total2[0:1] / pixels, total2[1:2] / pixels

        def body(w, carry):
            v = factor * (agrad[tile(h, w), :] - sh - second[tile(h, w), :] * ga)
            v = v.astype(BF)
            b2[slab(h + 1, w + 1, N), :] = v
            b2n[tile(h, w), :] = v
            return carry

        lax.fori_loop(0, W, body, 0)

    norm_two(0)
    halo2.start_up()
    norm_two(1)
    halo2.start_down()
    back1 = r["second_back"]
    convolve(b2, wallt, back1, False)
    b2t = r["b2t"]
    b2t[...] = b2n[...].T
    ggf = r["ggf"]
    fold = jnp.where(
        jnp.bitwise_and(lax.broadcasted_iota(jnp.int32, (GROUP, MID), 1), GROUP - 1)
        == lax.broadcasted_iota(jnp.int32, (GROUP, MID), 0),
        1.0,
        0.0,
    ).astype(BF)

    def group_grad(t, carry):
        kr, kc = lax.div(t, 3), lax.rem(t, 3)
        left = jnp.concatenate([a1[slab(kr, kc, R), :], a1[slab(kr + 1, kc, R), :]], axis=0)
        turned = jnp.where(block_diagonal, dot(b2t[...], left), 0.0).astype(BF)
        ggf[pl.ds(pl.multiple_of(t * GROUP, 8), GROUP), :] = dot_nt(fold, turned)
        return carry

    lax.fori_loop(0, 9, group_grad, 0)

    if own_gather:
        for o in range(HD):
            r["ggs"][o] = jnp.concatenate(
                [ggf[o * GB : (o + 1) * GB, :], jnp.zeros((SLOT - GB, MID), F32)], axis=0
            )
    piece_in.wait_recv()
    part = piece.at[rows(1 - xp), quarter(1 - xp, k)]
    core_last = send(part, part, core_peer)
    if own_gather:
        s_expand.start(late[:1])
    halo2.arrived()
    convolve(b2, wallt, back1, True)

    def slope_one(i, carry):
        h, w = lax.div(i, W), lax.rem(i, W)
        d = back1[tile(h, w), :] * slope1[tile(h, w), :]
        n = (first[tile(h, w), :] - mean1) * inv1
        first[tile(h, w), :] = n
        back1[tile(h, w), :] = d
        return carry[0] + jnp.sum(d, axis=0, keepdims=True), carry[1] + jnp.sum(
            d * n, axis=0, keepdims=True
        )

    carry = lax.fori_loop(0, 2 * W, slope_one, (zero, zero))
    stat1b = statistics(r["st1b"], owner, family, jnp.concatenate(carry, axis=0))

    core_last.wait_recv()
    if not own_gather:
        core_other.wait_recv()
    if own_gather:
        s_expand.start(late[1:])
        s_group = Scatter("gg", lambda o, part: r["ggs"][o])
        s_group.start(around)
    else:
        r["group_out"][...] = ggf[...].astype(BF)
        r["expand_out"][...] = dot(a2t[...], piece[...]).astype(BF)

    total1 = total(r["st1b"], stat1b)
    b1, ball = r["b1"], r["ball"]

    def norm_one(h):
        factor = gain1 * inv1 * valid(h)
        sh, ga = total1[0:1] / pixels, total1[1:2] / pixels

        def body(w, carry):
            v = factor * (back1[tile(h, w), :] - sh - first[tile(h, w), :] * ga)
            v = v.astype(BF)
            b1[tile(h, w), :] = v
            ball[tile(h, w), mids(c)] = v
            return carry

        lax.fori_loop(0, W, body, 0)

    ball_x, ball_core, ball_far = [], [], []
    for h in range(2):
        norm_one(h)
        part = ball.at[rows(h), mids(c)]
        ball_x.append(send(part, part, x_peer))
        ball_core.append(send(part, part, core_peer))

    def forward_ball(h):
        ball_x[h].wait_recv()
        part = ball.at[rows(h), mids(cx)]
        ball_far.append(send(part, part, core_peer))

    b1t = r["b1t"]
    b1t[...] = b1[...].T
    if own_gather:
        s_reduce = Scatter("rg", lambda o, part: wide(b1t, x_ref, o, part, 2), 2)
        here, there = z - parity, lax.rem(z - parity + 2, 4)
        ends = (there + 1 - parity, there + parity, here + 1 - parity, z)
        halves = [(2 * slot + part, zi) for slot, zi in enumerate(ends) for part in range(2)]
        s_reduce.start(halves)
        rest_early()
        rest_late = s_expand.fold(2, zones[1])
        s_group.middle(around)
        for half in halves[0:2]:
            s_reduce.to_near(*half)
        forward_ball(0)
        rest_late()
        for half in halves[2:4]:
            s_reduce.across(*half, half[0] - 2)
        forward_ball(1)
        for half in halves[4:6]:
            s_reduce.to_near(*half)
    else:
        forward_ball(0)
        forward_ball(1)
        r["reduce_out"][...] = dot(b1t[...], x_ref[...]).astype(BF)
    ig = r["ig"]

    def chip_mids(n):
        return pl.ds(pl.multiple_of(n * 2 * MID, 128), 2 * MID)

    r["inner_grad"][...] = jnp.concatenate(
        [total1[1:2], total1[0:1], total2[1:2], total2[0:1]], axis=0
    )
    mine = r["tot3"][:, pl.ds(pl.multiple_of(xp * OUT, 128), OUT)]
    r["outer_grad"][...] = jnp.concatenate([mine[1:2], mine[0:1]], axis=0)
    for copy in wrq_in:
        copy.wait_recv()
    ig[rows(xp), :] = dpre[xp]
    ig[rows(1 - xp), :] = dother[...]

    def input_part(h, n):
        ig[rows(h), :] = ig[rows(h), :] + dot_nt(ball[rows(h), chip_mids(n)], wrq[:, chip_mids(n)])

    for h in range(2):
        ball_core[h].wait_recv()
        input_part(h, xp)
    for h in range(2):
        ball_far[h].wait_recv()
        input_part(h, 1 - xp)
    if own_gather:
        r["group_out"][...] = s_group.finish()[0:GB]
        r["expand_out"][...] = s_expand.finish_fold()
        turned = jnp.concatenate(
            [s_reduce.whole_sum(*half, half[0] - 2, half[0] - 4) for half in halves[6:8]], axis=0
        )
        r["reduce_out"][...] = turned.T
        for scatter in (s_group, s_expand, s_reduce):
            scatter.sent()
    for copy in sends:
        copy.wait_send()
    halo1.sent()
    halo2.sent()


def adamw_step(master, gradient, moment_one, moment_two, average, rate):
    first_new = 0.5 * moment_one + 0.5 * gradient
    second_new = 0.5 * moment_two + 0.5 * gradient * gradient
    correct = 1.0 - 0.5**STEP
    direction = first_new / correct / (jnp.sqrt(second_new / correct) + 1e-08)
    master_new = master - rate * (direction + 0.05 * master)
    average_new = 0.75 * average + 0.25 * master_new
    return (first_new, second_new, master_new, average_new)


def last_kernel(*refs):
    ig_ref, bo_ref = refs[:2]
    ins, (bo_out, ig_out), outs = refs[2:27], refs[27:29], list(refs[29:-3])
    turned, bo_sem, ig_sem = refs[-3:]
    W = turned.shape[1]
    bo_copy = pltpu.make_async_copy(bo_ref, bo_out, bo_sem)
    bo_copy.start()

    def body(w, carry):
        turned[:, w] = jnp.swapaxes(ig_ref[:, w], 0, 1)
        return carry

    lax.fori_loop(0, W, body, 0)
    ig_copy = pltpu.make_async_copy(turned, ig_out, ig_sem)
    ig_copy.start()
    for n in range(5):
        gradient, master, one, two, average = (ref[...] for ref in ins[5 * n : 5 * n + 5])
        rate = CONV_RATE if n < 3 else NORM_RATE
        first, second, new, mean = adamw_step(master, gradient, one, two, average, rate)
        values = [gradient, first, second, new] + ([new.astype(BF)] if n < 3 else []) + [mean]
        for value in values:
            outs.pop(0)[...] = value
    bo_copy.wait()
    ig_copy.wait()


def local(
    inputs, cotangent,
    reduce_master, reduce_first, reduce_second, reduce_average,
    group_master, group_first, group_second, group_average,
    expand_master, expand_first, expand_second, expand_average,
    inner_master, inner_first, inner_second, inner_average,
    outer_master, outer_first, outer_second, outer_average,
):
    N, rows, W, CIN = inputs.shape
    OUT = cotangent.shape[3]
    MID = inner_master.shape[1]
    H, D = lax.axis_size("height"), lax.axis_size("dp")
    HD = H * D
    R = W * N
    GB = group_master.shape[0]
    RB, EB = reduce_master.shape[0], expand_master.shape[1]
    own_gather = RB % 128 == 0 and EB % 128 == 0
    dims = dict(H=H, D=D, N=N, W=W, MID=MID, OUT=OUT, CIN=CIN, own_gather=own_gather)

    shards = dict(x=inputs.transpose(0, 2, 1, 3), ct=cotangent.transpose(0, 2, 1, 3))
    shards.update(inner=inner_master, outer=outer_master)
    ins = {}
    outs = dict(
        turned=((N, W, rows, OUT), BF),
        ig=((rows * R, OUT), F32),
        inner_grad=(inner_master.shape, F32),
        outer_grad=(outer_master.shape, F32),
    )
    scratch = dict(
        x=((rows * R, CIN), BF),
        bo=((rows * R, OUT), BF),
        ct=((rows * R, OUT), BF),
        wep=((MID, CIN), BF),
        ct2=((2, R, OUT), BF),
        out2=((2, 2, OUT), F32),
        first=((2 * R, MID), F32),
        second=((2 * R, MID), F32),
        slope1=((2 * R, MID), F32),
        slope2=((2 * R, MID), F32),
        a1=((4 * (W + 2) * N, MID), BF),
        b2=((4 * (W + 2) * N, MID), BF),
        wall=((9 * MID, MID), BF),
        wallt=((9 * MID, MID), BF),
        gf=((9 * GROUP, MID), F32),
        ggf=((9 * GROUP, MID), F32),
        st1=((HD, 2, MID), F32),
        st2=((HD, 2, MID), F32),
        st3=((2 * HD, 2, 2 * OUT), F32),
        st3b=((2 * HD, 2, 2 * OUT), F32),
        st2b=((HD, 2, MID), F32),
        st1b=((HD, 2, MID), F32),
        tot3=((2, 2 * OUT), F32),
        a2=((2 * R, MID), BF),
        a2t=((MID, 2 * R), BF),
        ax=((R, MID), BF),
        third=((2, R, OUT), F32),
        tx=((R, OUT), BF),
        tother=((R, OUT), BF),
        nother=((R, OUT), F32),
        dother=((R, OUT), F32),
        mi3=((2, 2, OUT), F32),
        pair=((2, 2, OUT), F32),
        wrq=((OUT, 4 * MID), BF),
        ball=((2 * R, 4 * MID), BF),
        tsend=((2, R, OUT), BF),
        trecv=((2, R, OUT), BF),
        dpre=((2, R, OUT), F32),
        piece=((2 * R, CIN), BF),
        agrad=((2 * R, MID), F32),
        agsend=((R, MID), BF),
        agrecv=((R, MID), BF),
        b2n=((2 * R, MID), BF),
        b2t=((MID, 2 * R), BF),
        second_back=((2 * R, MID), F32),
        b1=((2 * R, MID), BF),
        b1t=((MID, 2 * R), BF),
    )
    if own_gather:
        shards.update(rm=reduce_master, gm=group_master, em=expand_master)
        outs.update(
            reduce_out=((RB, MID), F32), group_out=((GB, MID), F32), expand_out=((MID, EB), F32)
        )
        scratch.update(
            wr=((CIN, MID), BF), we=((MID, CIN), BF), wg=((HD, SLOT, MID), BF),
            ggs=((HD, SLOT, MID), F32),
        )
        for name, n, shape in (
            ("rg", 2, (MID // 2, RB)), ("eg", 1, (MID, EB)), ("gg", 1, (SLOT, MID))
        ):
            scratch[name + "_ys"] = scratch[name + "_yr"] = (((D - 1) * H * n, *shape), BF)
            scratch[name + "_zs"] = ((H * n, *shape), BF)
            scratch[name + "_zr"] = ((H * n + 1, *shape), BF)
            scratch[name + "_own"] = ((n, *shape), F32)
    else:
        both = ("height", "dp")
        ins.update(
            wr_full=lax.all_gather(reduce_master.astype(BF), both, axis=0, tiled=True),
            wg_full=lax.all_gather(group_master.astype(BF), both, axis=0, tiled=True),
            we_full=lax.all_gather(expand_master.astype(BF), both, axis=1, tiled=True),
        )
        outs.update(
            reduce_out=((MID, CIN), BF),
            group_out=((9 * GROUP, MID), BF),
            expand_out=((MID, CIN), BF),
        )
    dims["loads"] = list(shards)
    scratch.update({name + "_in": (a.shape, a.dtype) for name, a in shards.items()})
    names = [*(name + "_hbm" for name in shards), *ins, *outs, *scratch, "lsem", "ssem", "rsem"]
    whole = pl.BlockSpec(memory_space=pltpu.VMEM)
    results = pl.pallas_call(
        functools.partial(block_kernel, names, dims),
        out_shape=[pltpu.VMEM(*v) for v in outs.values()],
        in_specs=[pl.BlockSpec(memory_space=pltpu.HBM)] * len(shards) + [whole] * len(ins),
        out_specs=[whole] * len(outs),
        scratch_shapes=[pltpu.VMEM(*v) for v in scratch.values()]
        + [pltpu.SemaphoreType.DMA((len(shards),))]
        + [pltpu.SemaphoreType.DMA((dims.get("semaphores", SEMAPHORES + 16 * D),))] * 2,
        compiler_params=pltpu.CompilerParams(
            collective_id=0, has_side_effects=True, vmem_limit_bytes=48 << 20
        ),
        name="block",
    )(
        *(pltpu.with_memory_space_constraint(v, pltpu.HBM) for v in shards.values()),
        *(pltpu.with_memory_space_constraint(v, pltpu.VMEM) for v in ins.values()),
    )
    got = dict(zip(outs, results, strict=True))
    reduce_grad, group_grad, expand_grad = got["reduce_out"], got["group_out"], got["expand_out"]
    if not own_gather:
        both = ("height", "dp")
        reduce_grad = lax.psum_scatter(reduce_grad.T, both, scatter_dimension=0, tiled=True).astype(F32)
        group_grad = lax.psum_scatter(group_grad, both, scatter_dimension=0, tiled=True).astype(F32)
        expand_grad = lax.psum_scatter(expand_grad, both, scatter_dimension=1, tiled=True).astype(F32)
    groups = (
        (reduce_grad, reduce_master, reduce_first, reduce_second, reduce_average),
        (group_grad, group_master, group_first, group_second, group_average),
        (expand_grad, expand_master, expand_first, expand_second, expand_average),
        (got["inner_grad"], inner_master, inner_first, inner_second, inner_average),
        (got["outer_grad"], outer_master, outer_first, outer_second, outer_average),
    )
    shapes = [
        jax.ShapeDtypeStruct((N, W, rows, OUT), BF),
        jax.ShapeDtypeStruct((N, W, rows, OUT), F32),
    ]
    for n, group in enumerate(groups):
        kinds = [F32] * 4 + ([BF] if n < 3 else []) + [F32]
        shapes += [jax.ShapeDtypeStruct(group[0].shape, kind) for kind in kinds]
    flat = [got["ig"].reshape(rows, W, N, OUT), got["turned"]]
    flat += [a for group in groups for a in group]
    news = pl.pallas_call(
        last_kernel,
        out_shape=shapes,
        in_specs=[whole] * len(flat),
        out_specs=[pl.BlockSpec(memory_space=pltpu.HBM)] * 2 + [whole] * (len(shapes) - 2),
        scratch_shapes=[
            pltpu.VMEM((N, W, rows, OUT), F32),
            pltpu.SemaphoreType.DMA,
            pltpu.SemaphoreType.DMA,
        ],
        compiler_params=pltpu.CompilerParams(vmem_limit_bytes=40 << 20),
        name="adamw",
    )(*flat)
    pixel_outs = (a.transpose(0, 2, 1, 3) for a in news[:2])
    return (*pixel_outs, *news[2:])


def solution(mesh):
    pixel = P("dp", "height", None, "chan")
    first = P(("height", "dp"), "chan")
    last = P("chan", ("height", "dp"))
    table = P(None, "chan")
    return jax.shard_map(
        local,
        mesh=mesh,
        in_specs=(P("dp", "height", None, None), pixel)
        + (first,) * 8
        + (last,) * 4
        + (table,) * 8,
        out_specs=(pixel, pixel) + (first,) * 12 + (last,) * 6 + (table,) * 10,
        check_vma=False,
    )
```

```python
import functools

import jax
import jax.numpy as jnp
from jax import lax
from jax.experimental import pallas as pl
from jax.experimental.pallas import tpu as pltpu
from jax.sharding import PartitionSpec as P

GROUP = 32
HEIGHT = 7
STEP = 10
NORM_EPS = 1e-05
CONV_RATE = 0.02
NORM_RATE = 0.3

BF = jnp.bfloat16
F32 = jnp.float32
MESH = pl.DeviceIdType.MESH
SEMAPHORES = 192
SLOT = 48


def dot(a, b):
    return jnp.dot(a, b, preferred_element_type=F32)


def dot_nt(a, b):
    return lax.dot_general(a, b, (((1,), (1,)), ((), ())), preferred_element_type=F32)


def block_kernel(names, dims, *refs):
    r = dict(zip(names, refs, strict=True))
    H, D, N, W, MID, OUT, CIN = (dims[k] for k in ("H", "D", "N", "W", "MID", "OUT", "CIN"))
    own_gather = dims["own_gather"]
    R = W * N
    PITCH = (W + 2) * N
    HD = H * D
    pixels = float(N * D * HEIGHT * W)
    x_ref, ct_ref, inner_ref, outer_ref = r["x"], r["ct"], r["inner_in"], r["outer_in"]
    loads = {
        name: pltpu.make_async_copy(r[name + "_hbm"], r[name + "_in"], r["lsem"].at[i])
        for i, name in enumerate(dims["loads"])
    }
    for name in reversed(dims["loads"]):
        loads[name].start()

    z = lax.axis_index("height")
    c = lax.axis_index("chan")
    y = lax.axis_index("dp")
    xp = lax.div(c, 2)
    k = lax.rem(c, 2)
    cx = lax.rem(c + 2, 4)
    cc = c + 1 - 2 * k
    owner = z * D + y

    def dev(dz=0, chan=None, dy=0):
        return {
            "height": lax.rem(z + dz, H),
            "chan": c if chan is None else chan,
            "dp": lax.rem(y + dy, D),
        }

    offsets = [(dz, dy) for dz in range(H) for dy in range(D)]
    family = [dev(dz, None, dy) for dz, dy in offsets if dz or dy]
    twin_family = [dev(dz, cx, dy) for dz, dy in offsets]
    core_peer = dev(0, cc, 0)
    x_peer = dev(0, cx, 0)
    diagonal = dev(0, cx + 1 - 2 * k, 0)

    def rows(h):
        return pl.ds(pl.multiple_of(h * R, 16), R)

    def tile(h, w):
        return pl.ds(pl.multiple_of(h * R + w * N, 16), N)

    def slab(hh, ww, count):
        return pl.ds(pl.multiple_of((hh * (W + 2) + ww) * N, 16), count)

    def quarter(j, core):
        return pl.ds(pl.multiple_of((2 * j + core) * OUT, 128), OUT)

    def valid(h):
        return jnp.where(z * 2 + h < HEIGHT, 1.0, 0.0).astype(F32)

    sends = []
    used = [0]

    def make(src, dst, target, at=None):
        if at is None:
            at = (used[0], used[0])
            used[0] += 1
        return pltpu.make_async_remote_copy(
            src_ref=src,
            dst_ref=dst,
            send_sem=r["ssem"].at[at[0]],
            recv_sem=r["rsem"].at[at[1]],
            device_id=target,
            device_id_type=MESH,
        )

    def send(src, dst, target):
        copy = make(src, dst, target)
        copy.start()
        sends.append(copy)
        return copy

    barrier = pltpu.get_barrier_semaphore()
    everyone = family + twin_family + [core_peer, diagonal]
    for target in everyone:
        pl.semaphore_signal(barrier, inc=1, device_id=target, device_id_type=MESH)
    a1, b2 = r["a1"], r["b2"]
    lane_group = lax.shift_right_logical(lax.broadcasted_iota(jnp.int32, (MID, MID), 1), 5)
    row_group = lax.shift_right_logical(lax.broadcasted_iota(jnp.int32, (MID, MID), 0), 5)
    block_diagonal = lane_group == row_group
    if own_gather:
        wr, we, wg = r["wr"], r["we"], r["wg"]
        RB, EB = r["rm_in"].shape[0], r["em_in"].shape[1]
        GB = r["gm_in"].shape[0]

        def reduce_block(o):
            return wr.at[pl.ds(pl.multiple_of(o * RB, 16), RB), :]

        def expand_block(o):
            return we.at[:, pl.ds(pl.multiple_of(o * EB, 128), EB)]

        def group_block(o):
            return wg.at[o]

        loads["rm"].wait()
        reduce_block(owner)[...] = r["rm_in"][...].astype(BF)
    else:
        wr, we = r["wr_full"], r["we_full"]

    pl.semaphore_wait(barrier, len(everyone))

    near = [z + 1 - 2 * lax.rem(z, 2), jnp.where(z < 2, 2, 1), jnp.where(z < 2, 3, 0)]

    class Gather:
        def __init__(self, block):
            self.block = block
            self.here = block(owner)
            self.base = used[0]
            used[0] += H
            self.along_y = []

        def send_z(self, rank):
            target = {"height": near[rank], "chan": c, "dp": y}
            copy = make(self.here, self.here, target, (self.base + rank, self.base + z))
            copy.start()
            sends.append(copy)

        def send_y(self):
            self.pass_on(self.here)

        def pass_on(self, block):
            self.along_y.append([send(block, block, dev(0, None, dy)) for dy in range(1, D)])

        def forward(self, rank):
            source = near[rank]
            block = self.block(source * D + y)
            make(block, block, dev(), (self.base, self.base + source)).wait_recv()
            self.pass_on(block)
            return source

        def finish(self, number):
            for copy in self.along_y[number]:
                copy.wait_recv()

    if own_gather:
        def reduce_part(n):
            return lambda o: wr.at[pl.ds(pl.multiple_of(o * RB + n * (RB // 2), 16), RB // 2), :]

        g_reduce = [Gather(reduce_part(n)) for n in range(2)]
        g_group, g_expand = Gather(group_block), Gather(expand_block)
        for rank in range(3):
            for part in g_reduce:
                part.send_z(rank)
        for part in g_reduce:
            part.send_y()
        for name in ("gm", "em"):
            loads[name].wait()
        wg[owner] = jnp.concatenate(
            [r["gm_in"][...], jnp.zeros((SLOT - GB, MID), F32)], axis=0
        ).astype(BF)
        expand_block(owner)[...] = r["em_in"][...].astype(BF)
        for rank in range(3):
            g_group.send_z(rank)
        g_group.send_y()
    wep = r["wep"]
    twin_in = []

    def twin(o):
        twin_in.append(
            send(expand_block(o), wep.at[:, pl.ds(pl.multiple_of(o * EB, 128), EB)], x_peer)
        )

    def twin_y(number, zz):
        g_expand.finish(number)
        for dy in range(1, D):
            twin(zz * D + lax.rem(y + dy, D))

    if own_gather:
        g_expand.send_z(0)
        g_expand.send_z(1)
        g_expand.send_y()
        twin(owner)
    else:
        twin_in.append(send(we, wep, x_peer))

    def relay(source, target):
        def body(w, carry):
            turned = jnp.swapaxes(source[:, w], 0, 1)
            for h in range(2):
                target[tile(h, w), :] = turned[h]
            return carry

        lax.fori_loop(0, W, body, 0)

    loads["inner"].wait()
    loads["outer"].wait()
    loads["ct"].wait()
    relay(r["ct_in"], ct_ref)
    ct2, out2 = r["ct2"], r["out2"]
    ct_in = send(ct_ref.at[rows(1 - xp)], ct2.at[xp], x_peer)
    ct2[xp] = ct_ref[rows(xp), :]
    out2[xp] = outer_ref[...]
    outer_in = send(out2.at[xp], out2.at[xp], x_peer)
    a1[...] = jnp.zeros(a1.shape, BF)
    b2[...] = jnp.zeros(b2.shape, BF)
    loads["x"].wait()
    relay(r["x_in"], x_ref)

    def statistics(buf, position, targets, value):
        buf[position] = value
        return [send(buf.at[position], buf.at[position], t) for t in targets]

    def total(buf, copies):
        for copy in copies:
            copy.wait_recv()
        return jnp.sum(buf[...], axis=0)

    first = r["first"]

    def product(blocks, start):
        def body(h, carry):
            left = jnp.concatenate(
                [x_ref[rows(h), pl.ds(pl.multiple_of(o * RB, 128), RB)] for o in blocks], axis=1
            )
            right = jnp.concatenate([reduce_block(o)[...] for o in blocks], axis=0)
            part = dot(left, right)
            first[rows(h), :] = part if start else first[rows(h), :] + part
            return carry

        lax.fori_loop(0, 2, body, 0)

    if own_gather:
        for part in g_reduce:
            part.forward(0)
        twin_y(0, z)
        for rank in (1, 2):
            for part in g_reduce:
                part.forward(rank)
        product([zz * D + y for zz in range(H)], True)
        for rank in range(3):
            g_group.forward(rank)
        sources = [z]
        sources.append(g_expand.forward(0))
        twin(sources[1] * D + y)
        for number in range(4):
            for part in g_reduce:
                part.finish(number)
        for dy in range(1, D):
            product([zz * D + lax.rem(y + dy, D) for zz in range(H)], False)
    else:
        def body(h, carry):
            first[rows(h), :] = dot(x_ref[rows(h), :], wr[...])
            return carry

        lax.fori_loop(0, 2, body, 0)

    def moments(ref):
        def body(h, carry):
            v = ref[rows(h), :]
            return (
                carry[0] + jnp.sum(v, axis=0, keepdims=True) * valid(h),
                carry[1] + jnp.sum(v * v, axis=0, keepdims=True) * valid(h),
            )

        zero = jnp.zeros((1, ref.shape[1]), F32)
        return jnp.concatenate(lax.fori_loop(0, 2, body, (zero, zero)), axis=0)

    def average_and_inverse(sums):
        mean = sums[0:1] / pixels
        return mean, lax.rsqrt(sums[1:2] / pixels - mean * mean + NORM_EPS)

    stat1 = statistics(r["st1"], owner, family, moments(first))

    wall, wallt, gf = r["wall"], r["wallt"], r["gf"]
    if own_gather:
        g_expand.send_z(2)
        sources.append(g_expand.forward(1))
        twin(sources[2] * D + y)
        for number in range(4):
            g_group.finish(number)
        for o in range(HD):
            gf[o * GB : (o + 1) * GB, :] = wg[o].astype(F32)[0:GB]
    else:
        gf[...] = r["wg_full"][...].astype(F32)

    def spread(t, carry):
        piece = gf[pl.ds(pl.multiple_of(t * GROUP, 8), GROUP), :]
        full = jnp.where(block_diagonal, jnp.concatenate([piece] * (MID // GROUP), axis=0), 0.0)
        wall[pl.ds(pl.multiple_of(t * MID, 16), MID), :] = full.astype(BF)
        wallt[pl.ds(pl.multiple_of((8 - t) * MID, 16), MID), :] = full.T.astype(BF)
        return carry

    lax.fori_loop(0, 9, spread, 0)
    mean1, inv1 = average_and_inverse(total(r["st1"], stat1))
    gain1, shift1 = inner_ref[0:1, :], inner_ref[1:2, :]
    slope1 = r["slope1"]

    def activate(h):
        ok = valid(h)

        def body(w, carry):
            v = (first[tile(h, w), :] - mean1) * inv1
            v = v * gain1 + shift1
            q = jax.nn.sigmoid(v)
            a1[slab(h + 1, w + 1, N), :] = (v * q * ok).astype(BF)
            slope1[tile(h, w), :] = q * (1.0 + v * (1.0 - q)) * ok
            return carry

        lax.fori_loop(0, W, body, 0)

    class Halo:
        def __init__(self, ref):
            self.up = make(ref.at[slab(1, 1, R)], ref.at[slab(3, 1, R)], dev(H - 1, None, 0))
            self.down = make(ref.at[slab(2, 1, R)], ref.at[slab(0, 1, R)], dev(1, None, 0))

        def start_up(self):
            pl.when(z > 0)(self.up.start)

        def start_down(self):
            pl.when(z < H - 1)(self.down.start)

        def arrived(self):
            pl.when(z > 0)(self.down.wait_recv)
            pl.when(z < H - 1)(self.up.wait_recv)

        def sent(self):
            pl.when(z > 0)(self.up.wait_send)
            pl.when(z < H - 1)(self.down.wait_send)

    halo1, halo2 = Halo(a1), Halo(b2)
    activate(0)
    halo1.start_up()
    activate(1)
    halo1.start_down()

    def convolve(ref, weights, out, edge):
        def body(h, carry):
            if edge:
                hh, base, count = 3 * h, 6 * h, 1
            else:
                hh, base, count = 1, 3 * (1 - h), 2
            left = jnp.concatenate(
                [ref[slab(hh + i, kc, R), :] for i in range(count) for kc in range(3)], axis=1
            )
            part = dot(left, weights[pl.ds(pl.multiple_of(base * MID, 16), 3 * count * MID), :])
            out[rows(h), :] = out[rows(h), :] + part if edge else part
            return carry

        lax.fori_loop(0, 2, body, 0)

    second = r["second"]
    convolve(a1, wall, second, False)
    if own_gather:
        sources.append(g_expand.forward(2))
        twin(sources[3] * D + y)
        twin_y(1, sources[1])
        twin_y(2, sources[2])
    halo1.arrived()
    convolve(a1, wall, second, True)
    stat2 = statistics(r["st2"], owner, family, moments(second))
    mean2, inv2 = average_and_inverse(total(r["st2"], stat2))
    gain2, shift2 = inner_ref[2:3, :], inner_ref[3:4, :]
    a2, slope2 = r["a2"], r["slope2"]

    def activate_two(h):
        ok = valid(h)

        def body(w, carry):
            n = (second[tile(h, w), :] - mean2) * inv2
            second[tile(h, w), :] = n
            v = n * gain2 + shift2
            q = jax.nn.sigmoid(v)
            a2[tile(h, w), :] = (v * q * ok).astype(BF)
            slope2[tile(h, w), :] = q * (1.0 + v * (1.0 - q)) * ok
            return carry

        lax.fori_loop(0, W, body, 0)

    activate_two(1 - xp)
    ax_in = send(a2.at[rows(1 - xp)], r["ax"], x_peer)
    activate_two(xp)
    if own_gather:
        twin_y(3, sources[3])

    for copy in twin_in:
        copy.wait_recv()
    ax_in.wait_recv()
    third, tsend, trecv = r["third"], r["tsend"], r["trecv"]
    left = jnp.concatenate([a2[rows(xp), :], r["ax"][...]], axis=1)

    def expand(j, core):
        right = jnp.concatenate([we[:, quarter(j, core)], wep[:, quarter(j, core)]], axis=0)
        return dot(left, right)

    core_in = []
    for j in range(2):
        tsend[j] = expand(j, 1 - k).astype(BF)
        core_in.append(send(tsend.at[j], trecv.at[j], core_peer))
    for j in range(2):
        third[j] = expand(j, k)
    okx = valid(xp)
    sums = []
    for j in range(2):
        core_in[j].wait_recv()

        def body(w, carry):
            at = pl.ds(pl.multiple_of(w * N, 16), N)
            v = third[j, at, :] + trecv[j, at, :].astype(F32)
            third[j, at, :] = v
            return carry[0] + jnp.sum(v, axis=0, keepdims=True), carry[1] + jnp.sum(
                v * v, axis=0, keepdims=True
            )

        zero = jnp.zeros((1, OUT), F32)
        sums.append(lax.fori_loop(0, W, body, (zero, zero)))
    r["tx"][...] = third[1 - xp].astype(BF)
    position = xp * HD + owner
    both = family + twin_family
    stat3 = statistics(
        r["st3"],
        position,
        both,
        jnp.concatenate(
            [jnp.concatenate([s[i] for s in sums], axis=1) * okx for i in range(2)], axis=0
        ),
    )
    cut = (W + 1) // 2
    parts = [pl.ds(0, cut * N), pl.ds(cut * N, (W - cut) * N)]
    tx_in = [send(r["tx"].at[parts[0]], r["tother"].at[parts[0]], x_peer)]
    wrq = r["wrq"]

    def mids(chan):
        return pl.ds(pl.multiple_of(chan * MID, 128), MID)

    wrq[:, mids(c)] = wr[quarter(xp, k), :]
    wrq_in = [send(wr.at[quarter(xp, 1 - k), :], wrq.at[:, mids(c)], core_peer)]
    share = OUT // 2

    def send_wrq(n):
        target, core = ((x_peer, k), (diagonal, 1 - k))[n // 2]
        at = pl.ds(pl.multiple_of((2 * (1 - xp) + core) * OUT + n % 2 * share, 16), share)
        there = wrq.at[pl.ds(n % 2 * share, share), mids(c)]
        wrq_in.append(send(wr.at[at, :], there, target))

    a2t = r["a2t"]
    a2t[...] = a2[...].T
    ct_in.wait_recv()
    outer_in.wait_recv()
    mean3, inv3 = average_and_inverse(total(r["st3"], stat3))
    dpre, dother, bo = r["dpre"], r["dother"], r["bo"]
    mi3 = r["mi3"]
    for j in range(2):
        lanes = slice(j * OUT, (j + 1) * OUT)
        mi3[j] = jnp.concatenate([mean3[:, lanes], inv3[:, lanes]], axis=0)

    def outer_norm(j, h, values, grads, write, start=0, stop=W):
        m, iv = mi3[j, 0:1, :], mi3[j, 1:2, :]
        g, s = out2[j, 0:1, :], out2[j, 1:2, :]
        ok = valid(h)

        def body(w, carry):
            at = pl.ds(pl.multiple_of(w * N, 16), N)
            n = (values[0](at) - m) * iv
            values[1](at, n)
            v = n * g + s + x_ref[tile(h, w), quarter(j, k)].astype(F32)
            q = jax.nn.sigmoid(v)
            if write:
                bo[tile(h, w), :] = (v * q * ok).astype(BF)
            d = grads[0](at, w) * ok * (q * (1.0 + v * (1.0 - q)))
            grads[1](at, d)
            return carry[0] + jnp.sum(d, axis=0, keepdims=True), carry[1] + jnp.sum(
                d * n, axis=0, keepdims=True
            )

        zero = jnp.zeros((1, OUT), F32)
        return lax.fori_loop(start, stop, body, (zero, zero))

    def third_access(j):
        def get(at):
            return third[j, at, :]

        def put(at, n):
            third[j, at, :] = n

        def get_ct(at, w):
            return ct2[j, at, :].astype(F32)

        def put_d(at, d):
            dpre[j, at, :] = d

        return (get, put), (get_ct, put_d)

    st3b = r["st3b"]
    pair = r["pair"]
    for j, write in ((xp, True), (1 - xp, False)):
        pair[j] = jnp.concatenate(outer_norm(j, xp, *third_access(j), write), axis=0)
    stat3b = statistics(st3b, position, both, jnp.concatenate([pair[0], pair[1]], axis=1))

    tx_in.append(send(r["tx"].at[parts[1]], r["tother"].at[parts[1]], x_peer))
    send_wrq(0)
    tx_in[0].wait_recv()
    nother = r["nother"]

    def get_other(at):
        return r["tother"][at, :].astype(F32)

    def put_other(at, n):
        nother[at, :] = n

    def get_ct_other(at, w):
        return ct_ref[tile(1 - xp, w), :].astype(F32)

    def put_d_other(at, d):
        dother[at, :] = d

    other_row = ((get_other, put_other), (get_ct_other, put_d_other), True)
    outer_norm(xp, 1 - xp, *other_row, 0, cut)
    total3 = total(st3b, stat3b)
    r["tot3"][...] = total3
    for j in range(2):
        lanes = slice(j * OUT, (j + 1) * OUT)
        pair[j] = total3[:, lanes] / pixels
    piece = r["piece"]

    def back_three(j, h, upstream, normed):
        factor = out2[j, 0:1, :] * mi3[j, 1:2, :] * valid(h)
        sh, ga = pair[j, 0:1, :], pair[j, 1:2, :]

        def body(w, carry):
            at = pl.ds(pl.multiple_of(w * N, 16), N)
            v = factor * (upstream(at) - sh - normed(at) * ga)
            piece[tile(h, w), quarter(j, k)] = v.astype(BF)
            return carry

        lax.fori_loop(0, W, body, 0)
        part = piece.at[rows(h), quarter(j, k)]
        return send(part, part, core_peer)

    core_in = [
        back_three(j, xp, lambda at, j=j: dpre[j, at, :], lambda at, j=j: third[j, at, :])
        for j in range(2)
    ]
    for copy in core_in:
        copy.wait_recv()
    agrad = r["agrad"]
    r["agsend"][...] = dot_nt(piece[rows(xp), :], wep[...]).astype(BF)
    ag_in = send(r["agsend"], r["agrecv"], x_peer)
    part = piece.at[rows(xp), quarter(xp, k)]
    piece_in = send(part, part, x_peer)
    for n in range(1, 4):
        send_wrq(n)
    agrad[rows(xp), :] = dot_nt(piece[rows(xp), :], we[...])
    tx_in[1].wait_recv()
    outer_norm(xp, 1 - xp, *other_row, cut, W)
    core_other = back_three(xp, 1 - xp, lambda at: dother[at, :], lambda at: nother[at, :])

    class Scatter:
        def __init__(self, name, block, parts=1):
            self.block = block
            self.parts = parts
            self.ys, self.yr = r[name + "_ys"], r[name + "_yr"]
            self.zs, self.zr = r[name + "_zs"], r[name + "_zr"]
            self.own = r[name + "_own"]
            self.along_y, self.along_z = {}, []
            self.pair, self.cross = {}, {}
            self.base = used[0]
            used[0] += H * parts

        def start(self, targets):
            for slot, zi in targets:
                self.along_y[slot] = []
                for dy in range(1, D):
                    n = (dy - 1) * H * self.parts + slot
                    self.ys[n] = self.block(zi * D + lax.rem(y + dy, D), slot % self.parts).astype(BF)
                    self.along_y[slot].append(
                        (n, send(self.ys.at[n], self.yr.at[n], dev(0, None, dy)))
                    )

        def middle(self, targets):
            for slot, zi in targets:
                part = slot % self.parts
                value = self.block(zi * D + y, part)
                for n, copy in self.along_y[slot]:
                    copy.wait_recv()
                    value = value + self.yr[n].astype(F32)
                other = zi != z

                @pl.when(jnp.logical_not(other))
                def keep():
                    self.own[part] = value

                self.zs[slot] = value.astype(BF)
                target = {"height": zi, "chan": c, "dp": y}
                here = z * self.parts + part
                at = (self.base + slot, self.base + here)
                copy = make(self.zs.at[slot], self.zr.at[here], target, at)
                pl.when(other)(copy.start)
                self.along_z.append((other, copy))

        def fold(self, base, zone):
            far, kept = zone + 1 - lax.rem(z, 2), zone + lax.rem(z, 2)

            def received(zi):
                value = self.block(zi * D + y, 0)
                for dy in range(1, D):
                    value = value + self.yr[(dy - 1) * H + base + lax.rem(zi - zone + k, 2)].astype(F32)
                return value

            for slot in (base, base + 1):
                for n, copy in self.along_y[slot]:
                    copy.wait_recv()
            self.zs[base] = received(far).astype(BF)
            target = {"height": near[0], "chan": c, "dp": y}
            pair = send(self.zs.at[base], self.zr.at[base], target)

            def rest():
                value = received(kept)
                pair.wait_recv()
                value = value + self.zr[base].astype(F32)
                other = kept != z

                @pl.when(jnp.logical_not(other))
                def keep():
                    self.own[0] = value

                self.zs[base + 1] = value.astype(BF)
                target = {"height": lax.rem(z + 2, 4), "chan": c, "dp": y}
                at = (self.base, self.base)
                copy = make(self.zs.at[base + 1], self.zr.at[H], target, at)
                pl.when(other)(copy.start)
                self.along_z.append((other, copy))
                self.last = copy

            return rest

        def summed_y(self, slot, zi):
            part = slot % self.parts
            value = self.block(zi * D + y, part)
            for n, copy in self.along_y[slot]:
                copy.wait_recv()
                value = value + self.yr[n].astype(F32)
            return value

        def to_near(self, slot, zi):
            self.zs[slot] = self.summed_y(slot, zi).astype(BF)
            target = {"height": near[0], "chan": c, "dp": y}
            self.pair[slot] = send(self.zs.at[slot], self.zr.at[slot], target)

        def from_near(self, slot):
            self.pair[slot].wait_recv()
            return self.zr[slot].astype(F32)

        def across(self, slot, zi, pair):
            value = self.summed_y(slot, zi) + self.from_near(pair)
            self.zs[slot] = value.astype(BF)
            target = {"height": lax.rem(z + 2, 4), "chan": c, "dp": y}
            self.cross[slot] = send(self.zs.at[slot], self.zr.at[slot], target)

        def whole_sum(self, slot, zi, pair, cross):
            value = self.summed_y(slot, zi) + self.from_near(pair)
            self.cross[cross].wait_recv()
            return value + self.zr[cross].astype(F32)

        def finish_fold(self):
            self.last.wait_recv()
            return self.own[0] + self.zr[H].astype(F32)

        def finish(self, part=0):
            value = self.own[part]
            for dz in range(1, H):
                s = lax.rem(z + dz, H) * self.parts + part
                at = (self.base, self.base + s)
                make(self.zs.at[0], self.zr.at[s], dev(dz), at).wait_recv()
                value = value + self.zr[s].astype(F32)
            return value

        def sent(self):
            for other, copy in self.along_z:
                pl.when(other)(copy.wait_send)

    def wide(left_ref, right_ref, o, part, parts):
        share = left_ref.shape[0] // parts
        left = left_ref[part * share : (part + 1) * share, :]
        return dot(left, right_ref[:, pl.ds(pl.multiple_of(o * EB, 128), EB)])

    def slope_two(h, received, carry):
        def body(w, carry):
            if received:
                up = r["agrecv"][pl.ds(pl.multiple_of(w * N, 16), N), :].astype(F32)
            else:
                up = agrad[tile(h, w), :]
            d = up * slope2[tile(h, w), :]
            agrad[tile(h, w), :] = d
            return carry[0] + jnp.sum(d, axis=0, keepdims=True), carry[1] + jnp.sum(
                d * second[tile(h, w), :], axis=0, keepdims=True
            )

        return lax.fori_loop(0, W, body, carry)

    parity = lax.rem(z, 2)
    zones = (2 * xp, 2 * (1 - xp))
    early = [(0, zones[0] + k), (1, zones[0] + 1 - k)]
    late = [(2, zones[1] + k), (3, zones[1] + 1 - k)]
    around = [(0, lax.rem(z + 2, 4)), (1, 3 - z), (2, near[0]), (3, z)]
    if own_gather:
        s_expand = Scatter("eg", lambda o, part: wide(a2t, piece, o, part, 1))
        core_other.wait_recv()
        s_expand.start(early)
    zero = jnp.zeros((1, MID), F32)
    carry = slope_two(xp, False, (zero, zero))
    ag_in.wait_recv()
    carry = slope_two(1 - xp, True, carry)
    stat2b = statistics(r["st2b"], owner, family, jnp.concatenate(carry, axis=0))

    def turn(w, carry):
        r["turned"][:, w] = jnp.swapaxes(jnp.stack([bo[tile(h, w), :] for h in range(2)]), 0, 1)
        return carry

    lax.fori_loop(0, W, turn, 0)
    if own_gather:
        rest_early = s_expand.fold(0, zones[0])
    total2 = total(r["st2b"], stat2b)
    b2n = r["b2n"]

    def norm_two(h):
        factor = gain2 * inv2 * valid(h)
        sh, ga = total2[0:1] / pixels, total2[1:2] / pixels

        def body(w, carry):
            v = factor * (agrad[tile(h, w), :] - sh - second[tile(h, w), :] * ga)
            v = v.astype(BF)
            b2[slab(h + 1, w + 1, N), :] = v
            b2n[tile(h, w), :] = v
            return carry

        lax.fori_loop(0, W, body, 0)

    norm_two(0)
    halo2.start_up()
    norm_two(1)
    halo2.start_down()
    back1 = r["second_back"]
    convolve(b2, wallt, back1, False)
    b2t = r["b2t"]
    b2t[...] = b2n[...].T
    ggf = r["ggf"]
    fold = jnp.where(
        jnp.bitwise_and(lax.broadcasted_iota(jnp.int32, (GROUP, MID), 1), GROUP - 1)
        == lax.broadcasted_iota(jnp.int32, (GROUP, MID), 0),
        1.0,
        0.0,
    ).astype(BF)

    def group_grad(t, carry):
        kr, kc = lax.div(t, 3), lax.rem(t, 3)
        left = jnp.concatenate([a1[slab(kr, kc, R), :], a1[slab(kr + 1, kc, R), :]], axis=0)
        turned = jnp.where(block_diagonal, dot(b2t[...], left), 0.0).astype(BF)
        ggf[pl.ds(pl.multiple_of(t * GROUP, 8), GROUP), :] = dot_nt(fold, turned)
        return carry

    lax.fori_loop(0, 9, group_grad, 0)

    if own_gather:
        for o in range(HD):
            r["ggs"][o] = jnp.concatenate(
                [ggf[o * GB : (o + 1) * GB, :], jnp.zeros((SLOT - GB, MID), F32)], axis=0
            )
    piece_in.wait_recv()
    part = piece.at[rows(1 - xp), quarter(1 - xp, k)]
    core_last = send(part, part, core_peer)
    if own_gather:
        s_expand.start(late[:1])
    halo2.arrived()
    convolve(b2, wallt, back1, True)

    def slope_one(i, carry):
        h, w = lax.div(i, W), lax.rem(i, W)
        d = back1[tile(h, w), :] * slope1[tile(h, w), :]
        n = (first[tile(h, w), :] - mean1) * inv1
        first[tile(h, w), :] = n
        back1[tile(h, w), :] = d
        return carry[0] + jnp.sum(d, axis=0, keepdims=True), carry[1] + jnp.sum(
            d * n, axis=0, keepdims=True
        )

    carry = lax.fori_loop(0, 2 * W, slope_one, (zero, zero))
    stat1b = statistics(r["st1b"], owner, family, jnp.concatenate(carry, axis=0))

    core_last.wait_recv()
    if not own_gather:
        core_other.wait_recv()
    if own_gather:
        s_expand.start(late[1:])
        s_group = Scatter("gg", lambda o, part: r["ggs"][o])
        s_group.start(around)
    else:
        r["group_out"][...] = ggf[...].astype(BF)
        r["expand_out"][...] = dot(a2t[...], piece[...]).astype(BF)

    total1 = total(r["st1b"], stat1b)
    b1, ball = r["b1"], r["ball"]

    def norm_one(h):
        factor = gain1 * inv1 * valid(h)
        sh, ga = total1[0:1] / pixels, total1[1:2] / pixels

        def body(w, carry):
            v = factor * (back1[tile(h, w), :] - sh - first[tile(h, w), :] * ga)
            v = v.astype(BF)
            b1[tile(h, w), :] = v
            ball[tile(h, w), mids(c)] = v
            return carry

        lax.fori_loop(0, W, body, 0)

    ball_x, ball_core, ball_far = [], [], []
    for h in range(2):
        norm_one(h)
        part = ball.at[rows(h), mids(c)]
        ball_x.append(send(part, part, x_peer))
        ball_core.append(send(part, part, core_peer))

    def forward_ball(h):
        ball_x[h].wait_recv()
        part = ball.at[rows(h), mids(cx)]
        ball_far.append(send(part, part, core_peer))

    b1t = r["b1t"]
    b1t[...] = b1[...].T
    if own_gather:
        s_reduce = Scatter("rg", lambda o, part: wide(b1t, x_ref, o, part, 2), 2)
        here, there = z - parity, lax.rem(z - parity + 2, 4)
        ends = (there + 1 - parity, there + parity, here + 1 - parity, z)
        halves = [(2 * slot + part, zi) for slot, zi in enumerate(ends) for part in range(2)]
        s_reduce.start(halves)
        rest_early()
        rest_late = s_expand.fold(2, zones[1])
        s_group.middle(around)
        for half in halves[0:2]:
            s_reduce.to_near(*half)
        forward_ball(0)
        rest_late()
        for half in halves[2:4]:
            s_reduce.across(*half, half[0] - 2)
        forward_ball(1)
        for half in halves[4:6]:
            s_reduce.to_near(*half)
    else:
        forward_ball(0)
        forward_ball(1)
        r["reduce_out"][...] = dot(b1t[...], x_ref[...]).astype(BF)
    ig = r["ig"]

    def chip_mids(n):
        return pl.ds(pl.multiple_of(n * 2 * MID, 128), 2 * MID)

    r["inner_grad"][...] = jnp.concatenate(
        [total1[1:2], total1[0:1], total2[1:2], total2[0:1]], axis=0
    )
    mine = r["tot3"][:, pl.ds(pl.multiple_of(xp * OUT, 128), OUT)]
    r["outer_grad"][...] = jnp.concatenate([mine[1:2], mine[0:1]], axis=0)
    for copy in wrq_in:
        copy.wait_recv()
    ig[rows(xp), :] = dpre[xp]
    ig[rows(1 - xp), :] = dother[...]

    def input_part(h, n):
        ig[rows(h), :] = ig[rows(h), :] + dot_nt(ball[rows(h), chip_mids(n)], wrq[:, chip_mids(n)])

    for h in range(2):
        ball_core[h].wait_recv()
        input_part(h, xp)
    for h in range(2):
        ball_far[h].wait_recv()
        input_part(h, 1 - xp)
    if own_gather:
        r["group_out"][...] = s_group.finish()[0:GB]
        r["expand_out"][...] = s_expand.finish_fold()
        turned = jnp.concatenate(
            [s_reduce.whole_sum(*half, half[0] - 2, half[0] - 4) for half in halves[6:8]], axis=0
        )
        r["reduce_out"][...] = turned.T
        for scatter in (s_group, s_expand, s_reduce):
            scatter.sent()
    for copy in sends:
        copy.wait_send()
    halo1.sent()
    halo2.sent()


def adamw_step(master, gradient, moment_one, moment_two, average, rate):
    first_new = 0.5 * moment_one + 0.5 * gradient
    second_new = 0.5 * moment_two + 0.5 * gradient * gradient
    correct = 1.0 - 0.5**STEP
    direction = first_new / correct / (jnp.sqrt(second_new / correct) + 1e-08)
    master_new = master - rate * (direction + 0.05 * master)
    average_new = 0.75 * average + 0.25 * master_new
    return (first_new, second_new, master_new, average_new)


def last_kernel(*refs):
    ig_ref, bo_ref = refs[:2]
    ins, (bo_out, ig_out), outs = refs[2:27], refs[27:29], refs[29:57]
    turned, held, sems = refs[57], refs[58:-1], refs[-1]
    copies = []

    def put(source, target):
        copies.append(pltpu.make_async_copy(source, target, sems.at[len(copies)]))
        copies[-1].start()

    put(bo_ref, bo_out)
    number = 0
    for n in (0, 2, 1, 3, 4):
        gradient, master, one, two, average = (ref[...] for ref in ins[5 * n : 5 * n + 5])
        rate = CONV_RATE if n < 3 else NORM_RATE
        first, second, new, mean = adamw_step(master, gradient, one, two, average, rate)
        values = [first, second, new] + ([new.astype(BF)] if n < 3 else []) + [mean]
        number = 6 * n if n < 3 else 5 * n + 3
        put(ins[5 * n], outs[number])
        for at, value in enumerate(values, number + 1):
            held[at][...] = value
            put(held[at], outs[at])
    for w in range(turned.shape[1]):
        turned[:, w] = jnp.swapaxes(ig_ref[:, w], 0, 1)
        put(turned.at[:, w], ig_out.at[:, w])
    for copy in copies:
        copy.wait()


def local(
    inputs, cotangent,
    reduce_master, reduce_first, reduce_second, reduce_average,
    group_master, group_first, group_second, group_average,
    expand_master, expand_first, expand_second, expand_average,
    inner_master, inner_first, inner_second, inner_average,
    outer_master, outer_first, outer_second, outer_average,
):
    N, rows, W, CIN = inputs.shape
    OUT = cotangent.shape[3]
    MID = inner_master.shape[1]
    H, D = lax.axis_size("height"), lax.axis_size("dp")
    HD = H * D
    R = W * N
    GB = group_master.shape[0]
    RB, EB = reduce_master.shape[0], expand_master.shape[1]
    own_gather = RB % 128 == 0 and EB % 128 == 0
    dims = dict(H=H, D=D, N=N, W=W, MID=MID, OUT=OUT, CIN=CIN, own_gather=own_gather)

    shards = dict(x=inputs.transpose(0, 2, 1, 3), ct=cotangent.transpose(0, 2, 1, 3))
    shards.update(inner=inner_master, outer=outer_master)
    ins = {}
    outs = dict(
        turned=((N, W, rows, OUT), BF),
        ig=((rows * R, OUT), F32),
        inner_grad=(inner_master.shape, F32),
        outer_grad=(outer_master.shape, F32),
    )
    scratch = dict(
        x=((rows * R, CIN), BF),
        bo=((rows * R, OUT), BF),
        ct=((rows * R, OUT), BF),
        wep=((MID, CIN), BF),
        ct2=((2, R, OUT), BF),
        out2=((2, 2, OUT), F32),
        first=((2 * R, MID), F32),
        second=((2 * R, MID), F32),
        slope1=((2 * R, MID), F32),
        slope2=((2 * R, MID), F32),
        a1=((4 * (W + 2) * N, MID), BF),
        b2=((4 * (W + 2) * N, MID), BF),
        wall=((9 * MID, MID), BF),
        wallt=((9 * MID, MID), BF),
        gf=((9 * GROUP, MID), F32),
        ggf=((9 * GROUP, MID), F32),
        st1=((HD, 2, MID), F32),
        st2=((HD, 2, MID), F32),
        st3=((2 * HD, 2, 2 * OUT), F32),
        st3b=((2 * HD, 2, 2 * OUT), F32),
        st2b=((HD, 2, MID), F32),
        st1b=((HD, 2, MID), F32),
        tot3=((2, 2 * OUT), F32),
        a2=((2 * R, MID), BF),
        a2t=((MID, 2 * R), BF),
        ax=((R, MID), BF),
        third=((2, R, OUT), F32),
        tx=((R, OUT), BF),
        tother=((R, OUT), BF),
        nother=((R, OUT), F32),
        dother=((R, OUT), F32),
        mi3=((2, 2, OUT), F32),
        pair=((2, 2, OUT), F32),
        wrq=((OUT, 4 * MID), BF),
        ball=((2 * R, 4 * MID), BF),
        tsend=((2, R, OUT), BF),
        trecv=((2, R, OUT), BF),
        dpre=((2, R, OUT), F32),
        piece=((2 * R, CIN), BF),
        agrad=((2 * R, MID), F32),
        agsend=((R, MID), BF),
        agrecv=((R, MID), BF),
        b2n=((2 * R, MID), BF),
        b2t=((MID, 2 * R), BF),
        second_back=((2 * R, MID), F32),
        b1=((2 * R, MID), BF),
        b1t=((MID, 2 * R), BF),
    )
    if own_gather:
        shards.update(em=expand_master, gm=group_master, rm=reduce_master)
        outs.update(
            reduce_out=((RB, MID), F32), group_out=((GB, MID), F32), expand_out=((MID, EB), F32)
        )
        scratch.update(
            wr=((CIN, MID), BF), we=((MID, CIN), BF), wg=((HD, SLOT, MID), BF),
            ggs=((HD, SLOT, MID), F32),
        )
        for name, n, shape in (
            ("rg", 2, (MID // 2, RB)), ("eg", 1, (MID, EB)), ("gg", 1, (SLOT, MID))
        ):
            scratch[name + "_ys"] = scratch[name + "_yr"] = (((D - 1) * H * n, *shape), BF)
            scratch[name + "_zs"] = ((H * n, *shape), BF)
            scratch[name + "_zr"] = ((H * n + 1, *shape), BF)
            scratch[name + "_own"] = ((n, *shape), F32)
    else:
        both = ("height", "dp")
        ins.update(
            wr_full=lax.all_gather(reduce_master.astype(BF), both, axis=0, tiled=True),
            wg_full=lax.all_gather(group_master.astype(BF), both, axis=0, tiled=True),
            we_full=lax.all_gather(expand_master.astype(BF), both, axis=1, tiled=True),
        )
        outs.update(
            reduce_out=((MID, CIN), BF),
            group_out=((9 * GROUP, MID), BF),
            expand_out=((MID, CIN), BF),
        )
    dims["loads"] = list(shards)
    scratch.update({name + "_in": (a.shape, a.dtype) for name, a in shards.items()})
    names = [*(name + "_hbm" for name in shards), *ins, *outs, *scratch, "lsem", "ssem", "rsem"]
    whole = pl.BlockSpec(memory_space=pltpu.VMEM)
    results = pl.pallas_call(
        functools.partial(block_kernel, names, dims),
        out_shape=[pltpu.VMEM(*v) for v in outs.values()],
        in_specs=[pl.BlockSpec(memory_space=pltpu.HBM)] * len(shards) + [whole] * len(ins),
        out_specs=[whole] * len(outs),
        scratch_shapes=[pltpu.VMEM(*v) for v in scratch.values()]
        + [pltpu.SemaphoreType.DMA((len(shards),))]
        + [pltpu.SemaphoreType.DMA((dims.get("semaphores", SEMAPHORES + 16 * D),))] * 2,
        compiler_params=pltpu.CompilerParams(
            collective_id=0, has_side_effects=True, vmem_limit_bytes=48 << 20
        ),
        name="block",
    )(
        *(pltpu.with_memory_space_constraint(v, pltpu.HBM) for v in shards.values()),
        *(pltpu.with_memory_space_constraint(v, pltpu.VMEM) for v in ins.values()),
    )
    got = dict(zip(outs, results, strict=True))
    reduce_grad, group_grad, expand_grad = got["reduce_out"], got["group_out"], got["expand_out"]
    if not own_gather:
        both = ("height", "dp")
        reduce_grad = lax.psum_scatter(reduce_grad.T, both, scatter_dimension=0, tiled=True).astype(F32)
        group_grad = lax.psum_scatter(group_grad, both, scatter_dimension=0, tiled=True).astype(F32)
        expand_grad = lax.psum_scatter(expand_grad, both, scatter_dimension=1, tiled=True).astype(F32)
    groups = (
        (reduce_grad, reduce_master, reduce_first, reduce_second, reduce_average),
        (group_grad, group_master, group_first, group_second, group_average),
        (expand_grad, expand_master, expand_first, expand_second, expand_average),
        (got["inner_grad"], inner_master, inner_first, inner_second, inner_average),
        (got["outer_grad"], outer_master, outer_first, outer_second, outer_average),
    )
    shapes = [
        jax.ShapeDtypeStruct((N, W, rows, OUT), BF),
        jax.ShapeDtypeStruct((N, W, rows, OUT), F32),
    ]
    for n, group in enumerate(groups):
        kinds = [F32] * 4 + ([BF] if n < 3 else []) + [F32]
        shapes += [jax.ShapeDtypeStruct(group[0].shape, kind) for kind in kinds]
    flat = [got["ig"].reshape(rows, W, N, OUT), got["turned"]]
    flat += [a for group in groups for a in group]
    news = pl.pallas_call(
        last_kernel,
        out_shape=shapes,
        in_specs=[whole] * len(flat),
        out_specs=[pl.BlockSpec(memory_space=pltpu.HBM)] * len(shapes),
        scratch_shapes=[pltpu.VMEM((N, W, rows, OUT), F32)]
        + [pltpu.VMEM(a.shape, a.dtype) for a in shapes[2:]]
        + [pltpu.SemaphoreType.DMA((len(shapes) + W,))],
        compiler_params=pltpu.CompilerParams(vmem_limit_bytes=40 << 20),
        name="adamw",
    )(*flat)
    pixel_outs = (a.transpose(0, 2, 1, 3) for a in news[:2])
    return (*pixel_outs, *news[2:])


def solution(mesh):
    pixel = P("dp", "height", None, "chan")
    first = P(("height", "dp"), "chan")
    last = P("chan", ("height", "dp"))
    table = P(None, "chan")
    return jax.shard_map(
        local,
        mesh=mesh,
        in_specs=(P("dp", "height", None, None), pixel)
        + (first,) * 8
        + (last,) * 4
        + (table,) * 8,
        out_specs=(pixel, pixel) + (first,) * 12 + (last,) * 6 + (table,) * 10,
        check_vma=False,
    )
```

```python
import functools

import jax
import jax.numpy as jnp
from jax import lax
from jax.experimental import pallas as pl
from jax.experimental.pallas import tpu as pltpu
from jax.sharding import PartitionSpec as P

GROUP = 32
HEIGHT = 7
STEP = 10
NORM_EPS = 1e-05
CONV_RATE = 0.02
NORM_RATE = 0.3

BF = jnp.bfloat16
F32 = jnp.float32
MESH = pl.DeviceIdType.MESH
SEMAPHORES = 192
SLOT = 48


def dot(a, b):
    return jnp.dot(a, b, preferred_element_type=F32)


def dot_nt(a, b):
    return lax.dot_general(a, b, (((1,), (1,)), ((), ())), preferred_element_type=F32)


def block_kernel(names, dims, *refs):
    r = dict(zip(names, refs, strict=True))
    H, D, N, W, MID, OUT, CIN = (dims[k] for k in ("H", "D", "N", "W", "MID", "OUT", "CIN"))
    own_gather = dims["own_gather"]
    R = W * N
    PITCH = (W + 2) * N
    HD = H * D
    pixels = float(N * D * HEIGHT * W)
    x_ref, ct_ref, inner_ref, outer_ref = r["x"], r["ct"], r["inner_in"], r["outer_in"]
    loads = {
        name: pltpu.make_async_copy(r[name + "_hbm"], r[name + "_in"], r["lsem"].at[i])
        for i, name in enumerate(dims["loads"])
    }
    for name in reversed(dims["loads"]):
        loads[name].start()

    z = lax.axis_index("height")
    c = lax.axis_index("chan")
    y = lax.axis_index("dp")
    xp = lax.div(c, 2)
    k = lax.rem(c, 2)
    cx = lax.rem(c + 2, 4)
    cc = c + 1 - 2 * k
    owner = z * D + y

    def dev(dz=0, chan=None, dy=0):
        return {
            "height": lax.rem(z + dz, H),
            "chan": c if chan is None else chan,
            "dp": lax.rem(y + dy, D),
        }

    offsets = [(dz, dy) for dz in range(H) for dy in range(D)]
    family = [dev(dz, None, dy) for dz, dy in offsets if dz or dy]
    twin_family = [dev(dz, cx, dy) for dz, dy in offsets]
    core_peer = dev(0, cc, 0)
    x_peer = dev(0, cx, 0)
    diagonal = dev(0, cx + 1 - 2 * k, 0)

    def rows(h):
        return pl.ds(pl.multiple_of(h * R, 16), R)

    def tile(h, w):
        return pl.ds(pl.multiple_of(h * R + w * N, 16), N)

    def slab(hh, ww, count):
        return pl.ds(pl.multiple_of((hh * (W + 2) + ww) * N, 16), count)

    def quarter(j, core):
        return pl.ds(pl.multiple_of((2 * j + core) * OUT, 128), OUT)

    def valid(h):
        return jnp.where(z * 2 + h < HEIGHT, 1.0, 0.0).astype(F32)

    sends = []
    used = [0]

    def make(src, dst, target, at=None):
        if at is None:
            at = (used[0], used[0])
            used[0] += 1
        return pltpu.make_async_remote_copy(
            src_ref=src,
            dst_ref=dst,
            send_sem=r["ssem"].at[at[0]],
            recv_sem=r["rsem"].at[at[1]],
            device_id=target,
            device_id_type=MESH,
        )

    def send(src, dst, target):
        copy = make(src, dst, target)
        copy.start()
        sends.append(copy)
        return copy

    barrier = pltpu.get_barrier_semaphore()
    everyone = family + twin_family + [core_peer, diagonal]
    for target in everyone:
        pl.semaphore_signal(barrier, inc=1, device_id=target, device_id_type=MESH)
    a1, b2 = r["a1"], r["b2"]
    lane_group = lax.shift_right_logical(lax.broadcasted_iota(jnp.int32, (MID, MID), 1), 5)
    row_group = lax.shift_right_logical(lax.broadcasted_iota(jnp.int32, (MID, MID), 0), 5)
    block_diagonal = lane_group == row_group
    if own_gather:
        wr, we, wg = r["wr"], r["we"], r["wg"]
        RB, EB = r["rm_in"].shape[0], r["em_in"].shape[1]
        GB = r["gm_in"].shape[0]

        def reduce_block(o):
            return wr.at[pl.ds(pl.multiple_of(o * RB, 16), RB), :]

        def expand_block(o):
            return we.at[:, pl.ds(pl.multiple_of(o * EB, 128), EB)]

        def group_block(o):
            return wg.at[o]

        loads["rm"].wait()
        reduce_block(owner)[...] = r["rm_in"][...].astype(BF)
    else:
        wr, we = r["wr_full"], r["we_full"]

    pl.semaphore_wait(barrier, len(everyone))

    near = [z + 1 - 2 * lax.rem(z, 2), jnp.where(z < 2, 2, 1), jnp.where(z < 2, 3, 0)]

    class Gather:
        def __init__(self, block):
            self.block = block
            self.here = block(owner)
            self.base = used[0]
            used[0] += H
            self.along_y = []

        def send_z(self, rank):
            target = {"height": near[rank], "chan": c, "dp": y}
            copy = make(self.here, self.here, target, (self.base + rank, self.base + z))
            copy.start()
            sends.append(copy)

        def send_y(self):
            self.pass_on(self.here)

        def pass_on(self, block):
            self.along_y.append([send(block, block, dev(0, None, dy)) for dy in range(1, D)])

        def forward(self, rank):
            source = near[rank]
            block = self.block(source * D + y)
            make(block, block, dev(), (self.base, self.base + source)).wait_recv()
            self.pass_on(block)
            return source

        def finish(self, number):
            for copy in self.along_y[number]:
                copy.wait_recv()

    if own_gather:
        def reduce_part(n):
            return lambda o: wr.at[pl.ds(pl.multiple_of(o * RB + n * (RB // 2), 16), RB // 2), :]

        g_reduce = [Gather(reduce_part(n)) for n in range(2)]
        g_group, g_expand = Gather(group_block), Gather(expand_block)
        for rank in range(3):
            for part in g_reduce:
                part.send_z(rank)
        for part in g_reduce:
            part.send_y()
        for name in ("gm", "em"):
            loads[name].wait()
        wg[owner] = jnp.concatenate(
            [r["gm_in"][...], jnp.zeros((SLOT - GB, MID), F32)], axis=0
        ).astype(BF)
        expand_block(owner)[...] = r["em_in"][...].astype(BF)
        for rank in range(3):
            g_group.send_z(rank)
        g_group.send_y()
    wep = r["wep"]
    twin_in = []

    def twin(o):
        twin_in.append(
            send(expand_block(o), wep.at[:, pl.ds(pl.multiple_of(o * EB, 128), EB)], x_peer)
        )

    def twin_y(number, zz):
        g_expand.finish(number)
        for dy in range(1, D):
            twin(zz * D + lax.rem(y + dy, D))

    if own_gather:
        g_expand.send_z(0)
        g_expand.send_z(1)
        g_expand.send_y()
        twin(owner)
    else:
        twin_in.append(send(we, wep, x_peer))

    def relay(source, target):
        def body(w, carry):
            turned = jnp.swapaxes(source[:, w], 0, 1)
            for h in range(2):
                target[tile(h, w), :] = turned[h]
            return carry

        lax.fori_loop(0, W, body, 0)

    loads["inner"].wait()
    loads["outer"].wait()
    loads["ct"].wait()
    relay(r["ct_in"], ct_ref)
    ct2, out2 = r["ct2"], r["out2"]
    ct_in = send(ct_ref.at[rows(1 - xp)], ct2.at[xp], x_peer)
    ct2[xp] = ct_ref[rows(xp), :]
    out2[xp] = outer_ref[...]
    outer_in = send(out2.at[xp], out2.at[xp], x_peer)
    a1[...] = jnp.zeros(a1.shape, BF)
    b2[...] = jnp.zeros(b2.shape, BF)
    loads["x"].wait()
    relay(r["x_in"], x_ref)

    def statistics(buf, position, targets, value):
        buf[position] = value
        return [send(buf.at[position], buf.at[position], t) for t in targets]

    def total(buf, copies):
        for copy in copies:
            copy.wait_recv()
        return jnp.sum(buf[...], axis=0)

    first = r["first"]

    def product(blocks, start):
        def body(h, carry):
            left = jnp.concatenate(
                [x_ref[rows(h), pl.ds(pl.multiple_of(o * RB, 128), RB)] for o in blocks], axis=1
            )
            right = jnp.concatenate([reduce_block(o)[...] for o in blocks], axis=0)
            part = dot(left, right)
            first[rows(h), :] = part if start else first[rows(h), :] + part
            return carry

        lax.fori_loop(0, 2, body, 0)

    if own_gather:
        for part in g_reduce:
            part.forward(0)
        twin_y(0, z)
        for rank in (1, 2):
            for part in g_reduce:
                part.forward(rank)
        product([zz * D + y for zz in range(H)], True)
        for rank in range(3):
            g_group.forward(rank)
        sources = [z]
        sources.append(g_expand.forward(0))
        twin(sources[1] * D + y)
        for number in range(4):
            for part in g_reduce:
                part.finish(number)
        for dy in range(1, D):
            product([zz * D + lax.rem(y + dy, D) for zz in range(H)], False)
    else:
        def body(h, carry):
            first[rows(h), :] = dot(x_ref[rows(h), :], wr[...])
            return carry

        lax.fori_loop(0, 2, body, 0)

    def moments(ref):
        def body(h, carry):
            v = ref[rows(h), :]
            return (
                carry[0] + jnp.sum(v, axis=0, keepdims=True) * valid(h),
                carry[1] + jnp.sum(v * v, axis=0, keepdims=True) * valid(h),
            )

        zero = jnp.zeros((1, ref.shape[1]), F32)
        return jnp.concatenate(lax.fori_loop(0, 2, body, (zero, zero)), axis=0)

    def average_and_inverse(sums):
        mean = sums[0:1] / pixels
        return mean, lax.rsqrt(sums[1:2] / pixels - mean * mean + NORM_EPS)

    stat1 = statistics(r["st1"], owner, family, moments(first))

    wall, wallt, gf = r["wall"], r["wallt"], r["gf"]
    if own_gather:
        g_expand.send_z(2)
        sources.append(g_expand.forward(1))
        twin(sources[2] * D + y)
        for number in range(4):
            g_group.finish(number)
        for o in range(HD):
            gf[o * GB : (o + 1) * GB, :] = wg[o].astype(F32)[0:GB]
    else:
        gf[...] = r["wg_full"][...].astype(F32)

    def spread(t, carry):
        piece = gf[pl.ds(pl.multiple_of(t * GROUP, 8), GROUP), :]
        full = jnp.where(block_diagonal, jnp.concatenate([piece] * (MID // GROUP), axis=0), 0.0)
        wall[pl.ds(pl.multiple_of(t * MID, 16), MID), :] = full.astype(BF)
        wallt[pl.ds(pl.multiple_of((8 - t) * MID, 16), MID), :] = full.T.astype(BF)
        return carry

    lax.fori_loop(0, 9, spread, 0)
    mean1, inv1 = average_and_inverse(total(r["st1"], stat1))
    gain1, shift1 = inner_ref[0:1, :], inner_ref[1:2, :]
    slope1 = r["slope1"]

    def activate(h):
        ok = valid(h)

        def body(w, carry):
            v = (first[tile(h, w), :] - mean1) * inv1
            v = v * gain1 + shift1
            q = jax.nn.sigmoid(v)
            a1[slab(h + 1, w + 1, N), :] = (v * q * ok).astype(BF)
            slope1[tile(h, w), :] = q * (1.0 + v * (1.0 - q)) * ok
            return carry

        lax.fori_loop(0, W, body, 0)

    class Halo:
        def __init__(self, ref):
            self.up = make(ref.at[slab(1, 1, R)], ref.at[slab(3, 1, R)], dev(H - 1, None, 0))
            self.down = make(ref.at[slab(2, 1, R)], ref.at[slab(0, 1, R)], dev(1, None, 0))

        def start_up(self):
            pl.when(z > 0)(self.up.start)

        def start_down(self):
            pl.when(z < H - 1)(self.down.start)

        def arrived(self):
            pl.when(z > 0)(self.down.wait_recv)
            pl.when(z < H - 1)(self.up.wait_recv)

        def sent(self):
            pl.when(z > 0)(self.up.wait_send)
            pl.when(z < H - 1)(self.down.wait_send)

    halo1, halo2 = Halo(a1), Halo(b2)
    activate(0)
    halo1.start_up()
    activate(1)
    halo1.start_down()

    def convolve(ref, weights, out, edge):
        def body(h, carry):
            if edge:
                hh, base, count = 3 * h, 6 * h, 1
            else:
                hh, base, count = 1, 3 * (1 - h), 2
            left = jnp.concatenate(
                [ref[slab(hh + i, kc, R), :] for i in range(count) for kc in range(3)], axis=1
            )
            part = dot(left, weights[pl.ds(pl.multiple_of(base * MID, 16), 3 * count * MID), :])
            out[rows(h), :] = out[rows(h), :] + part if edge else part
            return carry

        lax.fori_loop(0, 2, body, 0)

    second = r["second"]
    convolve(a1, wall, second, False)
    if own_gather:
        sources.append(g_expand.forward(2))
        twin(sources[3] * D + y)
        twin_y(1, sources[1])
        twin_y(2, sources[2])
    halo1.arrived()
    convolve(a1, wall, second, True)
    stat2 = statistics(r["st2"], owner, family, moments(second))
    mean2, inv2 = average_and_inverse(total(r["st2"], stat2))
    gain2, shift2 = inner_ref[2:3, :], inner_ref[3:4, :]
    a2, slope2 = r["a2"], r["slope2"]

    def activate_two(h):
        ok = valid(h)

        def body(w, carry):
            n = (second[tile(h, w), :] - mean2) * inv2
            second[tile(h, w), :] = n
            v = n * gain2 + shift2
            q = jax.nn.sigmoid(v)
            a2[tile(h, w), :] = (v * q * ok).astype(BF)
            slope2[tile(h, w), :] = q * (1.0 + v * (1.0 - q)) * ok
            return carry

        lax.fori_loop(0, W, body, 0)

    activate_two(1 - xp)
    ax_in = send(a2.at[rows(1 - xp)], r["ax"], x_peer)
    activate_two(xp)
    if own_gather:
        twin_y(3, sources[3])

    for copy in twin_in:
        copy.wait_recv()
    ax_in.wait_recv()
    third, tsend, trecv = r["third"], r["tsend"], r["trecv"]
    left = jnp.concatenate([a2[rows(xp), :], r["ax"][...]], axis=1)

    def expand(j, core):
        right = jnp.concatenate([we[:, quarter(j, core)], wep[:, quarter(j, core)]], axis=0)
        return dot(left, right)

    core_in = []
    for j in range(2):
        tsend[j] = expand(j, 1 - k).astype(BF)
        core_in.append(send(tsend.at[j], trecv.at[j], core_peer))
    for j in range(2):
        third[j] = expand(j, k)
    okx = valid(xp)
    sums = []
    for j in range(2):
        core_in[j].wait_recv()

        def body(w, carry):
            at = pl.ds(pl.multiple_of(w * N, 16), N)
            v = third[j, at, :] + trecv[j, at, :].astype(F32)
            third[j, at, :] = v
            return carry[0] + jnp.sum(v, axis=0, keepdims=True), carry[1] + jnp.sum(
                v * v, axis=0, keepdims=True
            )

        zero = jnp.zeros((1, OUT), F32)
        sums.append(lax.fori_loop(0, W, body, (zero, zero)))
    r["tx"][...] = third[1 - xp].astype(BF)
    position = xp * HD + owner
    both = twin_family + family
    stat3 = statistics(
        r["st3"],
        position,
        both,
        jnp.concatenate(
            [jnp.concatenate([s[i] for s in sums], axis=1) * okx for i in range(2)], axis=0
        ),
    )
    cut = (W + 1) // 2
    parts = [pl.ds(0, cut * N), pl.ds(cut * N, (W - cut) * N)]
    tx_in = [send(r["tx"].at[parts[0]], r["tother"].at[parts[0]], x_peer)]
    wrq = r["wrq"]

    def mids(chan):
        return pl.ds(pl.multiple_of(chan * MID, 128), MID)

    wrq[:, mids(c)] = wr[quarter(xp, k), :]
    wrq_in = [send(wr.at[quarter(xp, 1 - k), :], wrq.at[:, mids(c)], core_peer)]
    share = OUT // 2

    def send_wrq(n):
        target, core = ((x_peer, k), (diagonal, 1 - k))[n // 2]
        at = pl.ds(pl.multiple_of((2 * (1 - xp) + core) * OUT + n % 2 * share, 16), share)
        there = wrq.at[pl.ds(n % 2 * share, share), mids(c)]
        wrq_in.append(send(wr.at[at, :], there, target))

    a2t = r["a2t"]
    a2t[...] = a2[...].T
    ct_in.wait_recv()
    outer_in.wait_recv()
    mean3, inv3 = average_and_inverse(total(r["st3"], stat3))
    dpre, dother, bo = r["dpre"], r["dother"], r["bo"]
    mi3 = r["mi3"]
    for j in range(2):
        lanes = slice(j * OUT, (j + 1) * OUT)
        mi3[j] = jnp.concatenate([mean3[:, lanes], inv3[:, lanes]], axis=0)

    def outer_norm(j, h, values, grads, write, start=0, stop=W):
        m, iv = mi3[j, 0:1, :], mi3[j, 1:2, :]
        g, s = out2[j, 0:1, :], out2[j, 1:2, :]
        ok = valid(h)

        def body(w, carry):
            at = pl.ds(pl.multiple_of(w * N, 16), N)
            n = (values[0](at) - m) * iv
            values[1](at, n)
            v = n * g + s + x_ref[tile(h, w), quarter(j, k)].astype(F32)
            q = jax.nn.sigmoid(v)
            if write:
                bo[tile(h, w), :] = (v * q * ok).astype(BF)
            d = grads[0](at, w) * ok * (q * (1.0 + v * (1.0 - q)))
            grads[1](at, d)
            return carry[0] + jnp.sum(d, axis=0, keepdims=True), carry[1] + jnp.sum(
                d * n, axis=0, keepdims=True
            )

        zero = jnp.zeros((1, OUT), F32)
        return lax.fori_loop(start, stop, body, (zero, zero))

    def third_access(j):
        def get(at):
            return third[j, at, :]

        def put(at, n):
            third[j, at, :] = n

        def get_ct(at, w):
            return ct2[j, at, :].astype(F32)

        def put_d(at, d):
            dpre[j, at, :] = d

        return (get, put), (get_ct, put_d)

    st3b = r["st3b"]
    pair = r["pair"]
    for j, write in ((xp, True), (1 - xp, False)):
        pair[j] = jnp.concatenate(outer_norm(j, xp, *third_access(j), write), axis=0)
    stat3b = statistics(st3b, position, both, jnp.concatenate([pair[0], pair[1]], axis=1))

    tx_in.append(send(r["tx"].at[parts[1]], r["tother"].at[parts[1]], x_peer))
    send_wrq(0)
    tx_in[0].wait_recv()
    nother = r["nother"]

    def get_other(at):
        return r["tother"][at, :].astype(F32)

    def put_other(at, n):
        nother[at, :] = n

    def get_ct_other(at, w):
        return ct_ref[tile(1 - xp, w), :].astype(F32)

    def put_d_other(at, d):
        dother[at, :] = d

    other_row = ((get_other, put_other), (get_ct_other, put_d_other), True)
    outer_norm(xp, 1 - xp, *other_row, 0, cut)
    total3 = total(st3b, stat3b)
    r["tot3"][...] = total3
    for j in range(2):
        lanes = slice(j * OUT, (j + 1) * OUT)
        pair[j] = total3[:, lanes] / pixels
    piece = r["piece"]

    def back_three(j, h, upstream, normed):
        factor = out2[j, 0:1, :] * mi3[j, 1:2, :] * valid(h)
        sh, ga = pair[j, 0:1, :], pair[j, 1:2, :]

        def body(w, carry):
            at = pl.ds(pl.multiple_of(w * N, 16), N)
            v = factor * (upstream(at) - sh - normed(at) * ga)
            piece[tile(h, w), quarter(j, k)] = v.astype(BF)
            return carry

        lax.fori_loop(0, W, body, 0)
        part = piece.at[rows(h), quarter(j, k)]
        return send(part, part, core_peer)

    core_in = [
        back_three(j, xp, lambda at, j=j: dpre[j, at, :], lambda at, j=j: third[j, at, :])
        for j in range(2)
    ]
    for copy in core_in:
        copy.wait_recv()
    agrad = r["agrad"]
    r["agsend"][...] = dot_nt(piece[rows(xp), :], wep[...]).astype(BF)
    ag_in = send(r["agsend"], r["agrecv"], x_peer)
    part = piece.at[rows(xp), quarter(xp, k)]
    piece_in = send(part, part, x_peer)
    for n in range(1, 4):
        send_wrq(n)
    agrad[rows(xp), :] = dot_nt(piece[rows(xp), :], we[...])
    tx_in[1].wait_recv()
    outer_norm(xp, 1 - xp, *other_row, cut, W)
    core_other = back_three(xp, 1 - xp, lambda at: dother[at, :], lambda at: nother[at, :])

    class Scatter:
        def __init__(self, name, block, parts=1):
            self.block = block
            self.parts = parts
            self.ys, self.yr = r[name + "_ys"], r[name + "_yr"]
            self.zs, self.zr = r[name + "_zs"], r[name + "_zr"]
            self.own = r[name + "_own"]
            self.along_y, self.along_z = {}, []
            self.pair, self.cross = {}, {}
            self.base = used[0]
            used[0] += H * parts

        def start(self, targets):
            for slot, zi in targets:
                self.along_y[slot] = []
                for dy in range(1, D):
                    n = (dy - 1) * H * self.parts + slot
                    self.ys[n] = self.block(zi * D + lax.rem(y + dy, D), slot % self.parts).astype(BF)
                    self.along_y[slot].append(
                        (n, send(self.ys.at[n], self.yr.at[n], dev(0, None, dy)))
                    )

        def middle(self, targets):
            for slot, zi in targets:
                part = slot % self.parts
                value = self.block(zi * D + y, part)
                for n, copy in self.along_y[slot]:
                    copy.wait_recv()
                    value = value + self.yr[n].astype(F32)
                other = zi != z

                @pl.when(jnp.logical_not(other))
                def keep():
                    self.own[part] = value

                self.zs[slot] = value.astype(BF)
                target = {"height": zi, "chan": c, "dp": y}
                here = z * self.parts + part
                at = (self.base + slot, self.base + here)
                copy = make(self.zs.at[slot], self.zr.at[here], target, at)
                pl.when(other)(copy.start)
                self.along_z.append((other, copy))

        def fold(self, base, zone):
            far, kept = zone + 1 - lax.rem(z, 2), zone + lax.rem(z, 2)

            def received(zi):
                value = self.block(zi * D + y, 0)
                for dy in range(1, D):
                    value = value + self.yr[(dy - 1) * H + base + lax.rem(zi - zone + k, 2)].astype(F32)
                return value

            for slot in (base, base + 1):
                for n, copy in self.along_y[slot]:
                    copy.wait_recv()
            self.zs[base] = received(far).astype(BF)
            target = {"height": near[0], "chan": c, "dp": y}
            pair = send(self.zs.at[base], self.zr.at[base], target)

            def rest():
                value = received(kept)
                pair.wait_recv()
                value = value + self.zr[base].astype(F32)
                other = kept != z

                @pl.when(jnp.logical_not(other))
                def keep():
                    self.own[0] = value

                self.zs[base + 1] = value.astype(BF)
                target = {"height": lax.rem(z + 2, 4), "chan": c, "dp": y}
                at = (self.base, self.base)
                copy = make(self.zs.at[base + 1], self.zr.at[H], target, at)
                pl.when(other)(copy.start)
                self.along_z.append((other, copy))
                self.last = copy

            return rest

        def summed_y(self, slot, zi):
            part = slot % self.parts
            value = self.block(zi * D + y, part)
            for n, copy in self.along_y[slot]:
                copy.wait_recv()
                value = value + self.yr[n].astype(F32)
            return value

        def to_near(self, slot, zi):
            self.zs[slot] = self.summed_y(slot, zi).astype(BF)
            target = {"height": near[0], "chan": c, "dp": y}
            self.pair[slot] = send(self.zs.at[slot], self.zr.at[slot], target)

        def from_near(self, slot):
            self.pair[slot].wait_recv()
            return self.zr[slot].astype(F32)

        def across(self, slot, zi, pair):
            value = self.summed_y(slot, zi) + self.from_near(pair)
            self.zs[slot] = value.astype(BF)
            target = {"height": lax.rem(z + 2, 4), "chan": c, "dp": y}
            self.cross[slot] = send(self.zs.at[slot], self.zr.at[slot], target)

        def whole_sum(self, slot, zi, pair, cross):
            value = self.summed_y(slot, zi) + self.from_near(pair)
            self.cross[cross].wait_recv()
            return value + self.zr[cross].astype(F32)

        def finish_fold(self):
            self.last.wait_recv()
            return self.own[0] + self.zr[H].astype(F32)

        def finish(self, part=0):
            value = self.own[part]
            for dz in range(1, H):
                s = lax.rem(z + dz, H) * self.parts + part
                at = (self.base, self.base + s)
                make(self.zs.at[0], self.zr.at[s], dev(dz), at).wait_recv()
                value = value + self.zr[s].astype(F32)
            return value

        def sent(self):
            for other, copy in self.along_z:
                pl.when(other)(copy.wait_send)

    def wide(left_ref, right_ref, o, part, parts):
        share = left_ref.shape[0] // parts
        left = left_ref[part * share : (part + 1) * share, :]
        return dot(left, right_ref[:, pl.ds(pl.multiple_of(o * EB, 128), EB)])

    def slope_two(h, received, carry):
        def body(w, carry):
            if received:
                up = r["agrecv"][pl.ds(pl.multiple_of(w * N, 16), N), :].astype(F32)
            else:
                up = agrad[tile(h, w), :]
            d = up * slope2[tile(h, w), :]
            agrad[tile(h, w), :] = d
            return carry[0] + jnp.sum(d, axis=0, keepdims=True), carry[1] + jnp.sum(
                d * second[tile(h, w), :], axis=0, keepdims=True
            )

        return lax.fori_loop(0, W, body, carry)

    parity = lax.rem(z, 2)
    zones = (2 * xp, 2 * (1 - xp))
    early = [(0, zones[0] + k), (1, zones[0] + 1 - k)]
    late = [(2, zones[1] + k), (3, zones[1] + 1 - k)]
    around = [(0, lax.rem(z + 2, 4)), (1, 3 - z), (2, near[0]), (3, z)]
    if own_gather:
        s_expand = Scatter("eg", lambda o, part: wide(a2t, piece, o, part, 1))
        core_other.wait_recv()
        s_expand.start(early)
    zero = jnp.zeros((1, MID), F32)
    carry = slope_two(xp, False, (zero, zero))
    ag_in.wait_recv()
    carry = slope_two(1 - xp, True, carry)
    stat2b = statistics(r["st2b"], owner, family, jnp.concatenate(carry, axis=0))

    def turn(w, carry):
        r["turned"][:, w] = jnp.swapaxes(jnp.stack([bo[tile(h, w), :] for h in range(2)]), 0, 1)
        return carry

    lax.fori_loop(0, W, turn, 0)
    if own_gather:
        rest_early = s_expand.fold(0, zones[0])
    total2 = total(r["st2b"], stat2b)
    b2n = r["b2n"]

    def norm_two(h):
        factor = gain2 * inv2 * valid(h)
        sh, ga = total2[0:1] / pixels, total2[1:2] / pixels

        def body(w, carry):
            v = factor * (agrad[tile(h, w), :] - sh - second[tile(h, w), :] * ga)
            v = v.astype(BF)
            b2[slab(h + 1, w + 1, N), :] = v
            b2n[tile(h, w), :] = v
            return carry

        lax.fori_loop(0, W, body, 0)

    norm_two(0)
    halo2.start_up()
    norm_two(1)
    halo2.start_down()
    back1 = r["second_back"]
    convolve(b2, wallt, back1, False)
    b2t = r["b2t"]
    b2t[...] = b2n[...].T
    ggf = r["ggf"]
    fold = jnp.where(
        jnp.bitwise_and(lax.broadcasted_iota(jnp.int32, (GROUP, MID), 1), GROUP - 1)
        == lax.broadcasted_iota(jnp.int32, (GROUP, MID), 0),
        1.0,
        0.0,
    ).astype(BF)

    def group_grad(t, carry):
        kr, kc = lax.div(t, 3), lax.rem(t, 3)
        left = jnp.concatenate([a1[slab(kr, kc, R), :], a1[slab(kr + 1, kc, R), :]], axis=0)
        turned = jnp.where(block_diagonal, dot(b2t[...], left), 0.0).astype(BF)
        ggf[pl.ds(pl.multiple_of(t * GROUP, 8), GROUP), :] = dot_nt(fold, turned)
        return carry

    lax.fori_loop(0, 9, group_grad, 0)

    if own_gather:
        for o in range(HD):
            r["ggs"][o] = jnp.concatenate(
                [ggf[o * GB : (o + 1) * GB, :], jnp.zeros((SLOT - GB, MID), F32)], axis=0
            )
    piece_in.wait_recv()
    part = piece.at[rows(1 - xp), quarter(1 - xp, k)]
    core_last = send(part, part, core_peer)
    if own_gather:
        s_expand.start(late[:1])
    halo2.arrived()
    convolve(b2, wallt, back1, True)

    def slope_one(i, carry):
        h, w = lax.div(i, W), lax.rem(i, W)
        d = back1[tile(h, w), :] * slope1[tile(h, w), :]
        n = (first[tile(h, w), :] - mean1) * inv1
        first[tile(h, w), :] = n
        back1[tile(h, w), :] = d
        return carry[0] + jnp.sum(d, axis=0, keepdims=True), carry[1] + jnp.sum(
            d * n, axis=0, keepdims=True
        )

    carry = lax.fori_loop(0, 2 * W, slope_one, (zero, zero))
    stat1b = statistics(r["st1b"], owner, family, jnp.concatenate(carry, axis=0))

    core_last.wait_recv()
    if not own_gather:
        core_other.wait_recv()
    if own_gather:
        s_expand.start(late[1:])
        s_group = Scatter("gg", lambda o, part: r["ggs"][o])
        s_group.start(around)
    else:
        r["group_out"][...] = ggf[...].astype(BF)
        r["expand_out"][...] = dot(a2t[...], piece[...]).astype(BF)

    total1 = total(r["st1b"], stat1b)
    b1, ball = r["b1"], r["ball"]

    def norm_one(h):
        factor = gain1 * inv1 * valid(h)
        sh, ga = total1[0:1] / pixels, total1[1:2] / pixels

        def body(w, carry):
            v = factor * (back1[tile(h, w), :] - sh - first[tile(h, w), :] * ga)
            v = v.astype(BF)
            b1[tile(h, w), :] = v
            ball[tile(h, w), mids(c)] = v
            return carry

        lax.fori_loop(0, W, body, 0)

    ball_x, ball_core, ball_far = [], [], []
    for h in range(2):
        norm_one(h)
        part = ball.at[rows(h), mids(c)]
        ball_x.append(send(part, part, x_peer))
        ball_core.append(send(part, part, core_peer))

    def forward_ball(h):
        ball_x[h].wait_recv()
        part = ball.at[rows(h), mids(cx)]
        ball_far.append(send(part, part, core_peer))

    if own_gather:
        rest_early()
    b1t = r["b1t"]
    b1t[...] = b1[...].T
    if own_gather:
        s_reduce = Scatter("rg", lambda o, part: wide(b1t, x_ref, o, part, 2), 2)
        here, there = z - parity, lax.rem(z - parity + 2, 4)
        ends = (there + 1 - parity, there + parity, here + 1 - parity, z)
        halves = [(2 * slot + part, zi) for slot, zi in enumerate(ends) for part in range(2)]
        s_reduce.start(halves[:4])
        rest_late = s_expand.fold(2, zones[1])
        s_reduce.start(halves[4:])
        s_group.middle(around)
        for half in halves[0:2]:
            s_reduce.to_near(*half)
        forward_ball(0)
        rest_late()
        for half in halves[2:4]:
            s_reduce.across(*half, half[0] - 2)
        forward_ball(1)
        for half in halves[4:6]:
            s_reduce.to_near(*half)
    else:
        forward_ball(0)
        forward_ball(1)
        r["reduce_out"][...] = dot(b1t[...], x_ref[...]).astype(BF)
    ig = r["ig"]

    def chip_mids(n):
        return pl.ds(pl.multiple_of(n * 2 * MID, 128), 2 * MID)

    r["inner_grad"][...] = jnp.concatenate(
        [total1[1:2], total1[0:1], total2[1:2], total2[0:1]], axis=0
    )
    mine = r["tot3"][:, pl.ds(pl.multiple_of(xp * OUT, 128), OUT)]
    r["outer_grad"][...] = jnp.concatenate([mine[1:2], mine[0:1]], axis=0)
    for copy in wrq_in:
        copy.wait_recv()
    ig[rows(xp), :] = dpre[xp]
    ig[rows(1 - xp), :] = dother[...]

    def input_part(h, n):
        ig[rows(h), :] = ig[rows(h), :] + dot_nt(ball[rows(h), chip_mids(n)], wrq[:, chip_mids(n)])

    for h in range(2):
        ball_core[h].wait_recv()
        input_part(h, xp)
    for h in range(2):
        ball_far[h].wait_recv()
        input_part(h, 1 - xp)
    if own_gather:
        r["group_out"][...] = s_group.finish()[0:GB]
        r["expand_out"][...] = s_expand.finish_fold()
        turned = jnp.concatenate(
            [s_reduce.whole_sum(*half, half[0] - 2, half[0] - 4) for half in halves[6:8]], axis=0
        )
        r["reduce_out"][...] = turned.T
        for scatter in (s_group, s_expand, s_reduce):
            scatter.sent()
    for copy in sends:
        copy.wait_send()
    halo1.sent()
    halo2.sent()


def adamw_step(master, gradient, moment_one, moment_two, average, rate):
    first_new = 0.5 * moment_one + 0.5 * gradient
    second_new = 0.5 * moment_two + 0.5 * gradient * gradient
    correct = 1.0 - 0.5**STEP
    direction = first_new / correct / (jnp.sqrt(second_new / correct) + 1e-08)
    master_new = master - rate * (direction + 0.05 * master)
    average_new = 0.75 * average + 0.25 * master_new
    return (first_new, second_new, master_new, average_new)


def last_kernel(*refs):
    ig_ref, bo_ref = refs[:2]
    ins, (bo_out, ig_out), outs = refs[2:27], refs[27:29], refs[29:57]
    turned, held, sems = refs[57], refs[58:-1], refs[-1]
    copies = []

    def put(source, target):
        copies.append(pltpu.make_async_copy(source, target, sems.at[len(copies)]))
        copies[-1].start()

    put(bo_ref, bo_out)
    number = 0
    for n in (0, 2, 1, 3, 4):
        gradient, master, one, two, average = (ref[...] for ref in ins[5 * n : 5 * n + 5])
        rate = CONV_RATE if n < 3 else NORM_RATE
        first, second, new, mean = adamw_step(master, gradient, one, two, average, rate)
        values = [first, second, new] + ([new.astype(BF)] if n < 3 else []) + [mean]
        number = 6 * n if n < 3 else 5 * n + 3
        put(ins[5 * n], outs[number])
        for at, value in enumerate(values, number + 1):
            held[at][...] = value
            put(held[at], outs[at])
    for w in range(turned.shape[1]):
        turned[:, w] = jnp.swapaxes(ig_ref[:, w], 0, 1)
        put(turned.at[:, w], ig_out.at[:, w])
    for copy in copies:
        copy.wait()


def local(
    inputs, cotangent,
    reduce_master, reduce_first, reduce_second, reduce_average,
    group_master, group_first, group_second, group_average,
    expand_master, expand_first, expand_second, expand_average,
    inner_master, inner_first, inner_second, inner_average,
    outer_master, outer_first, outer_second, outer_average,
):
    N, rows, W, CIN = inputs.shape
    OUT = cotangent.shape[3]
    MID = inner_master.shape[1]
    H, D = lax.axis_size("height"), lax.axis_size("dp")
    HD = H * D
    R = W * N
    GB = group_master.shape[0]
    RB, EB = reduce_master.shape[0], expand_master.shape[1]
    own_gather = RB % 128 == 0 and EB % 128 == 0
    dims = dict(H=H, D=D, N=N, W=W, MID=MID, OUT=OUT, CIN=CIN, own_gather=own_gather)

    shards = dict(x=inputs.transpose(0, 2, 1, 3), ct=cotangent.transpose(0, 2, 1, 3))
    shards.update(inner=inner_master, outer=outer_master)
    ins = {}
    outs = dict(
        turned=((N, W, rows, OUT), BF),
        ig=((rows * R, OUT), F32),
        inner_grad=(inner_master.shape, F32),
        outer_grad=(outer_master.shape, F32),
    )
    scratch = dict(
        x=((rows * R, CIN), BF),
        bo=((rows * R, OUT), BF),
        ct=((rows * R, OUT), BF),
        wep=((MID, CIN), BF),
        ct2=((2, R, OUT), BF),
        out2=((2, 2, OUT), F32),
        first=((2 * R, MID), F32),
        second=((2 * R, MID), F32),
        slope1=((2 * R, MID), F32),
        slope2=((2 * R, MID), F32),
        a1=((4 * (W + 2) * N, MID), BF),
        b2=((4 * (W + 2) * N, MID), BF),
        wall=((9 * MID, MID), BF),
        wallt=((9 * MID, MID), BF),
        gf=((9 * GROUP, MID), F32),
        ggf=((9 * GROUP, MID), F32),
        st1=((HD, 2, MID), F32),
        st2=((HD, 2, MID), F32),
        st3=((2 * HD, 2, 2 * OUT), F32),
        st3b=((2 * HD, 2, 2 * OUT), F32),
        st2b=((HD, 2, MID), F32),
        st1b=((HD, 2, MID), F32),
        tot3=((2, 2 * OUT), F32),
        a2=((2 * R, MID), BF),
        a2t=((MID, 2 * R), BF),
        ax=((R, MID), BF),
        third=((2, R, OUT), F32),
        tx=((R, OUT), BF),
        tother=((R, OUT), BF),
        nother=((R, OUT), F32),
        dother=((R, OUT), F32),
        mi3=((2, 2, OUT), F32),
        pair=((2, 2, OUT), F32),
        wrq=((OUT, 4 * MID), BF),
        ball=((2 * R, 4 * MID), BF),
        tsend=((2, R, OUT), BF),
        trecv=((2, R, OUT), BF),
        dpre=((2, R, OUT), F32),
        piece=((2 * R, CIN), BF),
        agrad=((2 * R, MID), F32),
        agsend=((R, MID), BF),
        agrecv=((R, MID), BF),
        b2n=((2 * R, MID), BF),
        b2t=((MID, 2 * R), BF),
        second_back=((2 * R, MID), F32),
        b1=((2 * R, MID), BF),
        b1t=((MID, 2 * R), BF),
    )
    if own_gather:
        shards.update(em=expand_master, gm=group_master, rm=reduce_master)
        outs.update(
            reduce_out=((RB, MID), F32), group_out=((GB, MID), F32), expand_out=((MID, EB), F32)
        )
        scratch.update(
            wr=((CIN, MID), BF), we=((MID, CIN), BF), wg=((HD, SLOT, MID), BF),
            ggs=((HD, SLOT, MID), F32),
        )
        for name, n, shape in (
            ("rg", 2, (MID // 2, RB)), ("eg", 1, (MID, EB)), ("gg", 1, (SLOT, MID))
        ):
            scratch[name + "_ys"] = scratch[name + "_yr"] = (((D - 1) * H * n, *shape), BF)
            scratch[name + "_zs"] = ((H * n, *shape), BF)
            scratch[name + "_zr"] = ((H * n + 1, *shape), BF)
            scratch[name + "_own"] = ((n, *shape), F32)
    else:
        both = ("height", "dp")
        ins.update(
            wr_full=lax.all_gather(reduce_master.astype(BF), both, axis=0, tiled=True),
            wg_full=lax.all_gather(group_master.astype(BF), both, axis=0, tiled=True),
            we_full=lax.all_gather(expand_master.astype(BF), both, axis=1, tiled=True),
        )
        outs.update(
            reduce_out=((MID, CIN), BF),
            group_out=((9 * GROUP, MID), BF),
            expand_out=((MID, CIN), BF),
        )
    dims["loads"] = list(shards)
    scratch.update({name + "_in": (a.shape, a.dtype) for name, a in shards.items()})
    names = [*(name + "_hbm" for name in shards), *ins, *outs, *scratch, "lsem", "ssem", "rsem"]
    whole = pl.BlockSpec(memory_space=pltpu.VMEM)
    results = pl.pallas_call(
        functools.partial(block_kernel, names, dims),
        out_shape=[pltpu.VMEM(*v) for v in outs.values()],
        in_specs=[pl.BlockSpec(memory_space=pltpu.HBM)] * len(shards) + [whole] * len(ins),
        out_specs=[whole] * len(outs),
        scratch_shapes=[pltpu.VMEM(*v) for v in scratch.values()]
        + [pltpu.SemaphoreType.DMA((len(shards),))]
        + [pltpu.SemaphoreType.DMA((dims.get("semaphores", SEMAPHORES + 16 * D),))] * 2,
        compiler_params=pltpu.CompilerParams(
            collective_id=0, has_side_effects=True, vmem_limit_bytes=48 << 20
        ),
        name="block",
    )(
        *(pltpu.with_memory_space_constraint(v, pltpu.HBM) for v in shards.values()),
        *(pltpu.with_memory_space_constraint(v, pltpu.VMEM) for v in ins.values()),
    )
    got = dict(zip(outs, results, strict=True))
    reduce_grad, group_grad, expand_grad = got["reduce_out"], got["group_out"], got["expand_out"]
    if not own_gather:
        both = ("height", "dp")
        reduce_grad = lax.psum_scatter(reduce_grad.T, both, scatter_dimension=0, tiled=True).astype(F32)
        group_grad = lax.psum_scatter(group_grad, both, scatter_dimension=0, tiled=True).astype(F32)
        expand_grad = lax.psum_scatter(expand_grad, both, scatter_dimension=1, tiled=True).astype(F32)
    groups = (
        (reduce_grad, reduce_master, reduce_first, reduce_second, reduce_average),
        (group_grad, group_master, group_first, group_second, group_average),
        (expand_grad, expand_master, expand_first, expand_second, expand_average),
        (got["inner_grad"], inner_master, inner_first, inner_second, inner_average),
        (got["outer_grad"], outer_master, outer_first, outer_second, outer_average),
    )
    shapes = [
        jax.ShapeDtypeStruct((N, W, rows, OUT), BF),
        jax.ShapeDtypeStruct((N, W, rows, OUT), F32),
    ]
    for n, group in enumerate(groups):
        kinds = [F32] * 4 + ([BF] if n < 3 else []) + [F32]
        shapes += [jax.ShapeDtypeStruct(group[0].shape, kind) for kind in kinds]
    flat = [got["ig"].reshape(rows, W, N, OUT), got["turned"]]
    flat += [a for group in groups for a in group]
    news = pl.pallas_call(
        last_kernel,
        out_shape=shapes,
        in_specs=[whole] * len(flat),
        out_specs=[pl.BlockSpec(memory_space=pltpu.HBM)] * len(shapes),
        scratch_shapes=[pltpu.VMEM((N, W, rows, OUT), F32)]
        + [pltpu.VMEM(a.shape, a.dtype) for a in shapes[2:]]
        + [pltpu.SemaphoreType.DMA((len(shapes) + W,))],
        compiler_params=pltpu.CompilerParams(vmem_limit_bytes=40 << 20),
        name="adamw",
    )(*flat)
    pixel_outs = (a.transpose(0, 2, 1, 3) for a in news[:2])
    return (*pixel_outs, *news[2:])


def solution(mesh):
    pixel = P("dp", "height", None, "chan")
    first = P(("height", "dp"), "chan")
    last = P("chan", ("height", "dp"))
    table = P(None, "chan")
    return jax.shard_map(
        local,
        mesh=mesh,
        in_specs=(P("dp", "height", None, None), pixel)
        + (first,) * 8
        + (last,) * 4
        + (table,) * 8,
        out_specs=(pixel, pixel) + (first,) * 12 + (last,) * 6 + (table,) * 10,
        check_vma=False,
    )
```

```python
import functools

import jax
import jax.numpy as jnp
from jax import lax
from jax.experimental import pallas as pl
from jax.experimental.pallas import tpu as pltpu
from jax.sharding import PartitionSpec as P

GROUP = 32
HEIGHT = 7
STEP = 10
NORM_EPS = 1e-05
CONV_RATE = 0.02
NORM_RATE = 0.3

BF = jnp.bfloat16
F32 = jnp.float32
MESH = pl.DeviceIdType.MESH
SEMAPHORES = 192
SLOT = 48


def dot(a, b):
    return jnp.dot(a, b, preferred_element_type=F32)


def dot_nt(a, b):
    return lax.dot_general(a, b, (((1,), (1,)), ((), ())), preferred_element_type=F32)


def block_kernel(names, dims, *refs):
    r = dict(zip(names, refs, strict=True))
    H, D, N, W, MID, OUT, CIN = (dims[k] for k in ("H", "D", "N", "W", "MID", "OUT", "CIN"))
    own_gather = dims["own_gather"]
    R = W * N
    PITCH = (W + 2) * N
    HD = H * D
    pixels = float(N * D * HEIGHT * W)
    x_ref, ct_ref, inner_ref, outer_ref = r["x"], r["ct"], r["inner_in"], r["outer_in"]
    loads = {
        name: pltpu.make_async_copy(r[name + "_hbm"], r[name + "_in"], r["lsem"].at[i])
        for i, name in enumerate(dims["loads"])
    }
    for name in reversed(dims["loads"]):
        loads[name].start()

    z = lax.axis_index("height")
    c = lax.axis_index("chan")
    y = lax.axis_index("dp")
    xp = lax.div(c, 2)
    k = lax.rem(c, 2)
    cx = lax.rem(c + 2, 4)
    cc = c + 1 - 2 * k
    owner = z * D + y

    def dev(dz=0, chan=None, dy=0):
        return {
            "height": lax.rem(z + dz, H),
            "chan": c if chan is None else chan,
            "dp": lax.rem(y + dy, D),
        }

    offsets = [(dz, dy) for dz in range(H) for dy in range(D)]
    family = [dev(dz, None, dy) for dz, dy in offsets if dz or dy]
    twin_family = [dev(dz, cx, dy) for dz, dy in offsets]
    core_peer = dev(0, cc, 0)
    x_peer = dev(0, cx, 0)
    diagonal = dev(0, cx + 1 - 2 * k, 0)

    def rows(h):
        return pl.ds(pl.multiple_of(h * R, 16), R)

    def tile(h, w):
        return pl.ds(pl.multiple_of(h * R + w * N, 16), N)

    def slab(hh, ww, count):
        return pl.ds(pl.multiple_of((hh * (W + 2) + ww) * N, 16), count)

    def quarter(j, core):
        return pl.ds(pl.multiple_of((2 * j + core) * OUT, 128), OUT)

    def valid(h):
        return jnp.where(z * 2 + h < HEIGHT, 1.0, 0.0).astype(F32)

    sends = []
    used = [0]

    def make(src, dst, target, at=None):
        if at is None:
            at = (used[0], used[0])
            used[0] += 1
        return pltpu.make_async_remote_copy(
            src_ref=src,
            dst_ref=dst,
            send_sem=r["ssem"].at[at[0]],
            recv_sem=r["rsem"].at[at[1]],
            device_id=target,
            device_id_type=MESH,
        )

    def send(src, dst, target):
        copy = make(src, dst, target)
        copy.start()
        sends.append(copy)
        return copy

    barrier = pltpu.get_barrier_semaphore()
    everyone = family + twin_family + [core_peer, diagonal]
    for target in everyone:
        pl.semaphore_signal(barrier, inc=1, device_id=target, device_id_type=MESH)
    a1, b2 = r["a1"], r["b2"]
    lane_group = lax.shift_right_logical(lax.broadcasted_iota(jnp.int32, (MID, MID), 1), 5)
    row_group = lax.shift_right_logical(lax.broadcasted_iota(jnp.int32, (MID, MID), 0), 5)
    block_diagonal = lane_group == row_group
    if own_gather:
        wr, we, wg = r["wr"], r["we"], r["wg"]
        RB, EB = r["rm_in"].shape[0], r["em_in"].shape[1]
        GB = r["gm_in"].shape[0]

        def reduce_block(o):
            return wr.at[pl.ds(pl.multiple_of(o * RB, 16), RB), :]

        def expand_block(o):
            return we.at[:, pl.ds(pl.multiple_of(o * EB, 128), EB)]

        def group_block(o):
            return wg.at[o]

        loads["rm"].wait()
        reduce_block(owner)[...] = r["rm_in"][...].astype(BF)
    else:
        wr, we = r["wr_full"], r["we_full"]

    pl.semaphore_wait(barrier, len(everyone))

    near = [z + 1 - 2 * lax.rem(z, 2), jnp.where(z < 2, 2, 1), jnp.where(z < 2, 3, 0)]

    class Gather:
        def __init__(self, block):
            self.block = block
            self.here = block(owner)
            self.base = used[0]
            used[0] += H
            self.along_y = []

        def send_z(self, rank):
            target = {"height": near[rank], "chan": c, "dp": y}
            copy = make(self.here, self.here, target, (self.base + rank, self.base + z))
            copy.start()
            sends.append(copy)

        def send_y(self):
            self.pass_on(self.here)

        def pass_on(self, block):
            self.along_y.append([send(block, block, dev(0, None, dy)) for dy in range(1, D)])

        def forward(self, rank):
            source = near[rank]
            block = self.block(source * D + y)
            make(block, block, dev(), (self.base, self.base + source)).wait_recv()
            self.pass_on(block)
            return source

        def finish(self, number):
            for copy in self.along_y[number]:
                copy.wait_recv()

    if own_gather:
        def reduce_part(n):
            return lambda o: wr.at[pl.ds(pl.multiple_of(o * RB + n * (RB // 2), 16), RB // 2), :]

        g_reduce = [Gather(reduce_part(n)) for n in range(2)]
        g_group, g_expand = Gather(group_block), Gather(expand_block)
        for rank in range(3):
            for part in g_reduce:
                part.send_z(rank)
        for part in g_reduce:
            part.send_y()
        for name in ("gm", "em"):
            loads[name].wait()
        wg[owner] = jnp.concatenate(
            [r["gm_in"][...], jnp.zeros((SLOT - GB, MID), F32)], axis=0
        ).astype(BF)
        expand_block(owner)[...] = r["em_in"][...].astype(BF)
        for rank in range(3):
            g_group.send_z(rank)
        g_group.send_y()
    wep = r["wep"]
    twin_in = []

    def twin(o):
        twin_in.append(
            send(expand_block(o), wep.at[:, pl.ds(pl.multiple_of(o * EB, 128), EB)], x_peer)
        )

    def twin_y(number, zz):
        g_expand.finish(number)
        for dy in range(1, D):
            twin(zz * D + lax.rem(y + dy, D))

    if own_gather:
        g_expand.send_z(0)
        g_expand.send_z(1)
        g_expand.send_y()
        twin(owner)
    else:
        twin_in.append(send(we, wep, x_peer))

    def relay(source, target):
        def body(w, carry):
            turned = jnp.swapaxes(source[:, w], 0, 1)
            for h in range(2):
                target[tile(h, w), :] = turned[h]
            return carry

        lax.fori_loop(0, W, body, 0)

    loads["inner"].wait()
    loads["outer"].wait()
    loads["ct"].wait()
    relay(r["ct_in"], ct_ref)
    ct2, out2 = r["ct2"], r["out2"]
    ct_in = send(ct_ref.at[rows(1 - xp)], ct2.at[xp], x_peer)
    ct2[xp] = ct_ref[rows(xp), :]
    out2[xp] = outer_ref[...]
    outer_in = send(out2.at[xp], out2.at[xp], x_peer)
    a1[...] = jnp.zeros(a1.shape, BF)
    b2[...] = jnp.zeros(b2.shape, BF)
    loads["x"].wait()
    relay(r["x_in"], x_ref)

    def statistics(buf, position, targets, value):
        buf[position] = value
        return [send(buf.at[position], buf.at[position], t) for t in targets]

    def total(buf, copies):
        for copy in copies:
            copy.wait_recv()
        return jnp.sum(buf[...], axis=0)

    first = r["first"]

    def product(blocks, start):
        def body(h, carry):
            left = jnp.concatenate(
                [x_ref[rows(h), pl.ds(pl.multiple_of(o * RB, 128), RB)] for o in blocks], axis=1
            )
            right = jnp.concatenate([reduce_block(o)[...] for o in blocks], axis=0)
            part = dot(left, right)
            first[rows(h), :] = part if start else first[rows(h), :] + part
            return carry

        lax.fori_loop(0, 2, body, 0)

    if own_gather:
        for part in g_reduce:
            part.forward(0)
        twin_y(0, z)
        for rank in (1, 2):
            for part in g_reduce:
                part.forward(rank)
        product([zz * D + y for zz in range(H)], True)
        for rank in range(3):
            g_group.forward(rank)
        sources = [z]
        sources.append(g_expand.forward(0))
        twin(sources[1] * D + y)
        for number in range(4):
            for part in g_reduce:
                part.finish(number)
        for dy in range(1, D):
            product([zz * D + lax.rem(y + dy, D) for zz in range(H)], False)
    else:
        def body(h, carry):
            first[rows(h), :] = dot(x_ref[rows(h), :], wr[...])
            return carry

        lax.fori_loop(0, 2, body, 0)

    def moments(ref):
        def body(h, carry):
            v = ref[rows(h), :]
            return (
                carry[0] + jnp.sum(v, axis=0, keepdims=True) * valid(h),
                carry[1] + jnp.sum(v * v, axis=0, keepdims=True) * valid(h),
            )

        zero = jnp.zeros((1, ref.shape[1]), F32)
        return jnp.concatenate(lax.fori_loop(0, 2, body, (zero, zero)), axis=0)

    def average_and_inverse(sums):
        mean = sums[0:1] / pixels
        return mean, lax.rsqrt(sums[1:2] / pixels - mean * mean + NORM_EPS)

    stat1 = statistics(r["st1"], owner, family, moments(first))

    wall, wallt, gf = r["wall"], r["wallt"], r["gf"]
    if own_gather:
        g_expand.send_z(2)
        sources.append(g_expand.forward(1))
        twin(sources[2] * D + y)
        for number in range(4):
            g_group.finish(number)
        for o in range(HD):
            gf[o * GB : (o + 1) * GB, :] = wg[o].astype(F32)[0:GB]
    else:
        gf[...] = r["wg_full"][...].astype(F32)

    def spread(t, carry):
        piece = gf[pl.ds(pl.multiple_of(t * GROUP, 8), GROUP), :]
        full = jnp.where(block_diagonal, jnp.concatenate([piece] * (MID // GROUP), axis=0), 0.0)
        wall[pl.ds(pl.multiple_of(t * MID, 16), MID), :] = full.astype(BF)
        wallt[pl.ds(pl.multiple_of((8 - t) * MID, 16), MID), :] = full.T.astype(BF)
        return carry

    lax.fori_loop(0, 9, spread, 0)
    mean1, inv1 = average_and_inverse(total(r["st1"], stat1))
    gain1, shift1 = inner_ref[0:1, :], inner_ref[1:2, :]
    slope1 = r["slope1"]

    def activate(h):
        ok = valid(h)

        def body(w, carry):
            v = (first[tile(h, w), :] - mean1) * inv1
            v = v * gain1 + shift1
            q = jax.nn.sigmoid(v)
            a1[slab(h + 1, w + 1, N), :] = (v * q * ok).astype(BF)
            slope1[tile(h, w), :] = q * (1.0 + v * (1.0 - q)) * ok
            return carry

        lax.fori_loop(0, W, body, 0)

    class Halo:
        def __init__(self, ref):
            self.up = make(ref.at[slab(1, 1, R)], ref.at[slab(3, 1, R)], dev(H - 1, None, 0))
            self.down = make(ref.at[slab(2, 1, R)], ref.at[slab(0, 1, R)], dev(1, None, 0))

        def start_up(self):
            pl.when(z > 0)(self.up.start)

        def start_down(self):
            pl.when(z < H - 1)(self.down.start)

        def arrived(self):
            pl.when(z > 0)(self.down.wait_recv)
            pl.when(z < H - 1)(self.up.wait_recv)

        def sent(self):
            pl.when(z > 0)(self.up.wait_send)
            pl.when(z < H - 1)(self.down.wait_send)

    halo1, halo2 = Halo(a1), Halo(b2)
    activate(0)
    halo1.start_up()
    activate(1)
    halo1.start_down()

    def convolve(ref, weights, out, edge):
        def body(h, carry):
            if edge:
                hh, base, count = 3 * h, 6 * h, 1
            else:
                hh, base, count = 1, 3 * (1 - h), 2
            left = jnp.concatenate(
                [ref[slab(hh + i, kc, R), :] for i in range(count) for kc in range(3)], axis=1
            )
            part = dot(left, weights[pl.ds(pl.multiple_of(base * MID, 16), 3 * count * MID), :])
            out[rows(h), :] = out[rows(h), :] + part if edge else part
            return carry

        lax.fori_loop(0, 2, body, 0)

    second = r["second"]
    convolve(a1, wall, second, False)
    if own_gather:
        sources.append(g_expand.forward(2))
        twin(sources[3] * D + y)
        twin_y(1, sources[1])
        twin_y(2, sources[2])
    halo1.arrived()
    convolve(a1, wall, second, True)
    stat2 = statistics(r["st2"], owner, family, moments(second))
    mean2, inv2 = average_and_inverse(total(r["st2"], stat2))
    gain2, shift2 = inner_ref[2:3, :], inner_ref[3:4, :]
    a2, slope2 = r["a2"], r["slope2"]

    def activate_two(h):
        ok = valid(h)

        def body(w, carry):
            n = (second[tile(h, w), :] - mean2) * inv2
            second[tile(h, w), :] = n
            v = n * gain2 + shift2
            q = jax.nn.sigmoid(v)
            a2[tile(h, w), :] = (v * q * ok).astype(BF)
            slope2[tile(h, w), :] = q * (1.0 + v * (1.0 - q)) * ok
            return carry

        lax.fori_loop(0, W, body, 0)

    activate_two(1 - xp)
    ax_in = send(a2.at[rows(1 - xp)], r["ax"], x_peer)
    activate_two(xp)
    if own_gather:
        twin_y(3, sources[3])

    for copy in twin_in:
        copy.wait_recv()
    ax_in.wait_recv()
    third, tsend, trecv = r["third"], r["tsend"], r["trecv"]
    left = jnp.concatenate([a2[rows(xp), :], r["ax"][...]], axis=1)

    def expand(j, core):
        right = jnp.concatenate([we[:, quarter(j, core)], wep[:, quarter(j, core)]], axis=0)
        return dot(left, right)

    core_in = []
    for j in range(2):
        tsend[j] = expand(j, 1 - k).astype(BF)
        core_in.append(send(tsend.at[j], trecv.at[j], core_peer))
    for j in range(2):
        third[j] = expand(j, k)
    okx = valid(xp)
    sums = []
    for j in range(2):
        core_in[j].wait_recv()

        def body(w, carry):
            at = pl.ds(pl.multiple_of(w * N, 16), N)
            v = third[j, at, :] + trecv[j, at, :].astype(F32)
            third[j, at, :] = v
            return carry[0] + jnp.sum(v, axis=0, keepdims=True), carry[1] + jnp.sum(
                v * v, axis=0, keepdims=True
            )

        zero = jnp.zeros((1, OUT), F32)
        sums.append(lax.fori_loop(0, W, body, (zero, zero)))
    r["tx"][...] = third[1 - xp].astype(BF)
    position = xp * HD + owner
    both = twin_family + family
    stat3 = statistics(
        r["st3"],
        position,
        both,
        jnp.concatenate(
            [jnp.concatenate([s[i] for s in sums], axis=1) * okx for i in range(2)], axis=0
        ),
    )
    cut = (W + 1) // 2
    parts = [pl.ds(0, cut * N), pl.ds(cut * N, (W - cut) * N)]
    tx_in = [send(r["tx"].at[parts[0]], r["tother"].at[parts[0]], x_peer)]
    wrq = r["wrq"]

    def mids(chan):
        return pl.ds(pl.multiple_of(chan * MID, 128), MID)

    wrq[:, mids(c)] = wr[quarter(xp, k), :]
    wrq_in = [send(wr.at[quarter(xp, 1 - k), :], wrq.at[:, mids(c)], core_peer)]
    share = OUT // 2

    def send_wrq(n):
        target, core = ((x_peer, k), (diagonal, 1 - k))[n // 2]
        at = pl.ds(pl.multiple_of((2 * (1 - xp) + core) * OUT + n % 2 * share, 16), share)
        there = wrq.at[pl.ds(n % 2 * share, share), mids(c)]
        wrq_in.append(send(wr.at[at, :], there, target))

    a2t = r["a2t"]
    a2t[...] = a2[...].T
    ct_in.wait_recv()
    outer_in.wait_recv()
    mean3, inv3 = average_and_inverse(total(r["st3"], stat3))
    dpre, dother, bo = r["dpre"], r["dother"], r["bo"]
    mi3 = r["mi3"]
    for j in range(2):
        lanes = slice(j * OUT, (j + 1) * OUT)
        mi3[j] = jnp.concatenate([mean3[:, lanes], inv3[:, lanes]], axis=0)

    def outer_norm(j, h, values, grads, write, start=0, stop=W):
        m, iv = mi3[j, 0:1, :], mi3[j, 1:2, :]
        g, s = out2[j, 0:1, :], out2[j, 1:2, :]
        ok = valid(h)

        def body(w, carry):
            at = pl.ds(pl.multiple_of(w * N, 16), N)
            n = (values[0](at) - m) * iv
            values[1](at, n)
            v = n * g + s + x_ref[tile(h, w), quarter(j, k)].astype(F32)
            q = jax.nn.sigmoid(v)
            if write:
                bo[tile(h, w), :] = (v * q * ok).astype(BF)
            d = grads[0](at, w) * ok * (q * (1.0 + v * (1.0 - q)))
            grads[1](at, d)
            return carry[0] + jnp.sum(d, axis=0, keepdims=True), carry[1] + jnp.sum(
                d * n, axis=0, keepdims=True
            )

        zero = jnp.zeros((1, OUT), F32)
        return lax.fori_loop(start, stop, body, (zero, zero))

    def third_access(j):
        def get(at):
            return third[j, at, :]

        def put(at, n):
            third[j, at, :] = n

        def get_ct(at, w):
            return ct2[j, at, :].astype(F32)

        def put_d(at, d):
            dpre[j, at, :] = d

        return (get, put), (get_ct, put_d)

    st3b = r["st3b"]
    pair = r["pair"]
    for j, write in ((xp, True), (1 - xp, False)):
        pair[j] = jnp.concatenate(outer_norm(j, xp, *third_access(j), write), axis=0)
    stat3b = statistics(st3b, position, both, jnp.concatenate([pair[0], pair[1]], axis=1))

    tx_in.append(send(r["tx"].at[parts[1]], r["tother"].at[parts[1]], x_peer))
    send_wrq(0)
    tx_in[0].wait_recv()
    nother = r["nother"]

    def get_other(at):
        return r["tother"][at, :].astype(F32)

    def put_other(at, n):
        nother[at, :] = n

    def get_ct_other(at, w):
        return ct_ref[tile(1 - xp, w), :].astype(F32)

    def put_d_other(at, d):
        dother[at, :] = d

    other_row = ((get_other, put_other), (get_ct_other, put_d_other), True)
    outer_norm(xp, 1 - xp, *other_row, 0, cut)
    total3 = total(st3b, stat3b)
    r["tot3"][...] = total3
    for j in range(2):
        lanes = slice(j * OUT, (j + 1) * OUT)
        pair[j] = total3[:, lanes] / pixels
    piece = r["piece"]

    def back_three(j, h, upstream, normed):
        factor = out2[j, 0:1, :] * mi3[j, 1:2, :] * valid(h)
        sh, ga = pair[j, 0:1, :], pair[j, 1:2, :]

        def body(w, carry):
            at = pl.ds(pl.multiple_of(w * N, 16), N)
            v = factor * (upstream(at) - sh - normed(at) * ga)
            piece[tile(h, w), quarter(j, k)] = v.astype(BF)
            return carry

        lax.fori_loop(0, W, body, 0)
        part = piece.at[rows(h), quarter(j, k)]
        return send(part, part, core_peer)

    core_in = [
        back_three(j, xp, lambda at, j=j: dpre[j, at, :], lambda at, j=j: third[j, at, :])
        for j in range(2)
    ]
    for copy in core_in:
        copy.wait_recv()
    agrad = r["agrad"]
    r["agsend"][...] = dot_nt(piece[rows(xp), :], wep[...]).astype(BF)
    ag_in = send(r["agsend"], r["agrecv"], x_peer)
    part = piece.at[rows(xp), quarter(xp, k)]
    piece_in = send(part, part, x_peer)
    agrad[rows(xp), :] = dot_nt(piece[rows(xp), :], we[...])
    tx_in[1].wait_recv()
    outer_norm(xp, 1 - xp, *other_row, cut, W)
    core_other = back_three(xp, 1 - xp, lambda at: dother[at, :], lambda at: nother[at, :])

    class Scatter:
        def __init__(self, name, block, parts=1):
            self.block = block
            self.parts = parts
            self.ys, self.yr = r[name + "_ys"], r[name + "_yr"]
            self.zs, self.zr = r[name + "_zs"], r[name + "_zr"]
            self.own = r[name + "_own"]
            self.along_y, self.along_z = {}, []
            self.pair, self.cross = {}, {}
            self.base = used[0]
            used[0] += H * parts

        def start(self, targets):
            for slot, zi in targets:
                self.along_y[slot] = []
                for dy in range(1, D):
                    n = (dy - 1) * H * self.parts + slot
                    self.ys[n] = self.block(zi * D + lax.rem(y + dy, D), slot % self.parts).astype(BF)
                    self.along_y[slot].append(
                        (n, send(self.ys.at[n], self.yr.at[n], dev(0, None, dy)))
                    )

        def middle(self, targets):
            for slot, zi in targets:
                part = slot % self.parts
                value = self.block(zi * D + y, part)
                for n, copy in self.along_y[slot]:
                    copy.wait_recv()
                    value = value + self.yr[n].astype(F32)
                other = zi != z

                @pl.when(jnp.logical_not(other))
                def keep():
                    self.own[part] = value

                self.zs[slot] = value.astype(BF)
                target = {"height": zi, "chan": c, "dp": y}
                here = z * self.parts + part
                at = (self.base + slot, self.base + here)
                copy = make(self.zs.at[slot], self.zr.at[here], target, at)
                pl.when(other)(copy.start)
                self.along_z.append((other, copy))

        def fold(self, base, zone):
            far, kept = zone + 1 - lax.rem(z, 2), zone + lax.rem(z, 2)

            def received(zi):
                value = self.block(zi * D + y, 0)
                for dy in range(1, D):
                    value = value + self.yr[(dy - 1) * H + base + lax.rem(zi - zone + k, 2)].astype(F32)
                return value

            for slot in (base, base + 1):
                for n, copy in self.along_y[slot]:
                    copy.wait_recv()
            self.zs[base] = received(far).astype(BF)
            target = {"height": near[0], "chan": c, "dp": y}
            pair = send(self.zs.at[base], self.zr.at[base], target)

            def rest():
                value = received(kept)
                pair.wait_recv()
                value = value + self.zr[base].astype(F32)
                other = kept != z

                @pl.when(jnp.logical_not(other))
                def keep():
                    self.own[0] = value

                self.zs[base + 1] = value.astype(BF)
                target = {"height": lax.rem(z + 2, 4), "chan": c, "dp": y}
                at = (self.base, self.base)
                copy = make(self.zs.at[base + 1], self.zr.at[H], target, at)
                pl.when(other)(copy.start)
                self.along_z.append((other, copy))
                self.last = copy

            return rest

        def summed_y(self, slot, zi):
            part = slot % self.parts
            value = self.block(zi * D + y, part)
            for n, copy in self.along_y[slot]:
                copy.wait_recv()
                value = value + self.yr[n].astype(F32)
            return value

        def to_near(self, slot, zi):
            self.zs[slot] = self.summed_y(slot, zi).astype(BF)
            target = {"height": near[0], "chan": c, "dp": y}
            self.pair[slot] = send(self.zs.at[slot], self.zr.at[slot], target)

        def from_near(self, slot):
            self.pair[slot].wait_recv()
            return self.zr[slot].astype(F32)

        def across(self, slot, zi, pair):
            value = self.summed_y(slot, zi) + self.from_near(pair)
            self.zs[slot] = value.astype(BF)
            target = {"height": lax.rem(z + 2, 4), "chan": c, "dp": y}
            self.cross[slot] = send(self.zs.at[slot], self.zr.at[slot], target)

        def whole_sum(self, slot, zi, pair, cross):
            value = self.summed_y(slot, zi) + self.from_near(pair)
            self.cross[cross].wait_recv()
            return value + self.zr[cross].astype(F32)

        def finish_fold(self):
            self.last.wait_recv()
            return self.own[0] + self.zr[H].astype(F32)

        def finish(self, part=0):
            value = self.own[part]
            for dz in range(1, H):
                s = lax.rem(z + dz, H) * self.parts + part
                at = (self.base, self.base + s)
                make(self.zs.at[0], self.zr.at[s], dev(dz), at).wait_recv()
                value = value + self.zr[s].astype(F32)
            return value

        def sent(self):
            for other, copy in self.along_z:
                pl.when(other)(copy.wait_send)

    def wide(left_ref, right_ref, o, part, parts):
        share = left_ref.shape[0] // parts
        left = left_ref[part * share : (part + 1) * share, :]
        return dot(left, right_ref[:, pl.ds(pl.multiple_of(o * EB, 128), EB)])

    def slope_two(h, received, carry):
        def body(w, carry):
            if received:
                up = r["agrecv"][pl.ds(pl.multiple_of(w * N, 16), N), :].astype(F32)
            else:
                up = agrad[tile(h, w), :]
            d = up * slope2[tile(h, w), :]
            agrad[tile(h, w), :] = d
            return carry[0] + jnp.sum(d, axis=0, keepdims=True), carry[1] + jnp.sum(
                d * second[tile(h, w), :], axis=0, keepdims=True
            )

        return lax.fori_loop(0, W, body, carry)

    parity = lax.rem(z, 2)
    zones = (2 * xp, 2 * (1 - xp))
    early = [(0, zones[0] + k), (1, zones[0] + 1 - k)]
    late = [(2, zones[1] + k), (3, zones[1] + 1 - k)]
    around = [(0, lax.rem(z + 2, 4)), (1, 3 - z), (2, near[0]), (3, z)]
    if own_gather:
        s_expand = Scatter("eg", lambda o, part: wide(a2t, piece, o, part, 1))
        core_other.wait_recv()
        s_expand.start(early)
    zero = jnp.zeros((1, MID), F32)
    carry = slope_two(xp, False, (zero, zero))
    ag_in.wait_recv()
    carry = slope_two(1 - xp, True, carry)
    stat2b = statistics(r["st2b"], owner, family, jnp.concatenate(carry, axis=0))

    def turn(w, carry):
        r["turned"][:, w] = jnp.swapaxes(jnp.stack([bo[tile(h, w), :] for h in range(2)]), 0, 1)
        return carry

    lax.fori_loop(0, W, turn, 0)
    if own_gather:
        rest_early = s_expand.fold(0, zones[0])
    for n in range(1, 4):
        send_wrq(n)
    total2 = total(r["st2b"], stat2b)
    b2n = r["b2n"]

    def norm_two(h):
        factor = gain2 * inv2 * valid(h)
        sh, ga = total2[0:1] / pixels, total2[1:2] / pixels

        def body(w, carry):
            v = factor * (agrad[tile(h, w), :] - sh - second[tile(h, w), :] * ga)
            v = v.astype(BF)
            b2[slab(h + 1, w + 1, N), :] = v
            b2n[tile(h, w), :] = v
            return carry

        lax.fori_loop(0, W, body, 0)

    norm_two(0)
    halo2.start_up()
    norm_two(1)
    halo2.start_down()
    back1 = r["second_back"]
    convolve(b2, wallt, back1, False)
    b2t = r["b2t"]
    b2t[...] = b2n[...].T
    ggf = r["ggf"]
    fold = jnp.where(
        jnp.bitwise_and(lax.broadcasted_iota(jnp.int32, (GROUP, MID), 1), GROUP - 1)
        == lax.broadcasted_iota(jnp.int32, (GROUP, MID), 0),
        1.0,
        0.0,
    ).astype(BF)

    def group_grad(t, carry):
        kr, kc = lax.div(t, 3), lax.rem(t, 3)
        left = jnp.concatenate([a1[slab(kr, kc, R), :], a1[slab(kr + 1, kc, R), :]], axis=0)
        turned = jnp.where(block_diagonal, dot(b2t[...], left), 0.0).astype(BF)
        ggf[pl.ds(pl.multiple_of(t * GROUP, 8), GROUP), :] = dot_nt(fold, turned)
        return carry

    lax.fori_loop(0, 9, group_grad, 0)

    if own_gather:
        for o in range(HD):
            r["ggs"][o] = jnp.concatenate(
                [ggf[o * GB : (o + 1) * GB, :], jnp.zeros((SLOT - GB, MID), F32)], axis=0
            )
    piece_in.wait_recv()
    part = piece.at[rows(1 - xp), quarter(1 - xp, k)]
    core_last = send(part, part, core_peer)
    if own_gather:
        s_expand.start(late[:1])
    halo2.arrived()
    convolve(b2, wallt, back1, True)

    def slope_one(i, carry):
        h, w = lax.div(i, W), lax.rem(i, W)
        d = back1[tile(h, w), :] * slope1[tile(h, w), :]
        n = (first[tile(h, w), :] - mean1) * inv1
        first[tile(h, w), :] = n
        back1[tile(h, w), :] = d
        return carry[0] + jnp.sum(d, axis=0, keepdims=True), carry[1] + jnp.sum(
            d * n, axis=0, keepdims=True
        )

    carry = lax.fori_loop(0, 2 * W, slope_one, (zero, zero))
    stat1b = statistics(r["st1b"], owner, family, jnp.concatenate(carry, axis=0))

    core_last.wait_recv()
    if not own_gather:
        core_other.wait_recv()
    if own_gather:
        s_expand.start(late[1:])
        s_group = Scatter("gg", lambda o, part: r["ggs"][o])
        s_group.start(around)
    else:
        r["group_out"][...] = ggf[...].astype(BF)
        r["expand_out"][...] = dot(a2t[...], piece[...]).astype(BF)

    total1 = total(r["st1b"], stat1b)
    b1, ball = r["b1"], r["ball"]

    def norm_one(h):
        factor = gain1 * inv1 * valid(h)
        sh, ga = total1[0:1] / pixels, total1[1:2] / pixels

        def body(w, carry):
            v = factor * (back1[tile(h, w), :] - sh - first[tile(h, w), :] * ga)
            v = v.astype(BF)
            b1[tile(h, w), :] = v
            ball[tile(h, w), mids(c)] = v
            return carry

        lax.fori_loop(0, W, body, 0)

    ball_x, ball_core, ball_far = [], [], []
    for h in range(2):
        norm_one(h)
        part = ball.at[rows(h), mids(c)]
        ball_x.append(send(part, part, x_peer))
        ball_core.append(send(part, part, core_peer))

    def forward_ball(h):
        ball_x[h].wait_recv()
        part = ball.at[rows(h), mids(cx)]
        ball_far.append(send(part, part, core_peer))

    if own_gather:
        rest_early()
    b1t = r["b1t"]
    b1t[...] = b1[...].T
    if own_gather:
        s_reduce = Scatter("rg", lambda o, part: wide(b1t, x_ref, o, part, 2), 2)
        here, there = z - parity, lax.rem(z - parity + 2, 4)
        ends = (there + 1 - parity, there + parity, here + 1 - parity, z)
        halves = [(2 * slot + part, zi) for slot, zi in enumerate(ends) for part in range(2)]
        s_reduce.start(halves[:4])
        rest_late = s_expand.fold(2, zones[1])
        s_reduce.start(halves[4:])
        s_group.middle(around)
        for half in halves[0:2]:
            s_reduce.to_near(*half)
        forward_ball(0)
        rest_late()
        for half in halves[2:4]:
            s_reduce.across(*half, half[0] - 2)
        forward_ball(1)
        for half in halves[4:6]:
            s_reduce.to_near(*half)
    else:
        forward_ball(0)
        forward_ball(1)
        r["reduce_out"][...] = dot(b1t[...], x_ref[...]).astype(BF)
    ig = r["ig"]

    def chip_mids(n):
        return pl.ds(pl.multiple_of(n * 2 * MID, 128), 2 * MID)

    r["inner_grad"][...] = jnp.concatenate(
        [total1[1:2], total1[0:1], total2[1:2], total2[0:1]], axis=0
    )
    mine = r["tot3"][:, pl.ds(pl.multiple_of(xp * OUT, 128), OUT)]
    r["outer_grad"][...] = jnp.concatenate([mine[1:2], mine[0:1]], axis=0)
    for copy in wrq_in:
        copy.wait_recv()
    ig[rows(xp), :] = dpre[xp]
    ig[rows(1 - xp), :] = dother[...]

    def input_part(h, n):
        ig[rows(h), :] = ig[rows(h), :] + dot_nt(ball[rows(h), chip_mids(n)], wrq[:, chip_mids(n)])

    for h in range(2):
        ball_core[h].wait_recv()
        input_part(h, xp)
    for h in range(2):
        ball_far[h].wait_recv()
        input_part(h, 1 - xp)
    if own_gather:
        r["group_out"][...] = s_group.finish()[0:GB]
        r["expand_out"][...] = s_expand.finish_fold()
        turned = jnp.concatenate(
            [s_reduce.whole_sum(*half, half[0] - 2, half[0] - 4) for half in halves[6:8]], axis=0
        )
        r["reduce_out"][...] = turned.T
        for scatter in (s_group, s_expand, s_reduce):
            scatter.sent()
    for copy in sends:
        copy.wait_send()
    halo1.sent()
    halo2.sent()


def adamw_step(master, gradient, moment_one, moment_two, average, rate):
    first_new = 0.5 * moment_one + 0.5 * gradient
    second_new = 0.5 * moment_two + 0.5 * gradient * gradient
    correct = 1.0 - 0.5**STEP
    direction = first_new / correct / (jnp.sqrt(second_new / correct) + 1e-08)
    master_new = master - rate * (direction + 0.05 * master)
    average_new = 0.75 * average + 0.25 * master_new
    return (first_new, second_new, master_new, average_new)


def last_kernel(*refs):
    ig_ref, bo_ref = refs[:2]
    ins, (bo_out, ig_out), outs = refs[2:27], refs[27:29], refs[29:57]
    turned, held, sems = refs[57], refs[58:-1], refs[-1]
    copies = []

    def put(source, target):
        copies.append(pltpu.make_async_copy(source, target, sems.at[len(copies)]))
        copies[-1].start()

    put(bo_ref, bo_out)
    number = 0
    for n in (0, 2, 1, 3, 4):
        gradient, master, one, two, average = (ref[...] for ref in ins[5 * n : 5 * n + 5])
        rate = CONV_RATE if n < 3 else NORM_RATE
        first, second, new, mean = adamw_step(master, gradient, one, two, average, rate)
        values = [first, second, new] + ([new.astype(BF)] if n < 3 else []) + [mean]
        number = 6 * n if n < 3 else 5 * n + 3
        put(ins[5 * n], outs[number])
        for at, value in enumerate(values, number + 1):
            held[at][...] = value
            put(held[at], outs[at])
    for w in range(turned.shape[1]):
        turned[:, w] = jnp.swapaxes(ig_ref[:, w], 0, 1)
        put(turned.at[:, w], ig_out.at[:, w])
    for copy in copies:
        copy.wait()


def local(
    inputs, cotangent,
    reduce_master, reduce_first, reduce_second, reduce_average,
    group_master, group_first, group_second, group_average,
    expand_master, expand_first, expand_second, expand_average,
    inner_master, inner_first, inner_second, inner_average,
    outer_master, outer_first, outer_second, outer_average,
):
    N, rows, W, CIN = inputs.shape
    OUT = cotangent.shape[3]
    MID = inner_master.shape[1]
    H, D = lax.axis_size("height"), lax.axis_size("dp")
    HD = H * D
    R = W * N
    GB = group_master.shape[0]
    RB, EB = reduce_master.shape[0], expand_master.shape[1]
    own_gather = RB % 128 == 0 and EB % 128 == 0
    dims = dict(H=H, D=D, N=N, W=W, MID=MID, OUT=OUT, CIN=CIN, own_gather=own_gather)

    shards = dict(x=inputs.transpose(0, 2, 1, 3), ct=cotangent.transpose(0, 2, 1, 3))
    shards.update(inner=inner_master, outer=outer_master)
    ins = {}
    outs = dict(
        turned=((N, W, rows, OUT), BF),
        ig=((rows * R, OUT), F32),
        inner_grad=(inner_master.shape, F32),
        outer_grad=(outer_master.shape, F32),
    )
    scratch = dict(
        x=((rows * R, CIN), BF),
        bo=((rows * R, OUT), BF),
        ct=((rows * R, OUT), BF),
        wep=((MID, CIN), BF),
        ct2=((2, R, OUT), BF),
        out2=((2, 2, OUT), F32),
        first=((2 * R, MID), F32),
        second=((2 * R, MID), F32),
        slope1=((2 * R, MID), F32),
        slope2=((2 * R, MID), F32),
        a1=((4 * (W + 2) * N, MID), BF),
        b2=((4 * (W + 2) * N, MID), BF),
        wall=((9 * MID, MID), BF),
        wallt=((9 * MID, MID), BF),
        gf=((9 * GROUP, MID), F32),
        ggf=((9 * GROUP, MID), F32),
        st1=((HD, 2, MID), F32),
        st2=((HD, 2, MID), F32),
        st3=((2 * HD, 2, 2 * OUT), F32),
        st3b=((2 * HD, 2, 2 * OUT), F32),
        st2b=((HD, 2, MID), F32),
        st1b=((HD, 2, MID), F32),
        tot3=((2, 2 * OUT), F32),
        a2=((2 * R, MID), BF),
        a2t=((MID, 2 * R), BF),
        ax=((R, MID), BF),
        third=((2, R, OUT), F32),
        tx=((R, OUT), BF),
        tother=((R, OUT), BF),
        nother=((R, OUT), F32),
        dother=((R, OUT), F32),
        mi3=((2, 2, OUT), F32),
        pair=((2, 2, OUT), F32),
        wrq=((OUT, 4 * MID), BF),
        ball=((2 * R, 4 * MID), BF),
        tsend=((2, R, OUT), BF),
        trecv=((2, R, OUT), BF),
        dpre=((2, R, OUT), F32),
        piece=((2 * R, CIN), BF),
        agrad=((2 * R, MID), F32),
        agsend=((R, MID), BF),
        agrecv=((R, MID), BF),
        b2n=((2 * R, MID), BF),
        b2t=((MID, 2 * R), BF),
        second_back=((2 * R, MID), F32),
        b1=((2 * R, MID), BF),
        b1t=((MID, 2 * R), BF),
    )
    if own_gather:
        shards.update(em=expand_master, gm=group_master, rm=reduce_master)
        outs.update(
            reduce_out=((RB, MID), F32), group_out=((GB, MID), F32), expand_out=((MID, EB), F32)
        )
        scratch.update(
            wr=((CIN, MID), BF), we=((MID, CIN), BF), wg=((HD, SLOT, MID), BF),
            ggs=((HD, SLOT, MID), F32),
        )
        for name, n, shape in (
            ("rg", 2, (MID // 2, RB)), ("eg", 1, (MID, EB)), ("gg", 1, (SLOT, MID))
        ):
            scratch[name + "_ys"] = scratch[name + "_yr"] = (((D - 1) * H * n, *shape), BF)
            scratch[name + "_zs"] = ((H * n, *shape), BF)
            scratch[name + "_zr"] = ((H * n + 1, *shape), BF)
            scratch[name + "_own"] = ((n, *shape), F32)
    else:
        both = ("height", "dp")
        ins.update(
            wr_full=lax.all_gather(reduce_master.astype(BF), both, axis=0, tiled=True),
            wg_full=lax.all_gather(group_master.astype(BF), both, axis=0, tiled=True),
            we_full=lax.all_gather(expand_master.astype(BF), both, axis=1, tiled=True),
        )
        outs.update(
            reduce_out=((MID, CIN), BF),
            group_out=((9 * GROUP, MID), BF),
            expand_out=((MID, CIN), BF),
        )
    dims["loads"] = list(shards)
    scratch.update({name + "_in": (a.shape, a.dtype) for name, a in shards.items()})
    names = [*(name + "_hbm" for name in shards), *ins, *outs, *scratch, "lsem", "ssem", "rsem"]
    whole = pl.BlockSpec(memory_space=pltpu.VMEM)
    results = pl.pallas_call(
        functools.partial(block_kernel, names, dims),
        out_shape=[pltpu.VMEM(*v) for v in outs.values()],
        in_specs=[pl.BlockSpec(memory_space=pltpu.HBM)] * len(shards) + [whole] * len(ins),
        out_specs=[whole] * len(outs),
        scratch_shapes=[pltpu.VMEM(*v) for v in scratch.values()]
        + [pltpu.SemaphoreType.DMA((len(shards),))]
        + [pltpu.SemaphoreType.DMA((dims.get("semaphores", SEMAPHORES + 16 * D),))] * 2,
        compiler_params=pltpu.CompilerParams(
            collective_id=0, has_side_effects=True, vmem_limit_bytes=48 << 20
        ),
        name="block",
    )(
        *(pltpu.with_memory_space_constraint(v, pltpu.HBM) for v in shards.values()),
        *(pltpu.with_memory_space_constraint(v, pltpu.VMEM) for v in ins.values()),
    )
    got = dict(zip(outs, results, strict=True))
    reduce_grad, group_grad, expand_grad = got["reduce_out"], got["group_out"], got["expand_out"]
    if not own_gather:
        both = ("height", "dp")
        reduce_grad = lax.psum_scatter(reduce_grad.T, both, scatter_dimension=0, tiled=True).astype(F32)
        group_grad = lax.psum_scatter(group_grad, both, scatter_dimension=0, tiled=True).astype(F32)
        expand_grad = lax.psum_scatter(expand_grad, both, scatter_dimension=1, tiled=True).astype(F32)
    groups = (
        (reduce_grad, reduce_master, reduce_first, reduce_second, reduce_average),
        (group_grad, group_master, group_first, group_second, group_average),
        (expand_grad, expand_master, expand_first, expand_second, expand_average),
        (got["inner_grad"], inner_master, inner_first, inner_second, inner_average),
        (got["outer_grad"], outer_master, outer_first, outer_second, outer_average),
    )
    shapes = [
        jax.ShapeDtypeStruct((N, W, rows, OUT), BF),
        jax.ShapeDtypeStruct((N, W, rows, OUT), F32),
    ]
    for n, group in enumerate(groups):
        kinds = [F32] * 4 + ([BF] if n < 3 else []) + [F32]
        shapes += [jax.ShapeDtypeStruct(group[0].shape, kind) for kind in kinds]
    flat = [got["ig"].reshape(rows, W, N, OUT), got["turned"]]
    flat += [a for group in groups for a in group]
    news = pl.pallas_call(
        last_kernel,
        out_shape=shapes,
        in_specs=[whole] * len(flat),
        out_specs=[pl.BlockSpec(memory_space=pltpu.HBM)] * len(shapes),
        scratch_shapes=[pltpu.VMEM((N, W, rows, OUT), F32)]
        + [pltpu.VMEM(a.shape, a.dtype) for a in shapes[2:]]
        + [pltpu.SemaphoreType.DMA((len(shapes) + W,))],
        compiler_params=pltpu.CompilerParams(vmem_limit_bytes=40 << 20),
        name="adamw",
    )(*flat)
    pixel_outs = (a.transpose(0, 2, 1, 3) for a in news[:2])
    return (*pixel_outs, *news[2:])


def solution(mesh):
    pixel = P("dp", "height", None, "chan")
    first = P(("height", "dp"), "chan")
    last = P("chan", ("height", "dp"))
    table = P(None, "chan")
    return jax.shard_map(
        local,
        mesh=mesh,
        in_specs=(P("dp", "height", None, None), pixel)
        + (first,) * 8
        + (last,) * 4
        + (table,) * 8,
        out_specs=(pixel, pixel) + (first,) * 12 + (last,) * 6 + (table,) * 10,
        check_vma=False,
    )
```
